512 devices in a mesh: ctx: 128 (over z, y, core), tile: 4 (over x).
Axes of the slice: x: 4, y: 8, z: 8, core: 2. Of those that a mesh axis runs over, the one named last changes fastest.
Arguments:
- masks: bfloat16 [256, 512, 512], P('ctx', 'tile'), may hold values from 0 to 1
- blur_rows: bfloat16 [512, 512], replicated, may hold values from -0.25 to 0.25
- blur_cols: bfloat16 [512, 512], replicated, may hold values from -0.25 to 0.25
- pupils: float32 [6, 64, 128], replicated, may hold values from -5 to 5
- targets: bfloat16 [256, 512, 512], P('ctx', 'tile'), may hold values from 0 to 1
- context_masters: int32 [256, 12], P('ctx'), may hold values from 0 to 255, as said below
- offsets: int32 [256, 12, 2], P('ctx'), may hold values from 0 to 511
Outputs:
- resist: bfloat16 [256, 512, 512], P('ctx', 'tile')
- mask_grad: float32 [256, 512, 512], P('ctx', 'tile')
The draws below stay inside these ranges and needn't reach their ends.
Inputs may be any that keep to these rules, and one draw needn't show every extreme that they name: `context_masters`: master m lies on ctx index m // 2. Among the masters named by the 2 contexts of one ctx index there is at most one lying on any one ctx index; a master may be named several times.
All inputs are finite; a program needn't handle non-finite values.
Results may differ from the reference program's by a relative error of at most 0.019.
Values may be sent and summed in bfloat16 or wider, within the bound.
A program may use at most 64 MiB of HBM per device.

```python
import math
import jax
import jax.numpy as jnp
from jax import lax

PIXELS = 512
MODE_SIDE = 64
KERNELS = 6
MASTER_DEV = 2
CONTEXT_DEV = 2
SOURCES = 12
MASTERS = 256
CONTEXTS = 256


def draw_context_masters(key, part):
    base_key = jax.random.fold_in(key, 7)
    hot_key, jitter_key, choose_key, order_key = jax.random.split(base_key, 4)
    owner_count = MASTERS // MASTER_DEV
    device_count = CONTEXTS // CONTEXT_DEV
    request_count = CONTEXT_DEV * SOURCES
    hotness = jax.random.randint(hot_key, (owner_count,), 0, 4, dtype=jnp.int32)
    jitter = jax.random.randint(jitter_key, (device_count, owner_count), 0, 65536, dtype=jnp.int32)
    scores = (jitter + hotness[None, :] * 65536) * owner_count + jnp.arange(owner_count, dtype=jnp.int32)[None, :]
    ranked = lax.top_k(scores, owner_count)[1].astype(jnp.int32)
    position = jnp.arange(request_count, dtype=jnp.int32) % owner_count
    owners = ranked[:, position]
    shuffle_scores = jax.random.randint(order_key, (device_count, request_count), 0, 65536, dtype=jnp.int32) * request_count + jnp.arange(request_count, dtype=jnp.int32)[None, :]
    shuffle = lax.top_k(shuffle_scores, request_count)[1].astype(jnp.int32)
    owners = jnp.take_along_axis(owners, shuffle, axis=1)
    master_pick = jax.random.randint(choose_key, (device_count, owner_count), 0, MASTER_DEV, dtype=jnp.int32)
    chosen_pick = jnp.take_along_axis(master_pick, owners, axis=1)
    return (owners * MASTER_DEV + chosen_pick).reshape(CONTEXTS, SOURCES).astype(jnp.int32)


def touch_ends(entries, key, smallest, top_value):
    spot = [jax.random.randint(jax.random.fold_in(key, axis), (), 0, length) for axis, length in enumerate(entries.shape)]
    longest = entries.shape.index(max(entries.shape))
    neighbour = spot[:longest] + [(spot[longest] + 1) % entries.shape[longest]] + spot[longest + 1:]
    return entries.at[tuple(spot)].set(smallest).at[tuple(neighbour)].set(top_value)


def block_scale(own_key, dims, cuts, least, largest):
    def one(dim, shards_of):
        heights = jax.random.uniform(jax.random.fold_in(jax.random.fold_in(own_key, 6), dim), (shards_of,), jnp.float32, least / len(cuts), largest / len(cuts))
        return jnp.repeat(jnp.exp(heights), dims[dim] // shards_of).reshape((-1,) + (1,) * (len(dims) - dim - 1))

    factor_of = one(*cuts[0])
    for cut in cuts[1:]:
        factor_of = factor_of * one(*cut)
    return factor_of


def gaussian(own_key, shape, scale, bound, held_as=jnp.bfloat16):
    array = jax.random.normal(own_key, shape, jnp.float32) * scale
    return jnp.minimum(jnp.maximum(array, -bound), bound).astype(held_as)


def setup_inputs(seed: int = 0) -> dict:
    keys = jax.random.split(jax.random.key(seed), 8)
    masks = jnp.clip(1.0 * jax.random.uniform(keys[0], (MASTERS, PIXELS, PIXELS), jnp.float32) ** block_scale(keys[0], (MASTERS, PIXELS, PIXELS), ((0, 128), (1, 4)), -0.2, 0.2), 0.0, 1.0).astype(jnp.bfloat16)
    blur_rows = gaussian(keys[1], (PIXELS, PIXELS), PIXELS ** -0.5, 0.25)
    blur_cols = gaussian(keys[2], (PIXELS, PIXELS), PIXELS ** -0.5, 0.25)
    pupils = gaussian(keys[3], (KERNELS, MODE_SIDE, 2 * MODE_SIDE), 0.8, 5.0, jnp.float32)
    targets = jnp.clip(1.0 * jax.random.uniform(keys[4], (CONTEXTS, PIXELS, PIXELS), jnp.float32) ** block_scale(keys[4], (CONTEXTS, PIXELS, PIXELS), ((0, 128), (1, 4)), -0.2, 0.2), 0.0, 1.0).astype(jnp.bfloat16)
    context_masters = draw_context_masters(jax.random.fold_in(keys[7], 71), 0)
    offsets = touch_ends(jax.random.randint(keys[6], (CONTEXTS, SOURCES, 2), 0, PIXELS), jax.random.fold_in(keys[6], 1), 0, PIXELS - 1).astype(jnp.int32)
    return dict(masks=masks, blur_rows=blur_rows, blur_cols=blur_cols, pupils=pupils, targets=targets, context_masters=context_masters, offsets=offsets)


STEEPNESS = 4.0
THRESHOLD = 1.0

def build_tables(extent, mode_count):
    frequency = (jnp.arange(mode_count, dtype=jnp.int32) - mode_count // 2) % extent
    positions = jnp.arange(extent, dtype=jnp.int32)
    windings = frequency[:, None] * positions[None, :] % extent
    angles = windings.astype(jnp.float32) * (2.0 * math.pi / extent)
    scale_factor = 1.0 / math.sqrt(extent)
    cosine_table = jnp.cos(angles) * scale_factor
    sine_table = jnp.sin(angles) * scale_factor
    row_real = cosine_table.astype(jnp.bfloat16)
    row_imag = (-sine_table).astype(jnp.bfloat16)
    col_fwd = jnp.concatenate([cosine_table.T, -sine_table.T], axis=1).astype(jnp.bfloat16)
    inverse_big = jnp.concatenate([jnp.concatenate([cosine_table, sine_table], axis=1), jnp.concatenate([-sine_table, cosine_table], axis=1)], axis=0).astype(jnp.bfloat16)
    back_real = cosine_table.T.astype(jnp.bfloat16)
    back_imag = sine_table.T.astype(jnp.bfloat16)
    adjoint_big = jnp.concatenate([jnp.concatenate([cosine_table.T, -sine_table.T], axis=1), jnp.concatenate([sine_table.T, cosine_table.T], axis=1)], axis=0).astype(jnp.bfloat16)
    return (row_real, row_imag, col_fwd, inverse_big, back_real, back_imag, adjoint_big)

def complex_left(left_real, left_imag, values):
    width = values.shape[-1] // 2
    real_lead = jnp.einsum('ux,...xv->...uv', left_real.astype(jnp.float32), values.astype(jnp.float32))
    imag_lead = jnp.einsum('ux,...xv->...uv', left_imag.astype(jnp.float32), values.astype(jnp.float32))
    return jnp.concatenate([real_lead[..., :width] - imag_lead[..., width:], real_lead[..., width:] + imag_lead[..., :width]], axis=-1)

def complex_times(factor, values, conjugate):
    width = values.shape[-1] // 2
    factor_real = factor[..., :width]
    factor_imag = factor[..., width:]
    if conjugate:
        factor_imag = -factor_imag
    values_real = values[..., :width]
    values_imag = values[..., width:]
    return jnp.concatenate([factor_real * values_real - factor_imag * values_imag, factor_real * values_imag + factor_imag * values_real], axis=-1)

def phase_table(shifts, row_begin, band_rows, mode_count, extent):
    freq_u = (jnp.arange(band_rows, dtype=jnp.int32) + row_begin - mode_count // 2) % extent
    freq_v = (jnp.arange(mode_count, dtype=jnp.int32) - mode_count // 2) % extent
    windings = (freq_u[None, :, None] * shifts[:, 0][:, None, None] + freq_v[None, None, :] * shifts[:, 1][:, None, None]) % extent
    angles = windings.astype(jnp.float32) * (2.0 * math.pi / extent)
    return jnp.concatenate([jnp.cos(angles), -jnp.sin(angles)], axis=-1)

def image_adjoint(spectrum, target, pupils, back_real, back_imag, row_real, row_imag, inverse_big, adjoint_big):
    amplitude = complex_times(pupils, spectrum[None], False).astype(jnp.bfloat16)
    spread = jnp.einsum('kuv,vy->kuy', amplitude.astype(jnp.float32), inverse_big.astype(jnp.float32)).astype(jnp.bfloat16)
    field = complex_left(back_real, back_imag, spread)
    width = field.shape[-1] // 2
    field_real = field[..., :width]
    field_imag = field[..., width:]
    intensity = lax.optimization_barrier(jnp.sum(field_real * field_real + field_imag * field_imag, axis=0))
    resist = jax.nn.sigmoid(STEEPNESS * (intensity - THRESHOLD))
    slope_term = (resist - target.astype(jnp.float32)) * STEEPNESS * resist * (1.0 - resist)
    pull_back = jnp.concatenate([2.0 * slope_term * field_real, 2.0 * slope_term * field_imag], axis=-1).astype(jnp.bfloat16)
    folded = jnp.einsum('kxy,yv->kxv', pull_back.astype(jnp.float32), adjoint_big.astype(jnp.float32)).astype(jnp.bfloat16)
    grad_amp = complex_left(row_real, row_imag, folded)
    grad_spec = lax.optimization_barrier(jnp.sum(complex_times(pupils, grad_amp, True), axis=0))
    return (resist.astype(jnp.bfloat16), grad_spec)

def reference(masks, blur_rows, blur_cols, pupils, targets, context_masters, offsets):
    extent = masks.shape[1]
    mode_count = pupils.shape[1]
    row_real, row_imag, col_fwd, inverse_big, back_real, back_imag, adjoint_big = build_tables(extent, mode_count)

    def forward(mask):
        half_blur = jnp.dot(mask, blur_cols.T, preferred_element_type=jnp.float32).astype(jnp.bfloat16)
        blurred = jnp.dot(blur_rows, half_blur, preferred_element_type=jnp.float32).astype(jnp.bfloat16)
        column = jnp.dot(blurred, col_fwd, preferred_element_type=jnp.float32).astype(jnp.bfloat16)
        return complex_left(row_real, row_imag, column).astype(jnp.bfloat16)
    spectra = lax.map(forward, masks)
    flat_ids = context_masters.reshape(-1)
    flat_shift = offsets.reshape(-1, 2)
    phases = phase_table(flat_shift, 0, mode_count, mode_count, extent)
    picked = spectra[flat_ids].astype(jnp.float32)
    turned = complex_times(phases, picked, False)
    context_spec = lax.optimization_barrier(jnp.sum(turned.reshape(CONTEXTS, SOURCES, mode_count, 2 * mode_count), axis=1))

    def one_context(inputs):
        spectrum, target = inputs
        return image_adjoint(spectrum, target, pupils, back_real, back_imag, row_real, row_imag, inverse_big, adjoint_big)
    resist, grad_spec = lax.map(one_context, (context_spec, targets))
    back_turn = complex_times(phases, jnp.repeat(grad_spec, SOURCES, axis=0), True)
    master_grad = jax.ops.segment_sum(back_turn, flat_ids, num_segments=MASTERS).astype(jnp.bfloat16)

    def backward(gradient):
        lifted = jnp.dot(gradient, inverse_big, preferred_element_type=jnp.float32).astype(jnp.bfloat16)
        surface = (jnp.dot(back_real, lifted[:, :extent], preferred_element_type=jnp.float32) - jnp.dot(back_imag, lifted[:, extent:], preferred_element_type=jnp.float32)).astype(jnp.bfloat16)
        settled = jnp.dot(surface, blur_cols, preferred_element_type=jnp.float32).astype(jnp.bfloat16)
        return jnp.dot(blur_rows.T, settled, preferred_element_type=jnp.float32)
    mask_grad = lax.map(backward, master_grad)
    return (resist, mask_grad)
```

```python
import functools
import math

import jax
import jax.numpy as jnp
import ml_dtypes
import numpy as np
from jax import lax
from jax.experimental import pallas as pl
from jax.experimental.pallas import tpu as pltpu
from jax.sharding import PartitionSpec as P

STEEPNESS = 4.0
THRESHOLD = 1.0
N = 512
M = 64
K = 6
T = 4
R = N // T
Q = M // T
SIDE = 8
CTX = 2 * SIDE * SIDE
SRC = 12
PAIRS = 2 * SRC
MESH = pl.DeviceIdType.MESH
F32 = jnp.float32
BF16 = jnp.bfloat16
NEAR_FIRST = (1, 7, 2, 6, 3, 5, 4)


def tables():
    freq = (np.arange(M) - M // 2) % N
    angle = (freq[:, None] * np.arange(N)[None, :] % N) * (2.0 * math.pi / N)
    cos = np.cos(angle) / math.sqrt(N)
    sin = np.sin(angle) / math.sqrt(N)
    fst = np.concatenate([cos, -sin], 0)
    gcat = np.concatenate([cos.T, sin.T], 1)
    inv = np.concatenate([np.concatenate([cos, sin], 1), np.concatenate([-sin, cos], 1)], 0)
    adj = np.concatenate([np.concatenate([cos.T, -sin.T], 1), np.concatenate([sin.T, cos.T], 1)], 0)
    adj = np.concatenate([adj, -adj[:, M:], adj[:, :M]], 1)
    order = np.arange(2 * N).reshape(2, T, N // T).transpose(1, 0, 2).reshape(-1)
    return [t.astype(ml_dtypes.bfloat16) for t in (fst, gcat, inv[:, order], adj[order])]


def sine_coefficients():
    w = 0.25 * np.cos(np.pi * (np.arange(400) + 0.5) / 400)
    powers = np.stack([w ** (2 * i + 1) for i in range(6)], 1)
    return [float(c) for c in np.linalg.lstsq(powers, np.sin(2 * np.pi * w), rcond=None)[0]]


SINE = sine_coefficients()


def swap(a):
    return pltpu.roll(a, M, 1)


def left_half(shape):
    return lax.broadcasted_iota(jnp.int32, shape, 1) < M


def turn_rates(tile):
    row = lax.broadcasted_iota(jnp.int32, (Q, 2 * M), 0) + (tile * Q - M // 2)
    lane = lax.broadcasted_iota(jnp.int32, (Q, 2 * M), 1)
    col = lane % M - M // 2
    late = jnp.where(lane < M, 0.0, 0.25).astype(F32)
    return row.astype(F32) * (1.0 / N), col.astype(F32) * (1.0 / N), late


def cos_sin(rates, r, s):
    y = rates[0] * r + rates[1] * s - rates[2]
    y = y - jnp.floor(y + 0.5)
    w = 0.25 - jnp.abs(y)
    z = w * w
    total = jnp.full_like(z, SINE[-1])
    for c in SINE[-2::-1]:
        total = total * z + c
    return total * w


def dot(a, b, dims=((1,), (0,))):
    return lax.dot_general(a, b, (dims, ((), ())), preferred_element_type=F32)


def wait_all(copies):
    for c in copies:
        c.wait()


def main_kernel(
    masks, br, bc, pupils, targets, ids_s, ids_v, fst, gcat, inv, adj,
    resist, g2, ids_all, p_out, q_out,
    g1, part, part_in, spec, prr, pii, amp, u_all, pull, phases,
    x_send, x_recv, a_send, a_recv, i_send, i_recv,
):
    tile = lax.axis_index("tile")
    q = lax.axis_index("ctx")
    core, y, z = q % 2, (q // 2) % SIDE, q // (2 * SIDE)
    major = z + core * (y - z)
    minor = y + core * (z - y)

    def ctx_id(mj, mn):
        zz = mj + core * (mn - mj)
        yy = mn + core * (mj - mn)
        return zz * (2 * SIDE) + yy * 2 + core

    sibling = q + 1 - 2 * core
    barrier = pltpu.get_barrier_semaphore()
    for k in range(1, T):
        pl.semaphore_signal(barrier, inc=1, device_id={"tile": (tile + k) % T}, device_id_type=MESH)
    for k in range(1, SIDE):
        pl.semaphore_signal(barrier, inc=1, device_id={"ctx": ctx_id(major, (minor + k) % SIDE)}, device_id_type=MESH)
        pl.semaphore_signal(barrier, inc=1, device_id={"ctx": ctx_id((major + k) % SIDE, minor)}, device_id_type=MESH)
    pl.semaphore_signal(barrier, inc=1, device_id={"ctx": sibling}, device_id_type=MESH)

    own = pl.ds(pl.multiple_of(tile * R, R), R)
    table = fst[...]
    p_st = dot(table, br[:, own]).astype(BF16)
    q_f = dot(table, bc[...])
    q_st = q_f.astype(BF16)
    p_out[...] = p_st
    q_out[...] = q_st
    qq = jnp.concatenate([q_st, -q_st[M:], q_st[:M]], 0)
    pcat = jnp.concatenate([p_st[:M], p_st[M:]], 1)
    for m in range(2):
        a = dot(masks[m], qq, ((1,), (1,))).astype(BF16)
        s = dot(pcat, jnp.concatenate([a[:, : 2 * M], a[:, 2 * M :]], 0))
        for t in range(T):
            part[0, t, m * Q : (m + 1) * Q] = s[t * Q : (t + 1) * Q]

    pl.semaphore_wait(barrier, T - 1 + 2 * (SIDE - 1) + 1)

    def tile_scatter(step):
        copies = []
        for k in range(1, T):
            to = (tile + k) % T
            copies.append(
                pltpu.make_async_remote_copy(
                    src_ref=part.at[step, to], dst_ref=part_in.at[step, k - 1],
                    send_sem=x_send.at[2 * step, k - 1], recv_sem=x_recv.at[2 * step, k - 1],
                    device_id={"tile": to}, device_id_type=MESH,
                )
            )
        for c in copies:
            c.start()
        return copies

    def tile_sum(step):
        return (part[step, tile] + part_in[step, 0]) + (part_in[step, 1] + part_in[step, 2])

    def line_copies(buf, unit, send, recv, phase):
        half = core * (SIDE * SIDE)
        copies = []
        for k in NEAR_FIRST:
            if phase == 0:
                place = pl.ds((half + major * SIDE + minor) * unit, unit)
                to = ctx_id(major, (minor + k) % SIDE)
            else:
                place = pl.ds((half + major * SIDE) * unit, SIDE * unit)
                to = ctx_id((major + k) % SIDE, minor)
            copies.append(
                pltpu.make_async_remote_copy(
                    src_ref=buf.at[place], dst_ref=buf.at[place],
                    send_sem=send.at[phase, k], recv_sem=recv.at[phase, k],
                    device_id={"ctx": to}, device_id_type=MESH,
                )
            )
        for c in copies:
            c.start()
        return copies

    def sibling_copy(buf, unit, send, recv, k):
        row = (major + SIDE - k) % SIDE
        place = pl.ds((core * (SIDE * SIDE) + row * SIDE) * unit, SIDE * unit)
        copy = pltpu.make_async_remote_copy(
            src_ref=buf.at[place], dst_ref=buf.at[place],
            send_sem=send.at[2, k], recv_sem=recv.at[2, k],
            device_id={"ctx": sibling}, device_id_type=MESH,
        )
        copy.start()
        return copy

    def gather(bufs, between):
        first = [line_copies(b, u, s, r, 0) for b, u, s, r in bufs]
        between()
        for f in first:
            wait_all(f)
        second = [line_copies(b, u, s, r, 1) for b, u, s, r in bufs]
        third = [sibling_copy(b, u, s, r, 0) for b, u, s, r in bufs]
        for i, k in enumerate(NEAR_FIRST):
            for (b, u, s, r), copies in zip(bufs, second):
                copies[i].wait()
                third.append(sibling_copy(b, u, s, r, k))
        wait_all(third)

    copies = tile_scatter(0)

    rates = turn_rates(tile)
    for p in range(PAIRS):
        r = ids_s[0, PAIRS + 2 * p].astype(F32)
        s = ids_s[0, PAIRS + 2 * p + 1].astype(F32)
        phases[p] = cos_sin(rates, r, s)
    left64 = left_half((M, 2 * M))
    for k in range(K):
        pk = pupils[k]
        turned = swap(pk)
        prr[k] = jnp.where(left64, pk, turned)
        pii[k] = jnp.where(left64, -turned, pk)

    slot = core * (SIDE * SIDE) + major * SIDE + minor
    wait_all(copies)
    g1[pl.ds(slot * 2, 2)] = tile_sum(0).astype(BF16).reshape(2, Q, 2 * M)
    ids_all[pl.ds(slot, 1)] = ids_v[...]
    gather([(g1, 2, a_send.at[0], a_recv.at[0]), (ids_all, 1, i_send, i_recv)], lambda: None)

    leftq = left_half((Q, 2 * M))
    for c in range(2):
        sum_a = jnp.zeros((Q, 2 * M), F32)
        sum_b = jnp.zeros((Q, 2 * M), F32)
        for j in range(SRC):
            p = c * SRC + j
            master = ids_s[0, p]
            owner = master >> 1
            ocore = owner & 1
            oy = (owner >> 1) & (SIDE - 1)
            oz = owner >> 4
            place = ocore * (SIDE * SIDE) + oz * SIDE + oy + ocore * (SIDE - 1) * (oy - oz)
            g = g1[place * 2 + (master & 1)].astype(F32)
            cs = phases[p]
            sum_a += g * cs
            sum_b += swap(g) * cs
        spec[tile, c * Q : (c + 1) * Q] = jnp.where(leftq, sum_a + swap(sum_a), swap(sum_b) - sum_b)
    copies = []
    for k in range(1, T):
        copies.append(
            pltpu.make_async_remote_copy(
                src_ref=spec.at[tile], dst_ref=spec.at[tile],
                send_sem=x_send.at[1, k - 1], recv_sem=x_recv.at[1, k - 1],
                device_id={"tile": (tile + k) % T}, device_id_type=MESH,
            )
        )
    for c in copies:
        c.start()
    wait_all(copies)

    fown = fst[:, own]
    fcat = jnp.concatenate([fown[:M], fown[M:]], 1)
    gown = gcat[own, :]
    for c in range(2):
        s = jnp.concatenate([spec[t, c * Q : (c + 1) * Q] for t in range(T)], 0)
        s_sw = swap(s)
        s2 = jnp.where(left64, -s_sw, s_sw)
        s2_sw = jnp.where(left64, s, -s)
        for k in range(K):
            a1 = prr[k] * s + pii[k] * s_sw
            a2 = prr[k] * s2 + pii[k] * s2_sw
            both = jnp.concatenate([a1, a2], 0).astype(BF16)
            u_all[k * R : (k + 1) * R] = dot(gown, both).astype(BF16)
        for b in range(T):
            cols = slice(b * R, (b + 1) * R)
            field = dot(u_all[...], inv[:, b * 2 * R : (b + 1) * 2 * R])
            intensity = jnp.zeros((R, R), F32)
            for k in range(K):
                fr = field[k * R : (k + 1) * R, :R]
                fi = field[k * R : (k + 1) * R, R:]
                intensity += fr * fr + fi * fi
            image = 1.0 / (1.0 + jnp.exp(-STEEPNESS * (intensity - THRESHOLD)))
            resist[c, :, cols] = image.astype(BF16)
            slope = (image - targets[c, :, cols].astype(F32)) * (2.0 * STEEPNESS) * image * (1.0 - image)
            slope2 = jnp.concatenate([slope, slope], 1)
            for k in range(K):
                pull[k * R : (k + 1) * R, b * 2 * R : (b + 1) * 2 * R] = (
                    slope2 * field[k * R : (k + 1) * R]
                ).astype(BF16)
        folded = dot(pull[...], adj[...]).astype(BF16)
        g_a = jnp.zeros((M, 2 * M), F32)
        g_b = jnp.zeros((M, 2 * M), F32)
        for k in range(K):
            fk = folded[k * R : (k + 1) * R]
            ga = dot(fcat, jnp.concatenate([fk[:, : 2 * M], fk[:, 2 * M :]], 0))
            g_a += prr[k] * ga
            g_b += pii[k] * ga
        grad = g_a + swap(g_b)
        for t in range(T):
            part[1, t, c * Q : (c + 1) * Q] = grad[t * Q : (t + 1) * Q]

    wait_all(tile_scatter(1))
    g2[pl.ds(slot * 2, 2)] = tile_sum(1).astype(BF16).reshape(2, Q, 2 * M)
    gather([(g2, 2, a_send.at[1], a_recv.at[1])], lambda: None)


def pair_kernel(where_s, ids_s, ids_v, g2, out, lists_v, lists_s, acc, sem):
    me = where_s[0]
    rates = turn_rates(where_s[1])
    ids = ids_v[...].reshape(CTX, 128)
    lane = lax.broadcasted_iota(jnp.int32, (CTX, 128), 1)
    sub = lax.broadcasted_iota(jnp.int32, (CTX, 128), 0)
    sub8 = lax.broadcasted_iota(jnp.int32, (8, 128), 0)
    lane8 = lax.broadcasted_iota(jnp.int32, (8, 128), 1)
    weights = jnp.where(sub8 == 0, 1, jnp.where(sub8 == 1, lane8, 0)).astype(F32).astype(BF16)
    before = jnp.where(sub < lane, 1.0, 0.0).astype(BF16)
    for m in range(2):
        match = jnp.where((ids == 2 * me + m) & (lane < PAIRS), 1.0, 0.0).astype(BF16)
        stats = dot(weights, match, ((1,), (1,)))
        count = jnp.broadcast_to(stats[0:1], (8, 128))
        index = jnp.broadcast_to(stats[1:2], (8, 128))
        single = jnp.where(count == 1.0, 1.0, 0.0)
        rank = dot(single.astype(BF16), before)
        hot = jnp.where(
            (jnp.broadcast_to(rank[0:1], (CTX, 128)) == sub.astype(F32))
            & (jnp.broadcast_to(single[0:1], (CTX, 128)) > 0.5),
            1.0, 0.0,
        ).astype(BF16)
        load = jnp.where(sub8 == 0, lane8.astype(F32), jnp.where(sub8 == 1, index * single, jnp.where(sub8 == 2, 1.0, 0.0)))
        listed = dot(load.astype(BF16), hot, ((1,), (1,)))
        n_single = jnp.sum(single, axis=1, keepdims=True)
        n_multi = jnp.sum(jnp.where(count > 1.5, 1.0, 0.0), axis=1, keepdims=True)
        rows = jnp.where(sub8 == 3, n_single, jnp.where(sub8 == 4, n_multi, jnp.where(sub8 == 5, count, listed)))
        lists_v[m * 8 : (m + 1) * 8] = rows.astype(jnp.int32)
    copy = pltpu.make_async_copy(lists_v, lists_s, sem)
    copy.start()
    copy.wait()

    def terms(h, j, weight):
        r = ids_s[h, 0, PAIRS + 2 * j].astype(F32)
        s = ids_s[h, 0, PAIRS + 2 * j + 1].astype(F32)
        g = g2[2 * h + j // SRC].astype(F32)
        cs = cos_sin(rates, r, s)
        if weight is not None:
            cs = cs * weight
        return g * cs, swap(g) * cs

    block = 8
    left = left_half((Q, 2 * M))
    for m in range(2):

        def step(i, carry):
            sum_a, sum_b = carry
            for b in range(block):
                k = i * block + b
                add_a, add_b = terms(
                    lists_s[m * 8, k], lists_s[m * 8 + 1, k], lists_s[m * 8 + 2, k].astype(F32)
                )
                sum_a += add_a
                sum_b += add_b
            return sum_a, sum_b

        zero = jnp.zeros((Q, 2 * M), F32)
        sum_a, sum_b = lax.fori_loop(0, (lists_s[m * 8 + 3, 0] + block - 1) // block, step, (zero, zero))
        acc[0] = sum_a
        acc[1] = sum_b

        @pl.when(lists_s[m * 8 + 4, 0] > 0)
        def _():
            def host(h, _):
                @pl.when(lists_s[m * 8 + 5, h] > 1)
                def _():
                    def one(j, _):
                        @pl.when(ids_s[h, 0, j] == 2 * me + m)
                        def _():
                            add_a, add_b = terms(h, j, None)
                            acc[0] += add_a
                            acc[1] += add_b

                        return 0

                    lax.fori_loop(0, PAIRS, one, 0)

                return 0

            lax.fori_loop(0, CTX, host, 0)

        sum_a, sum_b = acc[0], acc[1]
        out[m * Q : (m + 1) * Q] = jnp.where(left, sum_a - swap(sum_a), sum_b + swap(sum_b)).astype(BF16)


def last_kernel(gq, p_st, q_st, out, rows, x_send, x_recv):
    tile = lax.axis_index("tile")
    barrier = pltpu.get_barrier_semaphore()
    for k in range(1, T):
        pl.semaphore_signal(barrier, inc=1, device_id={"tile": (tile + k) % T}, device_id_type=MESH)
    rows[tile] = gq[...]
    pl.semaphore_wait(barrier, T - 1)
    copies = []
    for k in range(1, T):
        copies.append(
            pltpu.make_async_remote_copy(
                src_ref=rows.at[tile], dst_ref=rows.at[tile],
                send_sem=x_send.at[k - 1], recv_sem=x_recv.at[k - 1],
                device_id={"tile": (tile + k) % T}, device_id_type=MESH,
            )
        )
    for c in copies:
        c.start()
    wait_all(copies)
    left = left_half((M, 2 * M))
    for m in range(2):
        g = jnp.concatenate([rows[t, m * Q : (m + 1) * Q].astype(F32) for t in range(T)], 0)
        turned = swap(g)
        both = jnp.concatenate([g, jnp.where(left, turned, -turned)], 0).astype(BF16)
        lifted = dot(p_st[...], both, ((0,), (0,))).astype(BF16)
        out[m] = dot(lifted, q_st[...])


def local(masks, blur_rows, blur_cols, pupils, targets, context_masters, offsets):
    vmem = pl.BlockSpec(memory_space=pltpu.VMEM)
    smem = pl.BlockSpec(memory_space=pltpu.SMEM)
    dma = pltpu.SemaphoreType.DMA
    packed = jnp.concatenate(
        [context_masters.reshape(-1), offsets.reshape(-1), jnp.zeros((128 - 3 * PAIRS,), jnp.int32)]
    ).reshape(1, 128)
    resist, g2, ids_all, p_st, q_st = pl.pallas_call(
        main_kernel,
        out_shape=(
            jax.ShapeDtypeStruct((2, R, N), BF16),
            jax.ShapeDtypeStruct((2 * CTX, Q, 2 * M), BF16),
            jax.ShapeDtypeStruct((CTX, 1, 128), jnp.int32),
            jax.ShapeDtypeStruct((2 * M, R), BF16),
            jax.ShapeDtypeStruct((2 * M, N), BF16),
        ),
        in_specs=[vmem] * 5 + [smem] + [vmem] * 5,
        out_specs=(vmem,) * 5,
        scratch_shapes=[
            pltpu.VMEM((2 * CTX, Q, 2 * M), BF16),
            pltpu.VMEM((2, T, 2 * Q, 2 * M), F32),
            pltpu.VMEM((2, T - 1, 2 * Q, 2 * M), F32),
            pltpu.VMEM((T, 2 * Q, 2 * M), F32),
            pltpu.VMEM((K, M, 2 * M), F32),
            pltpu.VMEM((K, M, 2 * M), F32),
            pltpu.VMEM((8, 128), F32),
            pltpu.VMEM((K * R, 2 * M), BF16),
            pltpu.VMEM((K * R, 2 * N), BF16),
            pltpu.VMEM((PAIRS, Q, 2 * M), F32),
            dma((3, T - 1)),
            dma((3, T - 1)),
            dma((2, 3, SIDE)),
            dma((2, 3, SIDE)),
            dma((3, SIDE)),
            dma((3, SIDE)),
        ],
        compiler_params=pltpu.CompilerParams(
            collective_id=0, has_side_effects=True, vmem_limit_bytes=48 << 20
        ),
        name="main",
    )(masks, blur_rows, blur_cols, pupils, targets, packed, packed.reshape(1, 1, 128), *tables())
    where = jnp.stack([lax.axis_index("ctx"), lax.axis_index("tile")]).astype(jnp.int32)
    gq = pl.pallas_call(
        pair_kernel,
        out_shape=jax.ShapeDtypeStruct((2 * Q, 2 * M), BF16),
        in_specs=[smem, smem, vmem, vmem],
        out_specs=vmem,
        scratch_shapes=[
            pltpu.VMEM((16, 128), jnp.int32),
            pltpu.SMEM((16, 128), jnp.int32),
            pltpu.VMEM((2, Q, 2 * M), F32),
            dma,
        ],
        compiler_params=pltpu.CompilerParams(vmem_limit_bytes=32 << 20),
        name="pairs",
    )(where, ids_all, ids_all, g2)
    mask_grad = pl.pallas_call(
        last_kernel,
        out_shape=jax.ShapeDtypeStruct((2, R, N), F32),
        in_specs=[vmem] * 3,
        out_specs=vmem,
        scratch_shapes=[pltpu.VMEM((T, 2 * Q, 2 * M), BF16), dma((T - 1,)), dma((T - 1,))],
        compiler_params=pltpu.CompilerParams(
            collective_id=1, has_side_effects=True, vmem_limit_bytes=32 << 20
        ),
        name="last",
    )(gq, p_st, q_st)
    return (resist, mask_grad)


def solution(mesh):
    placed = (
        P("ctx", "tile", None),
        P(),
        P(),
        P(),
        P("ctx", "tile", None),
        P("ctx", None),
        P("ctx", None, None),
    )
    return jax.shard_map(
        local,
        mesh=mesh,
        in_specs=placed,
        out_specs=(P("ctx", "tile", None), P("ctx", "tile", None)),
        check_vma=False,
    )
```

```python
import functools
import math

import jax
import jax.numpy as jnp
import ml_dtypes
import numpy as np
from jax import lax
from jax.experimental import pallas as pl
from jax.experimental.pallas import tpu as pltpu
from jax.sharding import PartitionSpec as P

STEEPNESS = 4.0
THRESHOLD = 1.0
N = 512
M = 64
K = 6
T = 4
R = N // T
Q = M // T
SIDE = 8
CTX = 2 * SIDE * SIDE
SRC = 12
PAIRS = 2 * SRC
MESH = pl.DeviceIdType.MESH
F32 = jnp.float32
BF16 = jnp.bfloat16
NEAR_FIRST = (1, 7, 2, 6, 3, 5, 4)


def tables():
    freq = (np.arange(M) - M // 2) % N
    angle = (freq[:, None] * np.arange(N)[None, :] % N) * (2.0 * math.pi / N)
    cos = np.cos(angle) / math.sqrt(N)
    sin = np.sin(angle) / math.sqrt(N)
    fst = np.concatenate([cos, -sin], 0)
    gcat = np.concatenate([cos.T, sin.T], 1)
    inv = np.concatenate([np.concatenate([cos, sin], 1), np.concatenate([-sin, cos], 1)], 0)
    adj = np.concatenate([np.concatenate([cos.T, -sin.T], 1), np.concatenate([sin.T, cos.T], 1)], 0)
    adj = np.concatenate([adj, -adj[:, M:], adj[:, :M]], 1)
    order = np.arange(2 * N).reshape(2, T, N // T).transpose(1, 0, 2).reshape(-1)
    return [t.astype(ml_dtypes.bfloat16) for t in (fst, gcat, inv[:, order], adj[order])]


def sine_coefficients():
    w = 0.25 * np.cos(np.pi * (np.arange(400) + 0.5) / 400)
    powers = np.stack([w ** (2 * i + 1) for i in range(6)], 1)
    return [float(c) for c in np.linalg.lstsq(powers, np.sin(2 * np.pi * w), rcond=None)[0]]


SINE = sine_coefficients()


def swap(a):
    return pltpu.roll(a, M, 1)


def left_half(shape):
    return lax.broadcasted_iota(jnp.int32, shape, 1) < M


def turn_rates(tile):
    row = lax.broadcasted_iota(jnp.int32, (Q, 2 * M), 0) + (tile * Q - M // 2)
    lane = lax.broadcasted_iota(jnp.int32, (Q, 2 * M), 1)
    col = lane % M - M // 2
    late = jnp.where(lane < M, 0.0, 0.25).astype(F32)
    return row.astype(F32) * (1.0 / N), col.astype(F32) * (1.0 / N), late


def cos_sin(rates, r, s):
    y = rates[0] * r + rates[1] * s - rates[2]
    y = y - jnp.floor(y + 0.5)
    w = 0.25 - jnp.abs(y)
    z = w * w
    total = jnp.full_like(z, SINE[-1])
    for c in SINE[-2::-1]:
        total = total * z + c
    return total * w


def dot(a, b, dims=((1,), (0,))):
    return lax.dot_general(a, b, (dims, ((), ())), preferred_element_type=F32)


def wait_all(copies):
    for c in copies:
        c.wait()


def near_first(i):
    return (i % 2) * ((i + 1) // 2) + (1 - i % 2) * (SIDE - i // 2)


def pair_lists(ids, me):
    lane = lax.broadcasted_iota(jnp.int32, (CTX, 128), 1)
    sub = lax.broadcasted_iota(jnp.int32, (CTX, 128), 0)
    sub8 = lax.broadcasted_iota(jnp.int32, (8, 128), 0)
    lane8 = lax.broadcasted_iota(jnp.int32, (8, 128), 1).astype(F32)
    ones = jnp.full((8, 128), 1.0, BF16)
    before = jnp.where(sub < lane, 1.0, 0.0).astype(BF16)
    r = pltpu.roll(ids, 128 - 32, 1)
    s = pltpu.roll(ids, 128 - 64, 1)
    second = jnp.where(lane >= SRC, 1.0, 0.0)
    values = [second] + [v.astype(F32) for v in (r >> 4, r & 15, s >> 4, s & 15)]
    lists = []
    for m in range(2):
        match = jnp.where((ids == 2 * me + m) & (lane < PAIRS), 1.0, 0.0)
        count = dot(ones, match.astype(BF16), ((1,), (1,)))
        found = [dot(ones, (match * v).astype(BF16), ((1,), (1,))) for v in values]
        single = jnp.where(count == 1.0, 1.0, 0.0)
        rank = dot(single.astype(BF16), before)
        hot = jnp.where(
            (jnp.broadcast_to(rank[0:1], (CTX, 128)) == sub.astype(F32))
            & (jnp.broadcast_to(single[0:1], (CTX, 128)) > 0.5),
            1.0, 0.0,
        ).astype(BF16)
        load = jnp.where(sub8 == 5, single, 0.0)
        load = jnp.where(sub8 == 0, single * (2.0 * lane8 + found[0]), load)
        for i in range(1, 5):
            load = jnp.where(sub8 == i, single * found[i], load)
        listed = dot(load.astype(BF16), hot, ((1,), (1,)))
        line = [jnp.broadcast_to(listed[i : i + 1], (8, 128)) for i in range(6)]
        n_single = jnp.sum(single, axis=1, keepdims=True)
        n_multi = jnp.sum(jnp.where(count > 1.5, 1.0, 0.0), axis=1, keepdims=True)
        rows = jnp.where(sub8 == 6, count, line[0])
        rows = jnp.where(sub8 == 1, 16.0 * line[1] + line[2], rows)
        rows = jnp.where(sub8 == 2, 16.0 * line[3] + line[4], rows)
        rows = jnp.where(sub8 == 3, line[5], rows)
        rows = jnp.where(sub8 == 4, n_single, rows)
        rows = jnp.where(sub8 == 5, n_multi, rows)
        lists.append(rows.astype(jnp.int32))
    return lists


def main_kernel(
    masks_h, br_h, bc_h, pupils_h, targets_h, ids_s, ids_v, fst_h, gcat_h, inv_h, adj_h,
    resist, g2, ids_all, lists, p_out, q_out,
    masks, br, bc, pupils, targets, fst, gown_v, inv, adj,
    g1, part, part_in, spec, prr, pii, u_all, pull, phases,
    load_sem, x_send, x_recv, a_send, a_recv, f_send, f_recv, s_send, s_recv, i_send, i_recv,
):
    tile = lax.axis_index("tile")
    q = lax.axis_index("ctx")
    core, y, z = q % 2, (q // 2) % SIDE, q // (2 * SIDE)
    major = z + core * (y - z)
    minor = y + core * (z - y)
    half = core * (SIDE * SIDE)
    slot = half + major * SIDE + minor
    own = pl.ds(pl.multiple_of(tile * R, R), R)

    loads = [
        pltpu.make_async_copy(src, dst, load_sem.at[i])
        for i, (src, dst) in enumerate(
            [
                (fst_h, fst),
                (br_h.at[:, own], br),
                (bc_h, bc),
                (masks_h, masks),
                (pupils_h, pupils),
                (gcat_h.at[own, :], gown_v),
                (inv_h, inv),
                (targets_h, targets),
                (adj_h, adj),
            ]
        )
    ]
    for copy in loads:
        copy.start()

    def ctx_id(mj, mn):
        zz = mj + core * (mn - mj)
        yy = mn + core * (mj - mn)
        return zz * (2 * SIDE) + yy * 2 + core

    sibling = q + 1 - 2 * core
    barrier = pltpu.get_barrier_semaphore()
    for k in range(1, SIDE):
        pl.semaphore_signal(barrier, inc=1, device_id={"ctx": ctx_id(major, (minor + k) % SIDE)}, device_id_type=MESH)
        pl.semaphore_signal(barrier, inc=1, device_id={"ctx": ctx_id((major + k) % SIDE, minor)}, device_id_type=MESH)
    for k in range(1, T):
        pl.semaphore_signal(barrier, inc=1, device_id={"tile": (tile + k) % T}, device_id_type=MESH)
    pl.semaphore_signal(barrier, inc=1, device_id={"ctx": sibling}, device_id_type=MESH)

    loads[0].wait()
    loads[1].wait()
    table = fst[...]
    p_st = dot(table, br[...]).astype(BF16)
    loads[2].wait()
    q_st = dot(table, bc[...]).astype(BF16)
    p_out[...] = p_st
    q_out[...] = q_st
    qq = jnp.concatenate([q_st, -q_st[M:], q_st[:M]], 0)
    pcat = jnp.concatenate([p_st[:M], p_st[M:]], 1)
    loads[3].wait()
    for m in range(2):
        a = dot(masks[m], qq, ((1,), (1,))).astype(BF16)
        s = dot(pcat, jnp.concatenate([a[:, : 2 * M], a[:, 2 * M :]], 0))
        for t in range(T):
            part[0, t, m * Q : (m + 1) * Q] = s[t * Q : (t + 1) * Q]

    pl.semaphore_wait(barrier, T - 1 + 2 * (SIDE - 1) + 1)

    def tile_scatter(step):
        copies = []
        for k in range(1, T):
            to = (tile + k) % T
            copies.append(
                pltpu.make_async_remote_copy(
                    src_ref=part.at[step, to], dst_ref=part_in.at[step, k - 1],
                    send_sem=x_send.at[2 * step, k - 1], recv_sem=x_recv.at[2 * step, k - 1],
                    device_id={"tile": to}, device_id_type=MESH,
                )
            )
        for c in copies:
            c.start()
        return copies

    def tile_sum(step):
        return (part[step, tile] + part_in[step, 0]) + (part_in[step, 1] + part_in[step, 2])

    def to_ctx(ref, place, send_sem, recv_sem, to):
        return pltpu.make_async_remote_copy(
            src_ref=ref.at[place], dst_ref=ref.at[place], send_sem=send_sem, recv_sem=recv_sem,
            device_id={"ctx": to}, device_id_type=MESH,
        )

    def gather(buf, step, between, late):
        def along_minor(k):
            return to_ctx(
                buf, pl.ds(slot * 2, 2), a_send.at[step, k], a_recv.at[step, k], ctx_id(major, (minor + k) % SIDE)
            )

        def along_major(came, k):
            place = pl.ds((half + major * SIDE + (minor + SIDE - came) % SIDE) * 2, 2)
            return to_ctx(
                buf, place, f_send.at[step, came, k], f_recv.at[step, came, k], ctx_id((major + k) % SIDE, minor)
            )

        def to_sibling(k):
            place = pl.ds((half + (major + SIDE - k) % SIDE * SIDE) * 2, 2 * SIDE)
            return to_ctx(buf, place, s_send.at[step, k], s_recv.at[step, k], sibling)

        for k in NEAR_FIRST:
            along_minor(k).start()
        for k in NEAR_FIRST:
            along_major(0, k).start()
        between()

        def forward(i, _):
            came = near_first(i)
            along_minor(came).wait_recv()
            for k in NEAR_FIRST:
                along_major(came, k).start()
            return 0

        lax.fori_loop(1, SIDE, forward, 0)
        to_sibling(0).start()
        late()

        def arrive(i, _):
            k = near_first(i)
            for came in range(SIDE):
                along_major(came, k).wait_recv()
            to_sibling(k).start()
            return 0

        lax.fori_loop(1, SIDE, arrive, 0)
        for k in range(SIDE):
            to_sibling(k).wait()
        for k in range(1, SIDE):
            along_minor(k).wait_send()

        def sent(k, _):
            for came in range(SIDE):
                along_major(came, k).wait_send()
            return 0

        lax.fori_loop(1, SIDE, sent, 0)

    def ids_line(phase):
        copies = []
        for k in NEAR_FIRST:
            if phase == 0:
                place, to = pl.ds(slot, 1), ctx_id(major, (minor + k) % SIDE)
            else:
                place, to = pl.ds(half + major * SIDE, SIDE), ctx_id((major + k) % SIDE, minor)
            copies.append(to_ctx(ids_all, place, i_send.at[phase, k], i_recv.at[phase, k], to))
        for c in copies:
            c.start()
        return copies

    copies = tile_scatter(0)
    ids_all[pl.ds(slot, 1)] = ids_v[...]
    ids_first = ids_line(0)

    rates = turn_rates(tile)
    for p in range(PAIRS):
        phases[p] = cos_sin(rates, ids_s[0, 32 + p].astype(F32), ids_s[0, 64 + p].astype(F32))
    left64 = left_half((M, 2 * M))
    loads[4].wait()
    for k in range(K):
        pk = pupils[k]
        turned = swap(pk)
        prr[k] = jnp.where(left64, pk, turned)
        pii[k] = jnp.where(left64, -turned, pk)

    wait_all(copies)
    g1[pl.ds(slot * 2, 2)] = tile_sum(0).astype(BF16).reshape(2, Q, 2 * M)
    ids_second = []

    def ids_on():
        wait_all(ids_first)
        ids_second.extend(ids_line(1))

    def ids_end():
        wait_all(ids_second)
        copy = to_ctx(ids_all, pl.ds(half, SIDE * SIDE), i_send.at[2, 0], i_recv.at[2, 0], sibling)
        copy.start()
        ids_second[:] = [copy]

    gather(g1, 0, ids_on, ids_end)
    wait_all(ids_second)

    leftq = left_half((Q, 2 * M))
    for c in range(2):
        sum_a = jnp.zeros((Q, 2 * M), F32)
        sum_b = jnp.zeros((Q, 2 * M), F32)
        for j in range(SRC):
            p = c * SRC + j
            master = ids_s[0, p]
            owner = master >> 1
            ocore = owner & 1
            oy = (owner >> 1) & (SIDE - 1)
            oz = owner >> 4
            place = ocore * (SIDE * SIDE) + oz * SIDE + oy + ocore * (SIDE - 1) * (oy - oz)
            g = g1[place * 2 + (master & 1)].astype(F32)
            cs = phases[p]
            sum_a += g * cs
            sum_b += swap(g) * cs
        spec[tile, c * Q : (c + 1) * Q] = jnp.where(leftq, sum_a + swap(sum_a), swap(sum_b) - sum_b)
    copies = []
    for k in range(1, T):
        copies.append(
            pltpu.make_async_remote_copy(
                src_ref=spec.at[tile], dst_ref=spec.at[tile],
                send_sem=x_send.at[1, k - 1], recv_sem=x_recv.at[1, k - 1],
                device_id={"tile": (tile + k) % T}, device_id_type=MESH,
            )
        )
    for c in copies:
        c.start()
    for copy in loads[5:]:
        copy.wait()
    fown = fst[:, own]
    fcat = jnp.concatenate([fown[:M], fown[M:]], 1)
    gown = gown_v[...]
    wait_all(copies)

    for c in range(2):
        s = jnp.concatenate([spec[t, c * Q : (c + 1) * Q] for t in range(T)], 0)
        s_sw = swap(s)
        s2 = jnp.where(left64, -s_sw, s_sw)
        s2_sw = jnp.where(left64, s, -s)
        for k in range(K):
            a1 = prr[k] * s + pii[k] * s_sw
            a2 = prr[k] * s2 + pii[k] * s2_sw
            both = jnp.concatenate([a1, a2], 0).astype(BF16)
            u_all[k * R : (k + 1) * R] = dot(gown, both).astype(BF16)
        for b in range(T):
            cols = slice(b * R, (b + 1) * R)
            field = dot(u_all[...], inv[:, b * 2 * R : (b + 1) * 2 * R])
            intensity = jnp.zeros((R, R), F32)
            for k in range(K):
                fr = field[k * R : (k + 1) * R, :R]
                fi = field[k * R : (k + 1) * R, R:]
                intensity += fr * fr + fi * fi
            image = 1.0 / (1.0 + jnp.exp(-STEEPNESS * (intensity - THRESHOLD)))
            resist[c, :, cols] = image.astype(BF16)
            slope = (image - targets[c, :, cols].astype(F32)) * (2.0 * STEEPNESS) * image * (1.0 - image)
            slope2 = jnp.concatenate([slope, slope], 1)
            for k in range(K):
                pull[k * R : (k + 1) * R, b * 2 * R : (b + 1) * 2 * R] = (
                    slope2 * field[k * R : (k + 1) * R]
                ).astype(BF16)
        folded = dot(pull[...], adj[...]).astype(BF16)
        g_a = jnp.zeros((M, 2 * M), F32)
        g_b = jnp.zeros((M, 2 * M), F32)
        for k in range(K):
            fk = folded[k * R : (k + 1) * R]
            ga = dot(fcat, jnp.concatenate([fk[:, : 2 * M], fk[:, 2 * M :]], 0))
            g_a += prr[k] * ga
            g_b += pii[k] * ga
        grad = g_a + swap(g_b)
        for t in range(T):
            part[1, t, c * Q : (c + 1) * Q] = grad[t * Q : (t + 1) * Q]

    wait_all(tile_scatter(1))
    g2[pl.ds(slot * 2, 2)] = tile_sum(1).astype(BF16).reshape(2, Q, 2 * M)

    def make_lists():
        for m, rows in enumerate(pair_lists(ids_all[...].reshape(CTX, 128), q)):
            lists[m * 8 : (m + 1) * 8] = rows

    gather(g2, 1, make_lists, lambda: None)


def pair_kernel(where_s, lists_v, ids_v, g2, resist_v, out, resist, lists_s, ids_s, acc, sem, out_sem):
    resist_copy = pltpu.make_async_copy(resist_v, resist, out_sem)
    copy = pltpu.make_async_copy(lists_v, lists_s, sem)
    copy.start()
    resist_copy.start()
    me = where_s[0]
    rates = turn_rates(where_s[1])
    copy.wait()

    def terms(context, r, s, weight):
        g = g2[context].astype(F32)
        cs = cos_sin(rates, r.astype(F32), s.astype(F32))
        if weight is not None:
            cs = cs * weight.astype(F32)
        return g * cs, swap(g) * cs

    block = 8
    left = left_half((Q, 2 * M))
    for m in range(2):

        def step(i, carry):
            sum_a, sum_b = carry
            for b in range(block):
                k = i * block + b
                add_a, add_b = terms(*[lists_s[m * 8 + row, k] for row in range(4)])
                sum_a += add_a
                sum_b += add_b
            return sum_a, sum_b

        zero = jnp.zeros((Q, 2 * M), F32)
        sum_a, sum_b = lax.fori_loop(0, (lists_s[m * 8 + 4, 0] + block - 1) // block, step, (zero, zero))
        acc[0] = sum_a
        acc[1] = sum_b

        @pl.when(lists_s[m * 8 + 5, 0] > 0)
        def _():
            copy = pltpu.make_async_copy(ids_v, ids_s, sem)
            copy.start()
            copy.wait()

            def host(h, _):
                @pl.when(lists_s[m * 8 + 6, h] > 1)
                def _():
                    def one(j, _):
                        @pl.when(ids_s[h, 0, j] == 2 * me + m)
                        def _():
                            add_a, add_b = terms(2 * h + j // SRC, ids_s[h, 0, 32 + j], ids_s[h, 0, 64 + j], None)
                            acc[0] += add_a
                            acc[1] += add_b

                        return 0

                    lax.fori_loop(0, PAIRS, one, 0)

                return 0

            lax.fori_loop(0, CTX, host, 0)

        sum_a, sum_b = acc[0], acc[1]
        out[m * Q : (m + 1) * Q] = jnp.where(left, sum_a - swap(sum_a), sum_b + swap(sum_b)).astype(BF16)
    resist_copy.wait()


def rows_kernel(gq, rows, x_send, x_recv):
    tile = lax.axis_index("tile")
    barrier = pltpu.get_barrier_semaphore()
    for k in range(1, T):
        pl.semaphore_signal(barrier, inc=1, device_id={"tile": (tile + k) % T}, device_id_type=MESH)
    rows[tile] = gq[...]
    pl.semaphore_wait(barrier, T - 1)
    copies = []
    for k in range(1, T):
        copies.append(
            pltpu.make_async_remote_copy(
                src_ref=rows.at[tile], dst_ref=rows.at[tile],
                send_sem=x_send.at[k - 1], recv_sem=x_recv.at[k - 1],
                device_id={"tile": (tile + k) % T}, device_id_type=MESH,
            )
        )
    for c in copies:
        c.start()
    wait_all(copies)


def last_kernel(rows, p_st, q_st, out, held, sem):
    left = left_half((M, 2 * M))
    copies = []
    for m in range(2):
        g = jnp.concatenate([rows[t, m * Q : (m + 1) * Q].astype(F32) for t in range(T)], 0)
        turned = swap(g)
        both = jnp.concatenate([g, jnp.where(left, turned, -turned)], 0).astype(BF16)
        lifted = dot(p_st[...], both, ((0,), (0,))).astype(BF16)
        held[m] = dot(lifted, q_st[...])
        copies.append(pltpu.make_async_copy(held.at[m], out.at[m], sem.at[m]))
        copies[-1].start()
    wait_all(copies)


def local(masks, blur_rows, blur_cols, pupils, targets, context_masters, offsets):
    vmem = pl.BlockSpec(memory_space=pltpu.VMEM)
    smem = pl.BlockSpec(memory_space=pltpu.SMEM)
    hbm = pl.BlockSpec(memory_space=pltpu.HBM)
    dma = pltpu.SemaphoreType.DMA
    stay = functools.partial(pltpu.with_memory_space_constraint, memory_space=pltpu.HBM)
    gap = jnp.zeros((32 - PAIRS,), jnp.int32)
    shifts = offsets.reshape(PAIRS, 2)
    packed = jnp.concatenate(
        [context_masters.reshape(-1), gap, shifts[:, 0], gap, shifts[:, 1], gap, jnp.zeros((32,), jnp.int32)]
    ).reshape(1, 128)
    resist_v, g2, ids_all, lists, p_st, q_st = pl.pallas_call(
        main_kernel,
        out_shape=(
            jax.ShapeDtypeStruct((2, R, N), BF16),
            jax.ShapeDtypeStruct((2 * CTX, Q, 2 * M), BF16),
            jax.ShapeDtypeStruct((CTX, 1, 128), jnp.int32),
            jax.ShapeDtypeStruct((16, 128), jnp.int32),
            jax.ShapeDtypeStruct((2 * M, R), BF16),
            jax.ShapeDtypeStruct((2 * M, N), BF16),
        ),
        in_specs=[hbm] * 5 + [smem, vmem] + [hbm] * 4,
        out_specs=(vmem,) * 6,
        scratch_shapes=[
            pltpu.VMEM((2, R, N), BF16),
            pltpu.VMEM((N, R), BF16),
            pltpu.VMEM((N, N), BF16),
            pltpu.VMEM((K, M, 2 * M), F32),
            pltpu.VMEM((2, R, N), BF16),
            pltpu.VMEM((2 * M, N), BF16),
            pltpu.VMEM((R, 2 * M), BF16),
            pltpu.VMEM((2 * M, 2 * N), BF16),
            pltpu.VMEM((2 * N, 4 * M), BF16),
            pltpu.VMEM((2 * CTX, Q, 2 * M), BF16),
            pltpu.VMEM((2, T, 2 * Q, 2 * M), F32),
            pltpu.VMEM((2, T - 1, 2 * Q, 2 * M), F32),
            pltpu.VMEM((T, 2 * Q, 2 * M), F32),
            pltpu.VMEM((K, M, 2 * M), F32),
            pltpu.VMEM((K, M, 2 * M), F32),
            pltpu.VMEM((K * R, 2 * M), BF16),
            pltpu.VMEM((K * R, 2 * N), BF16),
            pltpu.VMEM((PAIRS, Q, 2 * M), F32),
            dma((9,)),
            dma((3, T - 1)),
            dma((3, T - 1)),
            dma((2, SIDE)),
            dma((2, SIDE)),
            dma((2, SIDE, SIDE)),
            dma((2, SIDE, SIDE)),
            dma((2, SIDE)),
            dma((2, SIDE)),
            dma((3, SIDE)),
            dma((3, SIDE)),
        ],
        compiler_params=pltpu.CompilerParams(
            collective_id=0, has_side_effects=True, vmem_limit_bytes=40 << 20
        ),
        name="main",
    )(
        *map(stay, (masks, blur_rows, blur_cols, pupils, targets)),
        packed,
        packed.reshape(1, 1, 128),
        *map(stay, map(jnp.asarray, tables())),
    )
    where = jnp.stack([lax.axis_index("ctx"), lax.axis_index("tile")]).astype(jnp.int32)
    gq, resist = pl.pallas_call(
        pair_kernel,
        out_shape=(
            jax.ShapeDtypeStruct((2 * Q, 2 * M), BF16),
            jax.ShapeDtypeStruct((2, R, N), BF16),
        ),
        in_specs=[smem] + [vmem] * 4,
        out_specs=(vmem, hbm),
        scratch_shapes=[
            pltpu.SMEM((16, 128), jnp.int32),
            pltpu.SMEM((CTX, 1, 128), jnp.int32),
            pltpu.VMEM((2, Q, 2 * M), F32),
            dma,
            dma,
        ],
        compiler_params=pltpu.CompilerParams(vmem_limit_bytes=32 << 20),
        name="pairs",
    )(where, lists, ids_all, g2, resist_v)
    rows = pl.pallas_call(
        rows_kernel,
        out_shape=jax.ShapeDtypeStruct((T, 2 * Q, 2 * M), BF16),
        in_specs=[vmem],
        out_specs=vmem,
        scratch_shapes=[dma((T - 1,)), dma((T - 1,))],
        compiler_params=pltpu.CompilerParams(
            collective_id=1, has_side_effects=True, vmem_limit_bytes=32 << 20
        ),
        name="rows",
    )(gq)
    mask_grad = pl.pallas_call(
        last_kernel,
        out_shape=jax.ShapeDtypeStruct((2, R, N), F32),
        in_specs=[vmem] * 3,
        out_specs=hbm,
        scratch_shapes=[pltpu.VMEM((2, R, N), F32), dma((2,))],
        compiler_params=pltpu.CompilerParams(vmem_limit_bytes=32 << 20),
        name="last",
    )(rows, p_st, q_st)
    return (resist, mask_grad)


def solution(mesh):
    placed = (
        P("ctx", "tile", None),
        P(),
        P(),
        P(),
        P("ctx", "tile", None),
        P("ctx", None),
        P("ctx", None, None),
    )
    return jax.shard_map(
        local,
        mesh=mesh,
        in_specs=placed,
        out_specs=(P("ctx", "tile", None), P("ctx", "tile", None)),
        check_vma=False,
    )
```

```python
import functools
import math

import jax
import jax.numpy as jnp
import ml_dtypes
import numpy as np
from jax import lax
from jax.experimental import pallas as pl
from jax.experimental.pallas import tpu as pltpu
from jax.sharding import PartitionSpec as P

STEEPNESS = 4.0
THRESHOLD = 1.0
N = 512
M = 64
K = 6
T = 4
R = N // T
H = M // (2 * T)
Q = 16
SIDE = 8
CTX = 2 * SIDE * SIDE
SRC = 12
PAIRS = 2 * SRC
MESH = pl.DeviceIdType.MESH
F32 = jnp.float32
BF16 = jnp.bfloat16
NEAR_FIRST = (1, 7, 2, 6, 3, 5, 4)


def tables():
    freq = (np.arange(M) - M // 2) % N
    angle = (freq[:, None] * np.arange(N)[None, :] % N) * (2.0 * math.pi / N)
    cos = np.cos(angle) / math.sqrt(N)
    sin = np.sin(angle) / math.sqrt(N)
    fst = np.concatenate([cos, -sin], 0)
    gcat = np.concatenate([cos.T, sin.T], 1)
    inv = np.concatenate([np.concatenate([cos, sin], 1), np.concatenate([-sin, cos], 1)], 0)
    adj = np.concatenate([np.concatenate([cos.T, -sin.T], 1), np.concatenate([sin.T, cos.T], 1)], 0)
    adj = np.concatenate([adj, -adj[:, M:], adj[:, :M]], 1)
    order = np.arange(2 * N).reshape(2, T, N // T).transpose(1, 0, 2).reshape(-1)
    return [t.astype(ml_dtypes.bfloat16) for t in (fst, gcat, inv[:, order], adj[order])]


def sine_coefficients():
    w = 0.25 * np.cos(np.pi * (np.arange(400) + 0.5) / 400)
    powers = np.stack([w ** (2 * i + 1) for i in range(6)], 1)
    return [float(c) for c in np.linalg.lstsq(powers, np.sin(2 * np.pi * w), rcond=None)[0]]


SINE = sine_coefficients()


def swap(a):
    return pltpu.roll(a, M, 1)


def left_half(shape):
    return lax.broadcasted_iota(jnp.int32, shape, 1) < M


def grid(shape):
    return lax.broadcasted_iota(jnp.int32, shape, 0), lax.broadcasted_iota(jnp.int32, shape, 1)


def turn_rates(tile):
    row, lane = grid((Q, 2 * M))
    v = lane % M
    plain = row < H
    early = v <= M // 2
    f_u = jnp.where(plain, row + (tile * H - M // 2), jnp.where(early, 0, v - M // 2))
    f_v = jnp.where(plain | early, v - M // 2, -(M // 2))
    late = jnp.where(lane < M, 0.0, 0.25).astype(F32)
    return f_u.astype(F32) * (1.0 / N), f_v.astype(F32) * (1.0 / N), late


def from_rows(a):
    row, lane = grid(a.shape)
    real = jnp.where((lane == row + M // 2) & (row > 0), jnp.broadcast_to(a[:, 0:1], a.shape), 0.0)
    imag = jnp.where((lane == row + M + M // 2) & (row > 0), jnp.broadcast_to(a[:, M : M + 1], a.shape), 0.0)
    return jnp.sum(real + imag, axis=0, keepdims=True)


def to_rows(e):
    shape = (M // 2, 2 * M)
    row, lane = grid(shape)
    wide = jnp.broadcast_to(e, shape)
    real = jnp.sum(jnp.where((lane == row + M // 2) & (row > 0), wide, 0.0), axis=1, keepdims=True)
    imag = jnp.sum(jnp.where((lane == row + M + M // 2) & (row > 0), wide, 0.0), axis=1, keepdims=True)
    first = jnp.where((row == 0) & (lane % M <= M // 2), wide, 0.0)
    return first + jnp.where(lane == 0, real, 0.0) + jnp.where(lane == M, imag, 0.0)


def exact(a, b):
    return lax.dot_general(
        a, b, (((1,), (0,)), ((), ())), precision=lax.Precision.HIGHEST, preferred_element_type=F32
    )


def mirrored(a):
    src, dst = grid((2 * M, 2 * M))
    both = jnp.where((src + dst == M) & (src < M) & (dst < M), 1.0, 0.0) - jnp.where((src + dst == 3 * M) & (src >= M), 1.0, 0.0)
    return exact(a, both)


def flipped(a):
    row, col = grid((M // 2, M // 2))
    return exact(jnp.where(row + col == M // 2, 1.0, 0.0), a)


def expand(half, e):
    row, lane = grid((M // 2, 2 * M))
    e_mirrored = mirrored(jnp.broadcast_to(e, (8, 2 * M)))[0:1]
    first = jnp.where((row == 0) & (lane % M > M // 2), jnp.broadcast_to(e_mirrored, row.shape), 0.0)
    return jnp.concatenate([half, flipped(mirrored(half)) + first + to_rows(e)], 0)


def fold(grad):
    low = grad[M // 2 :]
    turned = mirrored(low)
    v = lax.broadcasted_iota(jnp.int32, (1, 2 * M), 1) % M
    e = jnp.where(v <= M // 2, low[0:1], 0.0) + jnp.where((v > 0) & (v < M // 2), turned[0:1], 0.0)
    return grad[: M // 2] + flipped(turned), e + from_rows(low)


def half_of(spectrum):
    low = spectrum[M // 2 :]
    v = lax.broadcasted_iota(jnp.int32, (1, 2 * M), 1) % M
    return spectrum[: M // 2], jnp.where(v <= M // 2, low[0:1], 0.0) + from_rows(low)


def padded(e):
    return jnp.where(lax.broadcasted_iota(jnp.int32, (Q - H, 2 * M), 0) == 0, jnp.broadcast_to(e, (Q - H, 2 * M)), 0.0)


def pick(block, es, second):
    return jnp.concatenate(
        [jnp.where(second, block[H:], block[:H]), padded(jnp.where(second, es[1:2], es[0:1]))], 0
    )


def cos_sin(rates, r, s):
    y = rates[0] * r + rates[1] * s - rates[2]
    y = y - jnp.floor(y + 0.5)
    w = 0.25 - jnp.abs(y)
    z = w * w
    total = jnp.full_like(z, SINE[-1])
    for c in SINE[-2::-1]:
        total = total * z + c
    return total * w


def dot(a, b, dims=((1,), (0,))):
    return lax.dot_general(a, b, (dims, ((), ())), preferred_element_type=F32)


def wait_all(copies):
    for c in copies:
        c.wait()


def near_first(i):
    return (i % 2) * ((i + 1) // 2) + (1 - i % 2) * (SIDE - i // 2)


def pair_lists(ids, me):
    lane = lax.broadcasted_iota(jnp.int32, (CTX, 128), 1)
    sub = lax.broadcasted_iota(jnp.int32, (CTX, 128), 0)
    sub8 = lax.broadcasted_iota(jnp.int32, (8, 128), 0)
    lane8 = lax.broadcasted_iota(jnp.int32, (8, 128), 1).astype(F32)
    ones = jnp.full((8, 128), 1.0, BF16)
    before = jnp.where(sub < lane, 1.0, 0.0).astype(BF16)
    r = pltpu.roll(ids, 128 - 32, 1)
    s = pltpu.roll(ids, 128 - 64, 1)
    second = jnp.where(lane >= SRC, 1.0, 0.0)
    values = [second] + [v.astype(F32) for v in (r >> 4, r & 15, s >> 4, s & 15)]
    lists = []
    for m in range(2):
        match = jnp.where((ids == 2 * me + m) & (lane < PAIRS), 1.0, 0.0)
        count = dot(ones, match.astype(BF16), ((1,), (1,)))
        found = [dot(ones, (match * v).astype(BF16), ((1,), (1,))) for v in values]
        single = jnp.where(count == 1.0, 1.0, 0.0)
        rank = dot(single.astype(BF16), before)
        hot = jnp.where(
            (jnp.broadcast_to(rank[0:1], (CTX, 128)) == sub.astype(F32))
            & (jnp.broadcast_to(single[0:1], (CTX, 128)) > 0.5),
            1.0, 0.0,
        ).astype(BF16)
        load = jnp.where(sub8 == 5, single, 0.0)
        load = jnp.where(sub8 == 0, single * (2.0 * lane8 + found[0]), load)
        for i in range(1, 5):
            load = jnp.where(sub8 == i, single * found[i], load)
        listed = dot(load.astype(BF16), hot, ((1,), (1,)))
        line = [jnp.broadcast_to(listed[i : i + 1], (8, 128)) for i in range(6)]
        n_single = jnp.sum(single, axis=1, keepdims=True)
        n_multi = jnp.sum(jnp.where(count > 1.5, 1.0, 0.0), axis=1, keepdims=True)
        rows = jnp.where(sub8 == 6, count, line[0])
        rows = jnp.where(sub8 == 1, 16.0 * line[1] + line[2], rows)
        rows = jnp.where(sub8 == 2, 16.0 * line[3] + line[4], rows)
        rows = jnp.where(sub8 == 3, line[5], rows)
        rows = jnp.where(sub8 == 4, n_single, rows)
        rows = jnp.where(sub8 == 5, n_multi, rows)
        lists.append(rows.astype(jnp.int32))
    return lists


def main_kernel(
    masks_h, br_h, bc_h, pupils_h, targets_h, ids_h, shifts_h, fst_h, gcat_h, inv_h, adj_h,
    resist, g2, e2, ids_all, lists, p_out, q_out,
    masks, br, bc, pupils, targets, fst, gown_v, inv, adj,
    ids_s, shifts_s, g1, e1, part, part_in, spec, prr, pii, u_all, pull, phases,
    load_sem, x_send, x_recv, a_send, a_recv, f_send, f_recv, s_send, s_recv, i_send, i_recv, e_send, e_recv,
):
    tile = lax.axis_index("tile")
    q = lax.axis_index("ctx")
    core, y, z = q % 2, (q // 2) % SIDE, q // (2 * SIDE)
    major = z + core * (y - z)
    minor = y + core * (z - y)
    half = core * (SIDE * SIDE)
    slot = half + major * SIDE + minor
    own = pl.ds(pl.multiple_of(tile * R, R), R)

    loads = [
        pltpu.make_async_copy(src, dst, load_sem.at[i])
        for i, (src, dst) in enumerate(
            [
                (fst_h, fst),
                (br_h.at[:, own], br),
                (bc_h, bc),
                (masks_h, masks),
                (pupils_h, pupils),
                (gcat_h.at[own, :], gown_v),
                (inv_h, inv),
                (targets_h, targets),
                (adj_h, adj),
                (ids_h, ids_s),
                (shifts_h, shifts_s),
            ]
        )
    ]
    for copy in loads:
        copy.start()

    def ctx_id(mj, mn):
        zz = mj + core * (mn - mj)
        yy = mn + core * (mj - mn)
        return zz * (2 * SIDE) + yy * 2 + core

    sibling = q + 1 - 2 * core
    barrier = pltpu.get_barrier_semaphore()
    for k in range(1, SIDE):
        pl.semaphore_signal(barrier, inc=1, device_id={"ctx": ctx_id(major, (minor + k) % SIDE)}, device_id_type=MESH)
        pl.semaphore_signal(barrier, inc=1, device_id={"ctx": ctx_id((major + k) % SIDE, minor)}, device_id_type=MESH)
    for k in range(1, T):
        pl.semaphore_signal(barrier, inc=1, device_id={"tile": (tile + k) % T}, device_id_type=MESH)
    pl.semaphore_signal(barrier, inc=1, device_id={"ctx": sibling}, device_id_type=MESH)

    def put(step, i, half_rows, e):
        for t in range(T):
            part[step, t, i * Q : i * Q + H] = half_rows[t * H : (t + 1) * H]
            part[step, t, i * Q + H : (i + 1) * Q] = padded(e) if t == 0 else jnp.zeros((Q - H, 2 * M), F32)

    loads[0].wait()
    loads[1].wait()
    table = fst[...]
    p_st = dot(table, br[...]).astype(BF16)
    loads[2].wait()
    q_st = dot(table, bc[...]).astype(BF16)
    p_out[...] = p_st
    q_out[...] = q_st
    qq = jnp.concatenate([q_st, -q_st[M:], q_st[:M]], 0)
    pcat = jnp.concatenate([p_st[:M], p_st[M:]], 1)
    loads[3].wait()
    for m in range(2):
        a = dot(masks[m], qq, ((1,), (1,))).astype(BF16)
        s = dot(pcat, jnp.concatenate([a[:, : 2 * M], a[:, 2 * M :]], 0))
        put(0, m, *half_of(s))

    pl.semaphore_wait(barrier, T - 1 + 2 * (SIDE - 1) + 1)

    def tile_scatter(step):
        copies = []
        for k in range(1, T):
            to = (tile + k) % T
            copies.append(
                pltpu.make_async_remote_copy(
                    src_ref=part.at[step, to], dst_ref=part_in.at[step, k - 1],
                    send_sem=x_send.at[2 * step, k - 1], recv_sem=x_recv.at[2 * step, k - 1],
                    device_id={"tile": to}, device_id_type=MESH,
                )
            )
        for c in copies:
            c.start()
        return copies

    def tile_sum(step):
        return (part[step, tile] + part_in[step, 0]) + (part_in[step, 1] + part_in[step, 2])

    def to_ctx(ref, place, send_sem, recv_sem, to):
        return pltpu.make_async_remote_copy(
            src_ref=ref.at[place], dst_ref=ref.at[place], send_sem=send_sem, recv_sem=recv_sem,
            device_id={"ctx": to}, device_id_type=MESH,
        )

    def gather(buf, step, between, late, end):
        def along_minor(k):
            return to_ctx(
                buf, pl.ds(slot, 1), a_send.at[step, k], a_recv.at[step, k], ctx_id(major, (minor + k) % SIDE)
            )

        def along_major(came, k):
            place = pl.ds(half + major * SIDE + (minor + SIDE - came) % SIDE, 1)
            return to_ctx(
                buf, place, f_send.at[step, came, k], f_recv.at[step, came, k], ctx_id((major + k) % SIDE, minor)
            )

        def to_sibling(k):
            place = pl.ds(half + (major + SIDE - k) % SIDE * SIDE, SIDE)
            return to_ctx(buf, place, s_send.at[step, k], s_recv.at[step, k], sibling)

        for k in NEAR_FIRST:
            along_minor(k).start()
        for k in NEAR_FIRST:
            along_major(0, k).start()
        between()

        def forward(i, _):
            came = near_first(i)
            along_minor(came).wait_recv()
            for k in NEAR_FIRST:
                along_major(came, k).start()
            return 0

        lax.fori_loop(1, SIDE, forward, 0)
        to_sibling(0).start()
        late()

        def arrive(i, _):
            k = near_first(i)
            for came in range(SIDE):
                along_major(came, k).wait_recv()
            to_sibling(k).start()
            return 0

        lax.fori_loop(1, SIDE, arrive, 0)
        end()
        for k in range(SIDE):
            to_sibling(k).wait()
        for k in range(1, SIDE):
            along_minor(k).wait_send()

        def sent(k, _):
            for came in range(SIDE):
                along_major(came, k).wait_send()
            return 0

        lax.fori_loop(1, SIDE, sent, 0)

    def line(buf, send, recv, phase):
        copies = []
        if phase == 2:
            copies.append(to_ctx(buf, pl.ds(half, SIDE * SIDE), send.at[2, 0], recv.at[2, 0], sibling))
        else:
            for k in NEAR_FIRST:
                if phase == 0:
                    place, to = pl.ds(slot, 1), ctx_id(major, (minor + k) % SIDE)
                else:
                    place, to = pl.ds(half + major * SIDE, SIDE), ctx_id((major + k) % SIDE, minor)
                copies.append(to_ctx(buf, place, send.at[phase, k], recv.at[phase, k], to))
        for c in copies:
            c.start()
        return copies

    def spread_out(step, buf, es):
        total = tile_sum(step)
        buf[pl.ds(slot, 1)] = jnp.concatenate([total[:H], total[Q : Q + H]], 0).astype(BF16).reshape(1, 2 * H, 2 * M)
        es[pl.ds(slot, 1)] = jnp.concatenate([total[H : H + 1], total[Q + H : Q + H + 1]], 0).reshape(1, 2, 2 * M)
        e_sems = (e_send.at[step], e_recv.at[step])
        pending = []

        def between():
            pending.append(line(es, *e_sems, 0))
            if step == 0:
                wait_all(ids_copies.pop())
                ids_copies.append(line(ids_all, i_send, i_recv, 1))
            else:
                for m, rows in enumerate(pair_lists(ids_all[...].reshape(CTX, 128), q)):
                    lists[m * 8 : (m + 1) * 8] = rows

        def late():
            wait_all(pending.pop())
            pending.append(line(es, *e_sems, 1))
            if step == 0:
                wait_all(ids_copies.pop())
                ids_copies.append(line(ids_all, i_send, i_recv, 2))

        def end():
            wait_all(pending.pop())
            pending.append(line(es, *e_sems, 2))

        gather(buf, step, between, late, end)
        wait_all(pending.pop())

    copies = tile_scatter(0)
    loads[9].wait()
    loads[10].wait()
    lane = lax.broadcasted_iota(jnp.int32, (1, 128), 1)
    own_ids = jnp.zeros((1, 128), jnp.int32)
    for c in range(2):
        for j in range(SRC):
            for place, value in ((0, ids_s[c, j]), (32, shifts_s[c, 0, j]), (64, shifts_s[c, 1, j])):
                own_ids = jnp.where(lane == place + c * SRC + j, value, own_ids)
    ids_all[pl.ds(slot, 1)] = own_ids.reshape(1, 1, 128)
    ids_copies = [line(ids_all, i_send, i_recv, 0)]

    rates = turn_rates(tile)
    for p in range(PAIRS):
        c, j = p // SRC, p % SRC
        phases[p] = cos_sin(rates, shifts_s[c, 0, j].astype(F32), shifts_s[c, 1, j].astype(F32))
    left64 = left_half((M, 2 * M))
    loads[4].wait()
    for k in range(K):
        pk = pupils[k]
        turned = swap(pk)
        prr[k] = jnp.where(left64, pk, turned)
        pii[k] = jnp.where(left64, -turned, pk)

    wait_all(copies)
    spread_out(0, g1, e1)
    wait_all(ids_copies.pop())

    leftq = left_half((Q, 2 * M))
    for c in range(2):
        sum_a = jnp.zeros((Q, 2 * M), F32)
        sum_b = jnp.zeros((Q, 2 * M), F32)
        for j in range(SRC):
            p = c * SRC + j
            master = ids_s[c, j]
            owner = master >> 1
            ocore = owner & 1
            oy = (owner >> 1) & (SIDE - 1)
            oz = owner >> 4
            place = ocore * (SIDE * SIDE) + oz * SIDE + oy + ocore * (SIDE - 1) * (oy - oz)
            g = pick(g1[place].astype(F32), e1[place], (master & 1) > 0)
            cs = phases[p]
            sum_a += g * cs
            sum_b += swap(g) * cs
        spec[tile, c * Q : (c + 1) * Q] = jnp.where(leftq, sum_a + swap(sum_a), swap(sum_b) - sum_b)
    copies = []
    for k in range(1, T):
        copies.append(
            pltpu.make_async_remote_copy(
                src_ref=spec.at[tile], dst_ref=spec.at[tile],
                send_sem=x_send.at[1, k - 1], recv_sem=x_recv.at[1, k - 1],
                device_id={"tile": (tile + k) % T}, device_id_type=MESH,
            )
        )
    for c in copies:
        c.start()
    for copy in loads[5:9]:
        copy.wait()
    fown = fst[:, own]
    fcat = jnp.concatenate([fown[:M], fown[M:]], 1)
    gown = gown_v[...]
    wait_all(copies)

    for c in range(2):
        s = expand(
            jnp.concatenate([spec[t, c * Q : c * Q + H] for t in range(T)], 0), spec[0, c * Q + H : c * Q + H + 1]
        )
        s_sw = swap(s)
        s2 = jnp.where(left64, -s_sw, s_sw)
        s2_sw = jnp.where(left64, s, -s)
        for k in range(K):
            a1 = prr[k] * s + pii[k] * s_sw
            a2 = prr[k] * s2 + pii[k] * s2_sw
            both = jnp.concatenate([a1, a2], 0).astype(BF16)
            u_all[k * R : (k + 1) * R] = dot(gown, both).astype(BF16)
        for b in range(T):
            cols = slice(b * R, (b + 1) * R)
            field = dot(u_all[...], inv[:, b * 2 * R : (b + 1) * 2 * R])
            intensity = jnp.zeros((R, R), F32)
            for k in range(K):
                fr = field[k * R : (k + 1) * R, :R]
                fi = field[k * R : (k + 1) * R, R:]
                intensity += fr * fr + fi * fi
            image = 1.0 / (1.0 + jnp.exp(-STEEPNESS * (intensity - THRESHOLD)))
            resist[c, :, cols] = image.astype(BF16)
            slope = (image - targets[c, :, cols].astype(F32)) * (2.0 * STEEPNESS) * image * (1.0 - image)
            slope2 = jnp.concatenate([slope, slope], 1)
            for k in range(K):
                pull[k * R : (k + 1) * R, b * 2 * R : (b + 1) * 2 * R] = (
                    slope2 * field[k * R : (k + 1) * R]
                ).astype(BF16)
        folded = dot(pull[...], adj[...]).astype(BF16)
        g_a = jnp.zeros((M, 2 * M), F32)
        g_b = jnp.zeros((M, 2 * M), F32)
        for k in range(K):
            fk = folded[k * R : (k + 1) * R]
            ga = dot(fcat, jnp.concatenate([fk[:, : 2 * M], fk[:, 2 * M :]], 0))
            g_a += prr[k] * ga
            g_b += pii[k] * ga
        grad = g_a + swap(g_b)
        put(1, c, *fold(grad))

    wait_all(tile_scatter(1))
    spread_out(1, g2, e2)


def pair_kernel(lists_v, ids_v, g2, e2, resist_v, out, resist, lists_s, ids_s, acc, sem, out_sem):
    resist_copy = pltpu.make_async_copy(resist_v, resist, out_sem)
    copy = pltpu.make_async_copy(lists_v, lists_s, sem)
    copy.start()
    resist_copy.start()
    me = lax.axis_index("ctx")
    rates = turn_rates(lax.axis_index("tile"))
    copy.wait()

    def terms(context, r, s, weight):
        host = context // 2
        g = pick(g2[host].astype(F32), e2[host], context % 2 > 0)
        cs = cos_sin(rates, r.astype(F32), s.astype(F32))
        if weight is not None:
            cs = cs * weight.astype(F32)
        return g * cs, swap(g) * cs

    block = 8
    left = left_half((Q, 2 * M))
    for m in range(2):

        def step(i, carry):
            sum_a, sum_b = carry
            for b in range(block):
                k = i * block + b
                add_a, add_b = terms(*[lists_s[m * 8 + row, k] for row in range(4)])
                sum_a += add_a
                sum_b += add_b
            return sum_a, sum_b

        zero = jnp.zeros((Q, 2 * M), F32)
        sum_a, sum_b = lax.fori_loop(0, (lists_s[m * 8 + 4, 0] + block - 1) // block, step, (zero, zero))
        acc[0] = sum_a
        acc[1] = sum_b

        @pl.when(lists_s[m * 8 + 5, 0] > 0)
        def _():
            copy = pltpu.make_async_copy(ids_v, ids_s, sem)
            copy.start()
            copy.wait()

            def host(h, _):
                @pl.when(lists_s[m * 8 + 6, h] > 1)
                def _():
                    def one(j, _):
                        @pl.when(ids_s[h, 0, j] == 2 * me + m)
                        def _():
                            add_a, add_b = terms(2 * h + j // SRC, ids_s[h, 0, 32 + j], ids_s[h, 0, 64 + j], None)
                            acc[0] += add_a
                            acc[1] += add_b

                        return 0

                    lax.fori_loop(0, PAIRS, one, 0)

                return 0

            lax.fori_loop(0, CTX, host, 0)

        sum_a, sum_b = acc[0], acc[1]
        out[m * Q : (m + 1) * Q] = jnp.where(left, sum_a - swap(sum_a), sum_b + swap(sum_b)).astype(BF16)
    resist_copy.wait()


def rows_kernel(gq, rows, x_send, x_recv):
    tile = lax.axis_index("tile")
    barrier = pltpu.get_barrier_semaphore()
    for k in range(1, T):
        pl.semaphore_signal(barrier, inc=1, device_id={"tile": (tile + k) % T}, device_id_type=MESH)
    rows[tile] = gq[...]
    pl.semaphore_wait(barrier, T - 1)
    copies = []
    for k in range(1, T):
        copies.append(
            pltpu.make_async_remote_copy(
                src_ref=rows.at[tile], dst_ref=rows.at[tile],
                send_sem=x_send.at[k - 1], recv_sem=x_recv.at[k - 1],
                device_id={"tile": (tile + k) % T}, device_id_type=MESH,
            )
        )
    for c in copies:
        c.start()
    wait_all(copies)


def last_kernel(rows, p_st, q_st, out, held, sem):
    left = left_half((M, 2 * M))
    copies = []
    for m in range(2):
        parts = [rows[t].astype(F32)[m * Q : (m + 1) * Q] for t in range(T)]
        g = jnp.concatenate([part[:H] for part in parts] + [to_rows(parts[0][H : H + 1])], 0)
        turned = swap(g)
        both = jnp.concatenate([g, jnp.where(left, turned, -turned)], 0).astype(BF16)
        lifted = dot(p_st[...], both, ((0,), (0,))).astype(BF16)
        held[m] = dot(lifted, q_st[...])
        copies.append(pltpu.make_async_copy(held.at[m], out.at[m], sem.at[m]))
        copies[-1].start()
    wait_all(copies)


def local(masks, blur_rows, blur_cols, pupils, targets, context_masters, offsets):
    vmem = pl.BlockSpec(memory_space=pltpu.VMEM)
    hbm = pl.BlockSpec(memory_space=pltpu.HBM)
    dma = pltpu.SemaphoreType.DMA
    stay = functools.partial(pltpu.with_memory_space_constraint, memory_space=pltpu.HBM)
    resist_v, g2, e2, ids_all, lists, p_st, q_st = pl.pallas_call(
        main_kernel,
        out_shape=(
            jax.ShapeDtypeStruct((2, R, N), BF16),
            jax.ShapeDtypeStruct((CTX, 2 * H, 2 * M), BF16),
            jax.ShapeDtypeStruct((CTX, 2, 2 * M), F32),
            jax.ShapeDtypeStruct((CTX, 1, 128), jnp.int32),
            jax.ShapeDtypeStruct((16, 128), jnp.int32),
            jax.ShapeDtypeStruct((2 * M, R), BF16),
            jax.ShapeDtypeStruct((2 * M, N), BF16),
        ),
        in_specs=[hbm] * 11,
        out_specs=(vmem,) * 7,
        scratch_shapes=[
            pltpu.VMEM((2, R, N), BF16),
            pltpu.VMEM((N, R), BF16),
            pltpu.VMEM((N, N), BF16),
            pltpu.VMEM((K, M, 2 * M), F32),
            pltpu.VMEM((2, R, N), BF16),
            pltpu.VMEM((2 * M, N), BF16),
            pltpu.VMEM((R, 2 * M), BF16),
            pltpu.VMEM((2 * M, 2 * N), BF16),
            pltpu.VMEM((2 * N, 4 * M), BF16),
            pltpu.SMEM((2, SRC), jnp.int32),
            pltpu.SMEM((2, 2, SRC), jnp.int32),
            pltpu.VMEM((CTX, 2 * H, 2 * M), BF16),
            pltpu.VMEM((CTX, 2, 2 * M), F32),
            pltpu.VMEM((2, T, 2 * Q, 2 * M), F32),
            pltpu.VMEM((2, T - 1, 2 * Q, 2 * M), F32),
            pltpu.VMEM((T, 2 * Q, 2 * M), F32),
            pltpu.VMEM((K, M, 2 * M), F32),
            pltpu.VMEM((K, M, 2 * M), F32),
            pltpu.VMEM((K * R, 2 * M), BF16),
            pltpu.VMEM((K * R, 2 * N), BF16),
            pltpu.VMEM((PAIRS, Q, 2 * M), F32),
            dma((11,)),
            dma((3, T - 1)),
            dma((3, T - 1)),
            dma((2, SIDE)),
            dma((2, SIDE)),
            dma((2, SIDE, SIDE)),
            dma((2, SIDE, SIDE)),
            dma((2, SIDE)),
            dma((2, SIDE)),
            dma((3, SIDE)),
            dma((3, SIDE)),
            dma((2, 3, SIDE)),
            dma((2, 3, SIDE)),
        ],
        compiler_params=pltpu.CompilerParams(
            collective_id=0, has_side_effects=True, vmem_limit_bytes=40 << 20
        ),
        name="main",
    )(
        *map(stay, (masks, blur_rows, blur_cols, pupils, targets)),
        stay(context_masters),
        stay(jnp.transpose(offsets, (0, 2, 1))),
        *map(stay, map(jnp.asarray, tables())),
    )
    gq, resist = pl.pallas_call(
        pair_kernel,
        out_shape=(
            jax.ShapeDtypeStruct((2 * Q, 2 * M), BF16),
            jax.ShapeDtypeStruct((2, R, N), BF16),
        ),
        in_specs=[vmem] * 5,
        out_specs=(vmem, hbm),
        scratch_shapes=[
            pltpu.SMEM((16, 128), jnp.int32),
            pltpu.SMEM((CTX, 1, 128), jnp.int32),
            pltpu.VMEM((2, Q, 2 * M), F32),
            dma,
            dma,
        ],
        compiler_params=pltpu.CompilerParams(vmem_limit_bytes=32 << 20),
        name="pairs",
    )(lists, ids_all, g2, e2, resist_v)
    rows = pl.pallas_call(
        rows_kernel,
        out_shape=jax.ShapeDtypeStruct((T, 2 * Q, 2 * M), BF16),
        in_specs=[vmem],
        out_specs=vmem,
        scratch_shapes=[dma((T - 1,)), dma((T - 1,))],
        compiler_params=pltpu.CompilerParams(
            collective_id=1, has_side_effects=True, vmem_limit_bytes=32 << 20
        ),
        name="rows",
    )(gq)
    mask_grad = pl.pallas_call(
        last_kernel,
        out_shape=jax.ShapeDtypeStruct((2, R, N), F32),
        in_specs=[vmem] * 3,
        out_specs=hbm,
        scratch_shapes=[pltpu.VMEM((2, R, N), F32), dma((2,))],
        compiler_params=pltpu.CompilerParams(vmem_limit_bytes=32 << 20),
        name="last",
    )(rows, p_st, q_st)
    return (resist, mask_grad)


def solution(mesh):
    placed = (
        P("ctx", "tile", None),
        P(),
        P(),
        P(),
        P("ctx", "tile", None),
        P("ctx", None),
        P("ctx", None, None),
    )
    return jax.shard_map(
        local,
        mesh=mesh,
        in_specs=placed,
        out_specs=(P("ctx", "tile", None), P("ctx", "tile", None)),
        check_vma=False,
    )
```

```python
import functools
import math

import jax
import jax.numpy as jnp
import ml_dtypes
import numpy as np
from jax import lax
from jax.experimental import pallas as pl
from jax.experimental.pallas import tpu as pltpu
from jax.sharding import PartitionSpec as P

STEEPNESS = 4.0
THRESHOLD = 1.0
N = 512
M = 64
K = 6
T = 4
R = N // T
H = M // (2 * T)
Q = 16
SIDE = 8
CTX = 2 * SIDE * SIDE
SRC = 12
PAIRS = 2 * SRC
MESH = pl.DeviceIdType.MESH
F32 = jnp.float32
BF16 = jnp.bfloat16
NEAR_FIRST = (1, 7, 2, 6, 3, 5, 4)


def tables():
    freq = (np.arange(M) - M // 2) % N
    angle = (freq[:, None] * np.arange(N)[None, :] % N) * (2.0 * math.pi / N)
    cos = np.cos(angle) / math.sqrt(N)
    sin = np.sin(angle) / math.sqrt(N)
    fst = np.concatenate([cos, -sin], 0)
    gcat = np.concatenate([cos.T, sin.T], 1)
    inv = np.concatenate([np.concatenate([cos, sin], 1), np.concatenate([-sin, cos], 1)], 0)
    adj = np.concatenate([np.concatenate([cos.T, -sin.T], 1), np.concatenate([sin.T, cos.T], 1)], 0)
    adj = np.concatenate([adj, -adj[:, M:], adj[:, :M]], 1)
    order = np.arange(2 * N).reshape(2, T, N // T).transpose(1, 0, 2).reshape(-1)
    return [t.astype(ml_dtypes.bfloat16) for t in (fst, gcat, inv[:, order], adj[order])]


def sine_coefficients():
    w = 0.25 * np.cos(np.pi * (np.arange(400) + 0.5) / 400)
    powers = np.stack([w ** (2 * i + 1) for i in range(6)], 1)
    return [float(c) for c in np.linalg.lstsq(powers, np.sin(2 * np.pi * w), rcond=None)[0]]


SINE = sine_coefficients()


def swap(a):
    return pltpu.roll(a, M, 1)


def left_half(shape):
    return lax.broadcasted_iota(jnp.int32, shape, 1) < M


def grid(shape):
    return lax.broadcasted_iota(jnp.int32, shape, 0), lax.broadcasted_iota(jnp.int32, shape, 1)


def turn_rates(tile):
    row, lane = grid((Q, 2 * M))
    v = lane % M
    plain = row < H
    early = v <= M // 2
    f_u = jnp.where(plain, row + (tile * H - M // 2), jnp.where(early, 0, v - M // 2))
    f_v = jnp.where(plain | early, v - M // 2, -(M // 2))
    late = jnp.where(lane < M, 0.0, 0.25).astype(F32)
    return f_u.astype(F32) * (1.0 / N), f_v.astype(F32) * (1.0 / N), late


def from_rows(a):
    row, lane = grid(a.shape)
    real = jnp.where((lane == row + M // 2) & (row > 0), jnp.broadcast_to(a[:, 0:1], a.shape), 0.0)
    imag = jnp.where((lane == row + M + M // 2) & (row > 0), jnp.broadcast_to(a[:, M : M + 1], a.shape), 0.0)
    return jnp.sum(real + imag, axis=0, keepdims=True)


def to_rows(e):
    shape = (M // 2, 2 * M)
    row, lane = grid(shape)
    wide = jnp.broadcast_to(e, shape)
    real = jnp.sum(jnp.where((lane == row + M // 2) & (row > 0), wide, 0.0), axis=1, keepdims=True)
    imag = jnp.sum(jnp.where((lane == row + M + M // 2) & (row > 0), wide, 0.0), axis=1, keepdims=True)
    first = jnp.where((row == 0) & (lane % M <= M // 2), wide, 0.0)
    return first + jnp.where(lane == 0, real, 0.0) + jnp.where(lane == M, imag, 0.0)


def exact(a, b):
    return lax.dot_general(
        a, b, (((1,), (0,)), ((), ())), precision=lax.Precision.HIGHEST, preferred_element_type=F32
    )


def mirrored(a):
    src, dst = grid((2 * M, 2 * M))
    both = jnp.where((src + dst == M) & (src < M) & (dst < M), 1.0, 0.0) - jnp.where((src + dst == 3 * M) & (src >= M), 1.0, 0.0)
    return exact(a, both)


def flipped(a):
    row, col = grid((M // 2, M // 2))
    return exact(jnp.where(row + col == M // 2, 1.0, 0.0), a)


def expand(half, e):
    row, lane = grid((M // 2, 2 * M))
    e_mirrored = mirrored(jnp.broadcast_to(e, (8, 2 * M)))[0:1]
    first = jnp.where((row == 0) & (lane % M > M // 2), jnp.broadcast_to(e_mirrored, row.shape), 0.0)
    return jnp.concatenate([half, flipped(mirrored(half)) + first + to_rows(e)], 0)


def fold(grad):
    low = grad[M // 2 :]
    turned = mirrored(low)
    v = lax.broadcasted_iota(jnp.int32, (1, 2 * M), 1) % M
    e = jnp.where(v <= M // 2, low[0:1], 0.0) + jnp.where((v > 0) & (v < M // 2), turned[0:1], 0.0)
    return grad[: M // 2] + flipped(turned), e + from_rows(low)


def half_of(spectrum):
    low = spectrum[M // 2 :]
    v = lax.broadcasted_iota(jnp.int32, (1, 2 * M), 1) % M
    return spectrum[: M // 2], jnp.where(v <= M // 2, low[0:1], 0.0) + from_rows(low)


def padded(e):
    return jnp.where(lax.broadcasted_iota(jnp.int32, (Q - H, 2 * M), 0) == 0, jnp.broadcast_to(e, (Q - H, 2 * M)), 0.0)


def pick(block, es, second):
    return jnp.concatenate(
        [jnp.where(second, block[H:], block[:H]), padded(jnp.where(second, es[1:2], es[0:1]))], 0
    )


def cos_sin(rates, r, s):
    y = rates[0] * r + rates[1] * s - rates[2]
    y = y - jnp.floor(y + 0.5)
    w = 0.25 - jnp.abs(y)
    z = w * w
    total = jnp.full_like(z, SINE[-1])
    for c in SINE[-2::-1]:
        total = total * z + c
    return total * w


def dot(a, b, dims=((1,), (0,))):
    return lax.dot_general(a, b, (dims, ((), ())), preferred_element_type=F32)


def wait_all(copies):
    for c in copies:
        c.wait()


def near_first(i):
    return (i % 2) * ((i + 1) // 2) + (1 - i % 2) * (SIDE - i // 2)


def pair_list(ids, me):
    row, lane = grid((CTX, 128))
    row8, lane8 = grid((8, 128))
    ones = jnp.full((8, 128), 1.0, BF16)
    before = jnp.where(row < lane, 1.0, 0.0).astype(BF16)
    r = pltpu.roll(ids, 128 - 32, 1)
    s = pltpu.roll(ids, 128 - 64, 1)
    match = jnp.where((ids >> 1 == me) & (lane < PAIRS), 1.0, 0.0)
    values = [jnp.where(lane >= SRC, 1.0, 0.0)] + [v.astype(F32) for v in (r >> 4, r & 15, s >> 4, s & 15, ids & 1)]
    count = dot(ones, match.astype(BF16), ((1,), (1,)))
    found = [dot(ones, (match * v).astype(BF16), ((1,), (1,))) for v in values]
    single = jnp.where(count == 1.0, 1.0, 0.0)
    rank = dot(single.astype(BF16), before)
    hot = jnp.where(
        (jnp.broadcast_to(rank[0:1], (CTX, 128)) == row.astype(F32))
        & (jnp.broadcast_to(single[0:1], (CTX, 128)) > 0.5),
        1.0, 0.0,
    ).astype(BF16)
    load = jnp.where(row8 == 6, single, 0.0)
    load = jnp.where(row8 == 0, single * (2.0 * lane8.astype(F32) + found[0]), load)
    for i in range(1, 6):
        load = jnp.where(row8 == i, single * found[i], load)
    listed = dot(load.astype(BF16), hot, ((1,), (1,)))
    at = [jnp.broadcast_to(listed[i : i + 1], (8, 128)) for i in range(7)]
    several = jnp.where(count > 1.5, 1.0, 0.0)
    out = [at[0], 16.0 * at[1] + at[2], 16.0 * at[3] + at[4], at[6] - at[5], at[5]]
    out += [jnp.broadcast_to(jnp.sum(several, axis=1, keepdims=True), (8, 128)), several]
    rows = jnp.zeros((8, 128), F32)
    for i, value in enumerate(out):
        rows = jnp.where(row8 == i, value, rows)
    return rows.astype(jnp.int32)


def main_kernel(
    masks_h, br_h, bc_h, pupils_h, targets_h, ids_h, shifts_h, fst_h, gcat_h, inv_h, adj_h,
    resist, g2, e2, ids_all, listed, p_out, q_out,
    masks, br, bc, pupils, targets, fst, gown_v, inv, adj,
    ids_s, shifts_s, g1, e1, part, part_in, spec, prr, pii, u_all, pull, phases,
    load_sem, x_send, x_recv, g_send, a_recv, f_recv, s_send, s_recv, i_send, i_recv, e_send, e_recv,
):
    tile = lax.axis_index("tile")
    q = lax.axis_index("ctx")
    core, y, z = q % 2, (q // 2) % SIDE, q // (2 * SIDE)
    major = z + core * (y - z)
    minor = y + core * (z - y)
    half = core * (SIDE * SIDE)
    slot = half + major * SIDE + minor
    own = pl.ds(pl.multiple_of(tile * R, R), R)

    loads = [
        pltpu.make_async_copy(src, dst, load_sem.at[i])
        for i, (src, dst) in enumerate(
            [
                (fst_h, fst),
                (br_h.at[:, own], br),
                (bc_h, bc),
                (masks_h, masks),
                (pupils_h, pupils),
                (gcat_h.at[own, :], gown_v),
                (inv_h, inv),
                (targets_h, targets),
                (adj_h, adj),
                (ids_h, ids_s),
                (shifts_h, shifts_s),
            ]
        )
    ]
    for copy in loads:
        copy.start()

    def ctx_id(mj, mn):
        zz = mj + core * (mn - mj)
        yy = mn + core * (mj - mn)
        return zz * (2 * SIDE) + yy * 2 + core

    sibling = q + 1 - 2 * core
    barrier = pltpu.get_barrier_semaphore()
    for k in range(1, SIDE):
        pl.semaphore_signal(barrier, inc=1, device_id={"ctx": ctx_id(major, (minor + k) % SIDE)}, device_id_type=MESH)
        pl.semaphore_signal(barrier, inc=1, device_id={"ctx": ctx_id((major + k) % SIDE, minor)}, device_id_type=MESH)
    for k in range(1, T):
        pl.semaphore_signal(barrier, inc=1, device_id={"tile": (tile + k) % T}, device_id_type=MESH)
    pl.semaphore_signal(barrier, inc=1, device_id={"ctx": sibling}, device_id_type=MESH)

    def put(step, i, half_rows, e):
        for t in range(T):
            part[step, t, i * Q : i * Q + H] = half_rows[t * H : (t + 1) * H]
            part[step, t, i * Q + H : (i + 1) * Q] = padded(e) if t == 0 else jnp.zeros((Q - H, 2 * M), F32)

    loads[0].wait()
    loads[1].wait()
    table = fst[...]
    p_st = dot(table, br[...]).astype(BF16)
    loads[2].wait()
    q_st = dot(table, bc[...]).astype(BF16)
    p_out[...] = p_st
    q_out[...] = q_st
    qq = jnp.concatenate([q_st, -q_st[M:], q_st[:M]], 0)
    pcat = jnp.concatenate([p_st[:M], p_st[M:]], 1)
    loads[3].wait()
    for m in range(2):
        a = dot(masks[m], qq, ((1,), (1,))).astype(BF16)
        s = dot(pcat, jnp.concatenate([a[:, : 2 * M], a[:, 2 * M :]], 0))
        put(0, m, *half_of(s))

    pl.semaphore_wait(barrier, T - 1 + 2 * (SIDE - 1) + 1)

    def tile_scatter(step):
        copies = []
        for k in range(1, T):
            to = (tile + k) % T
            copies.append(
                pltpu.make_async_remote_copy(
                    src_ref=part.at[step, to], dst_ref=part_in.at[step, k - 1],
                    send_sem=x_send.at[2 * step, k - 1], recv_sem=x_recv.at[2 * step, k - 1],
                    device_id={"tile": to}, device_id_type=MESH,
                )
            )
        for c in copies:
            c.start()
        return copies

    def tile_sum(step):
        return (part[step, tile] + part_in[step, 0]) + (part_in[step, 1] + part_in[step, 2])

    def to_ctx(ref, place, send_sem, recv_sem, to):
        return pltpu.make_async_remote_copy(
            src_ref=ref.at[place], dst_ref=ref.at[place], send_sem=send_sem, recv_sem=recv_sem,
            device_id={"ctx": to}, device_id_type=MESH,
        )

    minor_ids = {k: ctx_id(major, (minor + k) % SIDE) for k in NEAR_FIRST}
    major_ids = {k: ctx_id((major + k) % SIDE, minor) for k in NEAR_FIRST}
    first = half + major * SIDE

    def gather(buf, step, between, late, end):
        def along_minor(k, to):
            return to_ctx(buf, pl.ds(slot, 1), g_send.at[step], a_recv.at[step, k], to)

        def along_major(came, k):
            place = pl.ds(first + (minor + SIDE - came) % SIDE, 1)
            return to_ctx(buf, place, g_send.at[step], f_recv.at[step, k], major_ids[k])

        def to_sibling(row):
            return to_ctx(buf, pl.ds(half + row * SIDE, SIDE), s_send.at[step], s_recv.at[step], sibling)

        def bytes_of(blocks, send_sem, recv_sem):
            return to_ctx(buf, pl.ds(0, blocks), send_sem, recv_sem, sibling)

        for k in NEAR_FIRST:
            along_minor(k, minor_ids[k]).start()
        for k in NEAR_FIRST:
            along_major(0, k).start()
        between()

        def forward(i, _):
            came = near_first(i)
            along_minor(came, sibling).wait_recv()
            for k in NEAR_FIRST:
                along_major(came, k).start()
            return 0

        lax.fori_loop(1, SIDE, forward, 0)
        to_sibling(major).start()
        late()

        def arrive(i, _):
            k = near_first(i)
            bytes_of(SIDE, g_send.at[step], f_recv.at[step, k]).wait_recv()
            to_sibling((major + SIDE - k) % SIDE).start()
            return 0

        lax.fori_loop(1, SIDE, arrive, 0)
        end()
        bytes_of((SIDE - 1) * (SIDE + 1), g_send.at[step], f_recv.at[step, 0]).wait_send()
        bytes_of(SIDE * SIDE, s_send.at[step], s_recv.at[step]).wait()

    def line(buf, send, recv, phase):
        if phase == 2:
            places = [(pl.ds(half, SIDE * SIDE), sibling)]
        elif phase == 1:
            places = [(pl.ds(first, SIDE), major_ids[k]) for k in NEAR_FIRST]
        else:
            places = [(pl.ds(slot, 1), minor_ids[k]) for k in NEAR_FIRST]
        for place, to in places:
            to_ctx(buf, place, send.at[phase], recv.at[phase], to).start()
        blocks = (SIDE - 1, (SIDE - 1) * SIDE, SIDE * SIDE)[phase]
        return [to_ctx(buf, pl.ds(0, blocks), send.at[phase], recv.at[phase], sibling)]

    def spread_out(step, buf, es):
        total = tile_sum(step)
        buf[pl.ds(slot, 1)] = jnp.concatenate([total[:H], total[Q : Q + H]], 0).astype(BF16).reshape(1, 2 * H, 2 * M)
        es[pl.ds(slot, 1)] = jnp.concatenate([total[H : H + 1], total[Q + H : Q + H + 1]], 0).reshape(1, 2, 2 * M)
        e_sems = (e_send.at[step], e_recv.at[step])
        pending = []

        def between():
            pending.append(line(es, *e_sems, 0))
            if step == 0:
                wait_all(ids_copies.pop())
                ids_copies.append(line(ids_all, i_send, i_recv, 1))
            else:
                listed[...] = pair_list(ids_all[...].reshape(CTX, 128), q)

        def late():
            wait_all(pending.pop())
            pending.append(line(es, *e_sems, 1))
            if step == 0:
                wait_all(ids_copies.pop())
                ids_copies.append(line(ids_all, i_send, i_recv, 2))

        def end():
            wait_all(pending.pop())
            pending.append(line(es, *e_sems, 2))

        gather(buf, step, between, late, end)
        wait_all(pending.pop())

    copies = tile_scatter(0)
    loads[9].wait()
    loads[10].wait()
    lane = lax.broadcasted_iota(jnp.int32, (1, 128), 1)
    own_ids = jnp.zeros((1, 128), jnp.int32)
    for c in range(2):
        for j in range(SRC):
            for place, value in ((0, ids_s[c, j]), (32, shifts_s[c, 0, j]), (64, shifts_s[c, 1, j])):
                own_ids = jnp.where(lane == place + c * SRC + j, value, own_ids)
    ids_all[pl.ds(slot, 1)] = own_ids.reshape(1, 1, 128)
    ids_copies = [line(ids_all, i_send, i_recv, 0)]

    rates = turn_rates(tile)
    for p in range(PAIRS):
        c, j = p // SRC, p % SRC
        phases[p] = cos_sin(rates, shifts_s[c, 0, j].astype(F32), shifts_s[c, 1, j].astype(F32))
    left64 = left_half((M, 2 * M))
    loads[4].wait()
    for k in range(K):
        pk = pupils[k]
        turned = swap(pk)
        prr[k] = jnp.where(left64, pk, turned)
        pii[k] = jnp.where(left64, -turned, pk)

    wait_all(copies)
    spread_out(0, g1, e1)
    wait_all(ids_copies.pop())

    leftq = left_half((Q, 2 * M))
    for c in range(2):
        sum_a = jnp.zeros((Q, 2 * M), F32)
        sum_b = jnp.zeros((Q, 2 * M), F32)
        for j in range(SRC):
            p = c * SRC + j
            master = ids_s[c, j]
            owner = master >> 1
            ocore = owner & 1
            oy = (owner >> 1) & (SIDE - 1)
            oz = owner >> 4
            place = ocore * (SIDE * SIDE) + oz * SIDE + oy + ocore * (SIDE - 1) * (oy - oz)
            g = pick(g1[place].astype(F32), e1[place], (master & 1) > 0)
            cs = phases[p]
            sum_a += g * cs
            sum_b += swap(g) * cs
        spec[tile, c * Q : (c + 1) * Q] = jnp.where(leftq, sum_a + swap(sum_a), swap(sum_b) - sum_b)
    copies = []
    for k in range(1, T):
        copies.append(
            pltpu.make_async_remote_copy(
                src_ref=spec.at[tile], dst_ref=spec.at[tile],
                send_sem=x_send.at[1, k - 1], recv_sem=x_recv.at[1, k - 1],
                device_id={"tile": (tile + k) % T}, device_id_type=MESH,
            )
        )
    for c in copies:
        c.start()
    for copy in loads[5:9]:
        copy.wait()
    fown = fst[:, own]
    fcat = jnp.concatenate([fown[:M], fown[M:]], 1)
    gown = gown_v[...]
    wait_all(copies)

    for c in range(2):
        s = expand(
            jnp.concatenate([spec[t, c * Q : c * Q + H] for t in range(T)], 0), spec[0, c * Q + H : c * Q + H + 1]
        )
        s_sw = swap(s)
        s2 = jnp.where(left64, -s_sw, s_sw)
        s2_sw = jnp.where(left64, s, -s)
        for k in range(K):
            a1 = prr[k] * s + pii[k] * s_sw
            a2 = prr[k] * s2 + pii[k] * s2_sw
            both = jnp.concatenate([a1, a2], 0).astype(BF16)
            u_all[k * R : (k + 1) * R] = dot(gown, both).astype(BF16)
        for b in range(T):
            cols = slice(b * R, (b + 1) * R)
            field = dot(u_all[...], inv[:, b * 2 * R : (b + 1) * 2 * R])
            intensity = jnp.zeros((R, R), F32)
            for k in range(K):
                fr = field[k * R : (k + 1) * R, :R]
                fi = field[k * R : (k + 1) * R, R:]
                intensity += fr * fr + fi * fi
            image = 1.0 / (1.0 + jnp.exp(-STEEPNESS * (intensity - THRESHOLD)))
            resist[c, :, cols] = image.astype(BF16)
            slope = (image - targets[c, :, cols].astype(F32)) * (2.0 * STEEPNESS) * image * (1.0 - image)
            slope2 = jnp.concatenate([slope, slope], 1)
            for k in range(K):
                pull[k * R : (k + 1) * R, b * 2 * R : (b + 1) * 2 * R] = (
                    slope2 * field[k * R : (k + 1) * R]
                ).astype(BF16)
        folded = dot(pull[...], adj[...]).astype(BF16)
        g_a = jnp.zeros((M, 2 * M), F32)
        g_b = jnp.zeros((M, 2 * M), F32)
        for k in range(K):
            fk = folded[k * R : (k + 1) * R]
            ga = dot(fcat, jnp.concatenate([fk[:, : 2 * M], fk[:, 2 * M :]], 0))
            g_a += prr[k] * ga
            g_b += pii[k] * ga
        grad = g_a + swap(g_b)
        put(1, c, *fold(grad))

    wait_all(tile_scatter(1))
    spread_out(1, g2, e2)


def pair_terms(g2, e2, rates, context, r, s):
    host = context // 2
    g = pick(g2[host].astype(F32), e2[host], context % 2 > 0)
    cs = cos_sin(rates, r.astype(F32), s.astype(F32))
    return g * cs, swap(g) * cs


def several_kernel(list_v, ids_v, g2, e2, sums, list_s, ids_s, sems):
    me = lax.axis_index("ctx")
    rates = turn_rates(lax.axis_index("tile"))
    sums[...] = jnp.zeros_like(sums)

    @pl.when(jnp.max(list_v[5:6, :]) > 0)
    def _():
        copies = [
            pltpu.make_async_copy(list_v, list_s, sems.at[0]),
            pltpu.make_async_copy(ids_v, ids_s, sems.at[1]),
        ]
        for copy in copies:
            copy.start()
        wait_all(copies)

        def host(h, _):
            @pl.when(list_s[6, h] > 0)
            def _():
                def one(j, _):
                    master = ids_s[h, 0, j]

                    @pl.when(master >> 1 == me)
                    def _():
                        m = master & 1
                        a, b = pair_terms(g2, e2, rates, 2 * h + j // SRC, ids_s[h, 0, 32 + j], ids_s[h, 0, 64 + j])
                        sums[2 * m] += a
                        sums[2 * m + 1] += b

                    return 0

                lax.fori_loop(0, PAIRS, one, 0)

            return 0

        lax.fori_loop(0, CTX, host, 0)


def rows_kernel(list_v, g2, e2, sums, rows, list_s, sem, x_send, x_recv):
    tile = lax.axis_index("tile")
    copy = pltpu.make_async_copy(list_v, list_s, sem)
    copy.start()
    barrier = pltpu.get_barrier_semaphore()
    for k in range(1, T):
        pl.semaphore_signal(barrier, inc=1, device_id={"tile": (tile + k) % T}, device_id_type=MESH)
    rates = turn_rates(tile)
    left = left_half((Q, 2 * M))
    copy.wait()
    block = 8

    def step(i, carry):
        total = list(carry)
        for b in range(block):
            k = i * block + b
            a, b = pair_terms(g2, e2, rates, list_s[0, k], list_s[1, k], list_s[2, k])
            for m in range(2):
                weight = list_s[3 + m, k].astype(F32)
                total[2 * m] += a * weight
                total[2 * m + 1] += b * weight
        return tuple(total)

    total = lax.fori_loop(0, CTX // block, step, tuple(sums[i] for i in range(4)))
    for m in range(2):
        a, b = total[2 * m : 2 * m + 2]
        rows[tile, m * Q : (m + 1) * Q] = jnp.where(left, a - swap(a), b + swap(b)).astype(BF16)
    pl.semaphore_wait(barrier, T - 1)
    copies = []
    for k in range(1, T):
        copies.append(
            pltpu.make_async_remote_copy(
                src_ref=rows.at[tile], dst_ref=rows.at[tile],
                send_sem=x_send.at[k - 1], recv_sem=x_recv.at[k - 1],
                device_id={"tile": (tile + k) % T}, device_id_type=MESH,
            )
        )
    for c in copies:
        c.start()
    wait_all(copies)


def last_kernel(rows, p_st, q_st, resist_v, out, resist, held, sem):
    left = left_half((M, 2 * M))
    copies = [pltpu.make_async_copy(resist_v, resist, sem.at[2])]
    copies[0].start()
    for m in range(2):
        parts = [rows[t].astype(F32)[m * Q : (m + 1) * Q] for t in range(T)]
        g = jnp.concatenate([part[:H] for part in parts] + [to_rows(parts[0][H : H + 1])], 0)
        turned = swap(g)
        both = jnp.concatenate([g, jnp.where(left, turned, -turned)], 0).astype(BF16)
        lifted = dot(p_st[...], both, ((0,), (0,))).astype(BF16)
        held[m] = dot(lifted, q_st[...])
        copies.append(pltpu.make_async_copy(held.at[m], out.at[m], sem.at[m]))
        copies[-1].start()
    wait_all(copies)


def local(masks, blur_rows, blur_cols, pupils, targets, context_masters, offsets):
    vmem = pl.BlockSpec(memory_space=pltpu.VMEM)
    hbm = pl.BlockSpec(memory_space=pltpu.HBM)
    dma = pltpu.SemaphoreType.DMA
    stay = functools.partial(pltpu.with_memory_space_constraint, memory_space=pltpu.HBM)
    resist_v, g2, e2, ids_all, listed, p_st, q_st = pl.pallas_call(
        main_kernel,
        out_shape=(
            jax.ShapeDtypeStruct((2, R, N), BF16),
            jax.ShapeDtypeStruct((CTX, 2 * H, 2 * M), BF16),
            jax.ShapeDtypeStruct((CTX, 2, 2 * M), F32),
            jax.ShapeDtypeStruct((CTX, 1, 128), jnp.int32),
            jax.ShapeDtypeStruct((8, 128), jnp.int32),
            jax.ShapeDtypeStruct((2 * M, R), BF16),
            jax.ShapeDtypeStruct((2 * M, N), BF16),
        ),
        in_specs=[hbm] * 11,
        out_specs=(vmem,) * 7,
        scratch_shapes=[
            pltpu.VMEM((2, R, N), BF16),
            pltpu.VMEM((N, R), BF16),
            pltpu.VMEM((N, N), BF16),
            pltpu.VMEM((K, M, 2 * M), F32),
            pltpu.VMEM((2, R, N), BF16),
            pltpu.VMEM((2 * M, N), BF16),
            pltpu.VMEM((R, 2 * M), BF16),
            pltpu.VMEM((2 * M, 2 * N), BF16),
            pltpu.VMEM((2 * N, 4 * M), BF16),
            pltpu.SMEM((2, SRC), jnp.int32),
            pltpu.SMEM((2, 2, SRC), jnp.int32),
            pltpu.VMEM((CTX, 2 * H, 2 * M), BF16),
            pltpu.VMEM((CTX, 2, 2 * M), F32),
            pltpu.VMEM((2, T, 2 * Q, 2 * M), F32),
            pltpu.VMEM((2, T - 1, 2 * Q, 2 * M), F32),
            pltpu.VMEM((T, 2 * Q, 2 * M), F32),
            pltpu.VMEM((K, M, 2 * M), F32),
            pltpu.VMEM((K, M, 2 * M), F32),
            pltpu.VMEM((K * R, 2 * M), BF16),
            pltpu.VMEM((K * R, 2 * N), BF16),
            pltpu.VMEM((PAIRS, Q, 2 * M), F32),
            dma((11,)),
            dma((3, T - 1)),
            dma((3, T - 1)),
            dma((2,)),
            dma((2, SIDE)),
            dma((2, SIDE)),
            dma((2,)),
            dma((2,)),
            dma((3,)),
            dma((3,)),
            dma((2, 3)),
            dma((2, 3)),
        ],
        compiler_params=pltpu.CompilerParams(
            collective_id=0, has_side_effects=True, vmem_limit_bytes=40 << 20
        ),
        name="main",
    )(
        *map(stay, (masks, blur_rows, blur_cols, pupils, targets)),
        stay(context_masters),
        stay(jnp.transpose(offsets, (0, 2, 1))),
        *map(stay, map(jnp.asarray, tables())),
    )
    sums = pl.pallas_call(
        several_kernel,
        out_shape=jax.ShapeDtypeStruct((4, Q, 2 * M), F32),
        in_specs=[vmem] * 4,
        out_specs=vmem,
        scratch_shapes=[
            pltpu.SMEM((8, 128), jnp.int32),
            pltpu.SMEM((CTX, 1, 128), jnp.int32),
            dma((2,)),
        ],
        compiler_params=pltpu.CompilerParams(vmem_limit_bytes=32 << 20),
        name="several",
    )(listed, ids_all, g2, e2)
    rows = pl.pallas_call(
        rows_kernel,
        out_shape=jax.ShapeDtypeStruct((T, 2 * Q, 2 * M), BF16),
        in_specs=[vmem] * 4,
        out_specs=vmem,
        scratch_shapes=[pltpu.SMEM((8, 128), jnp.int32), dma, dma((T - 1,)), dma((T - 1,))],
        compiler_params=pltpu.CompilerParams(
            collective_id=1, has_side_effects=True, vmem_limit_bytes=32 << 20
        ),
        name="rows",
    )(listed, g2, e2, sums)
    mask_grad, resist = pl.pallas_call(
        last_kernel,
        out_shape=(
            jax.ShapeDtypeStruct((2, R, N), F32),
            jax.ShapeDtypeStruct((2, R, N), BF16),
        ),
        in_specs=[vmem] * 4,
        out_specs=(hbm, hbm),
        scratch_shapes=[pltpu.VMEM((2, R, N), F32), dma((3,))],
        compiler_params=pltpu.CompilerParams(vmem_limit_bytes=32 << 20),
        name="last",
    )(rows, p_st, q_st, resist_v)
    return (resist, mask_grad)


def solution(mesh):
    placed = (
        P("ctx", "tile", None),
        P(),
        P(),
        P(),
        P("ctx", "tile", None),
        P("ctx", None),
        P("ctx", None, None),
    )
    return jax.shard_map(
        local,
        mesh=mesh,
        in_specs=placed,
        out_specs=(P("ctx", "tile", None), P("ctx", "tile", None)),
        check_vma=False,
    )
```

```python
import functools
import math

import jax
import jax.numpy as jnp
import ml_dtypes
import numpy as np
from jax import lax
from jax.experimental import pallas as pl
from jax.experimental.pallas import tpu as pltpu
from jax.sharding import PartitionSpec as P

STEEPNESS = 4.0
THRESHOLD = 1.0
N = 512
M = 64
K = 6
T = 4
R = N // T
H = M // (2 * T)
Q = 16
SIDE = 8
CTX = 2 * SIDE * SIDE
SRC = 12
PAIRS = 2 * SRC
MESH = pl.DeviceIdType.MESH
F32 = jnp.float32
BF16 = jnp.bfloat16
NEAR_FIRST = (1, 7, 2, 6, 3, 5, 4)


def tables():
    freq = (np.arange(M) - M // 2) % N
    angle = (freq[:, None] * np.arange(N)[None, :] % N) * (2.0 * math.pi / N)
    cos = np.cos(angle) / math.sqrt(N)
    sin = np.sin(angle) / math.sqrt(N)
    fst = np.concatenate([cos, -sin], 0)
    gcat = np.concatenate([cos.T, sin.T], 1)
    inv = np.concatenate([np.concatenate([cos, sin], 1), np.concatenate([-sin, cos], 1)], 0)
    adj = np.concatenate([np.concatenate([cos.T, -sin.T], 1), np.concatenate([sin.T, cos.T], 1)], 0)
    adj = np.concatenate([adj, -adj[:, M:], adj[:, :M]], 1)
    order = np.arange(2 * N).reshape(2, T, N // T).transpose(1, 0, 2).reshape(-1)
    return [t.astype(ml_dtypes.bfloat16) for t in (fst, gcat, inv[:, order], adj[order])]


def sine_coefficients():
    w = 0.25 * np.cos(np.pi * (np.arange(400) + 0.5) / 400)
    powers = np.stack([w ** (2 * i + 1) for i in range(6)], 1)
    return [float(c) for c in np.linalg.lstsq(powers, np.sin(2 * np.pi * w), rcond=None)[0]]


SINE = sine_coefficients()


def swap(a):
    return pltpu.roll(a, M, 1)


def left_half(shape):
    return lax.broadcasted_iota(jnp.int32, shape, 1) < M


def grid(shape):
    return lax.broadcasted_iota(jnp.int32, shape, 0), lax.broadcasted_iota(jnp.int32, shape, 1)


def turn_rates(tile):
    row, lane = grid((Q, 2 * M))
    v = lane % M
    plain = row < H
    early = v <= M // 2
    f_u = jnp.where(plain, row + (tile * H - M // 2), jnp.where(early, 0, v - M // 2))
    f_v = jnp.where(plain | early, v - M // 2, -(M // 2))
    late = jnp.where(lane < M, 0.0, 0.25).astype(F32)
    return f_u.astype(F32) * (1.0 / N), f_v.astype(F32) * (1.0 / N), late


def from_rows(a):
    row, lane = grid(a.shape)
    real = jnp.where((lane == row + M // 2) & (row > 0), jnp.broadcast_to(a[:, 0:1], a.shape), 0.0)
    imag = jnp.where((lane == row + M + M // 2) & (row > 0), jnp.broadcast_to(a[:, M : M + 1], a.shape), 0.0)
    return jnp.sum(real + imag, axis=0, keepdims=True)


def to_rows(e):
    shape = (M // 2, 2 * M)
    row, lane = grid(shape)
    wide = jnp.broadcast_to(e, shape)
    real = jnp.sum(jnp.where((lane == row + M // 2) & (row > 0), wide, 0.0), axis=1, keepdims=True)
    imag = jnp.sum(jnp.where((lane == row + M + M // 2) & (row > 0), wide, 0.0), axis=1, keepdims=True)
    first = jnp.where((row == 0) & (lane % M <= M // 2), wide, 0.0)
    return first + jnp.where(lane == 0, real, 0.0) + jnp.where(lane == M, imag, 0.0)


def split(a):
    high = a.astype(BF16)
    return high, (a - high.astype(F32)).astype(BF16)


def mirrored(a):
    src, dst = grid((2 * M, 2 * M))
    real = jnp.where((src + dst == M) & (src < M) & (dst < M), 1.0, 0.0)
    both = real - jnp.where((src + dst == 3 * M) & (src >= M), 1.0, 0.0)
    out = dot(jnp.concatenate(split(a), 0), both.astype(BF16))
    return out[: a.shape[0]] + out[a.shape[0] :]


def flipped(blocks):
    row, col = grid((M // 2, M // 2))
    turn = jnp.where(row + col == M // 2, 1.0, 0.0).astype(BF16)
    out = dot(turn, jnp.concatenate([part for a in blocks for part in split(a)], 1))
    part = [out[:, i * 2 * M : (i + 1) * 2 * M] for i in range(2 * len(blocks))]
    return [part[2 * i] + part[2 * i + 1] for i in range(len(blocks))]


def expand(halves, es):
    row, lane = grid((M // 2, 2 * M))
    wide = [jnp.broadcast_to(e, (16, 2 * M)) for e in es]
    turned = mirrored(jnp.concatenate([*halves, *wide], 0))
    lower = flipped([turned[: M // 2], turned[M // 2 : M]])
    out = []
    for i in range(2):
        e_turned = jnp.broadcast_to(turned[M + 16 * i : M + 16 * i + 1], row.shape)
        first = jnp.where((row == 0) & (lane % M > M // 2), e_turned, 0.0)
        out.append(jnp.concatenate([halves[i], lower[i] + first + to_rows(es[i])], 0))
    return out


def fold(grads):
    low = [grad[M // 2 :] for grad in grads]
    turned = mirrored(jnp.concatenate(low, 0))
    upper = flipped([turned[: M // 2], turned[M // 2 :]])
    v = lax.broadcasted_iota(jnp.int32, (1, 2 * M), 1) % M
    out = []
    for i in range(2):
        t = turned[i * (M // 2) : i * (M // 2) + 1]
        e = jnp.where(v <= M // 2, low[i][0:1], 0.0) + jnp.where((v > 0) & (v < M // 2), t, 0.0)
        out.append((grads[i][: M // 2] + upper[i], e + from_rows(low[i])))
    return out


def half_of(spectrum):
    low = spectrum[M // 2 :]
    v = lax.broadcasted_iota(jnp.int32, (1, 2 * M), 1) % M
    return spectrum[: M // 2], jnp.where(v <= M // 2, low[0:1], 0.0) + from_rows(low)


def padded(e):
    return jnp.where(lax.broadcasted_iota(jnp.int32, (Q - H, 2 * M), 0) == 0, jnp.broadcast_to(e, (Q - H, 2 * M)), 0.0)


def pick(block, es, second):
    return jnp.concatenate(
        [jnp.where(second, block[H:], block[:H]), padded(jnp.where(second, es[1:2], es[0:1]))], 0
    )


def cos_sin(rates, r, s):
    y = rates[0] * r + rates[1] * s - rates[2]
    y = y - jnp.floor(y + 0.5)
    w = 0.25 - jnp.abs(y)
    z = w * w
    total = jnp.full_like(z, SINE[-1])
    for c in SINE[-2::-1]:
        total = total * z + c
    return total * w


def dot(a, b, dims=((1,), (0,))):
    return lax.dot_general(a, b, (dims, ((), ())), preferred_element_type=F32)


def wait_all(copies):
    for c in copies:
        c.wait()


def near_first(i):
    return (i % 2) * ((i + 1) // 2) + (1 - i % 2) * (SIDE - i // 2)


def pair_list(ids, me):
    row, lane = grid((CTX, 128))
    row8, lane8 = grid((8, 128))
    ones = jnp.full((8, 128), 1.0, BF16)
    before = jnp.where(row < lane, 1.0, 0.0).astype(BF16)
    r = pltpu.roll(ids, 128 - 32, 1)
    s = pltpu.roll(ids, 128 - 64, 1)
    match = jnp.where((ids >> 1 == me) & (lane < PAIRS), 1.0, 0.0)
    values = [jnp.where(lane >= SRC, 1.0, 0.0)] + [v.astype(F32) for v in (r >> 4, r & 15, s >> 4, s & 15, ids & 1)]
    count = dot(ones, match.astype(BF16), ((1,), (1,)))
    found = [dot(ones, (match * v).astype(BF16), ((1,), (1,))) for v in values]
    single = jnp.where(count == 1.0, 1.0, 0.0)
    rank = dot(single.astype(BF16), before)
    hot = jnp.where(
        (jnp.broadcast_to(rank[0:1], (CTX, 128)) == row.astype(F32))
        & (jnp.broadcast_to(single[0:1], (CTX, 128)) > 0.5),
        1.0, 0.0,
    ).astype(BF16)
    load = jnp.where(row8 == 6, single, 0.0)
    load = jnp.where(row8 == 0, single * (2.0 * lane8.astype(F32) + found[0]), load)
    for i in range(1, 6):
        load = jnp.where(row8 == i, single * found[i], load)
    listed = dot(load.astype(BF16), hot, ((1,), (1,)))
    at = [jnp.broadcast_to(listed[i : i + 1], (8, 128)) for i in range(7)]
    several = jnp.where(count > 1.5, 1.0, 0.0)
    out = [at[0], 16.0 * at[1] + at[2], 16.0 * at[3] + at[4], at[6] - at[5], at[5]]
    out += [jnp.broadcast_to(jnp.sum(several, axis=1, keepdims=True), (8, 128)), several]
    rows = jnp.zeros((8, 128), F32)
    for i, value in enumerate(out):
        rows = jnp.where(row8 == i, value, rows)
    return rows.astype(jnp.int32)


def main_kernel(
    masks_h, br_h, bc_h, pupils_h, targets_h, ids_h, shifts_h, fst_h, gcat_h, inv_h, adj_h,
    resist, g2, e2, ids_all, listed, pair_cs, p_out, q_out,
    masks, br, bc, pupils, targets, fst, gown_v, inv, adj,
    ids_s, shifts_s, list_s, g1, e1, part, part_in, spec, prr, pii, u_all, pull, phases,
    load_sem, list_sem, x_send, x_recv, g_send, a_recv, f_recv, s_send, s_recv, i_send, i_recv, e_send, e_recv,
):
    tile = lax.axis_index("tile")
    q = lax.axis_index("ctx")
    core, y, z = q % 2, (q // 2) % SIDE, q // (2 * SIDE)
    major = z + core * (y - z)
    minor = y + core * (z - y)
    half = core * (SIDE * SIDE)
    slot = half + major * SIDE + minor
    own = pl.ds(pl.multiple_of(tile * R, R), R)

    loads = [
        pltpu.make_async_copy(src, dst, load_sem.at[i])
        for i, (src, dst) in enumerate(
            [
                (fst_h, fst),
                (br_h.at[:, own], br),
                (bc_h, bc),
                (masks_h, masks),
                (pupils_h, pupils),
                (gcat_h.at[own, :], gown_v),
                (inv_h, inv),
                (targets_h, targets),
                (adj_h, adj),
                (ids_h, ids_s),
                (shifts_h, shifts_s),
            ]
        )
    ]
    for copy in loads:
        copy.start()

    def ctx_id(mj, mn):
        zz = mj + core * (mn - mj)
        yy = mn + core * (mj - mn)
        return zz * (2 * SIDE) + yy * 2 + core

    sibling = q + 1 - 2 * core
    barrier = pltpu.get_barrier_semaphore()
    for k in range(1, SIDE):
        pl.semaphore_signal(barrier, inc=1, device_id={"ctx": ctx_id(major, (minor + k) % SIDE)}, device_id_type=MESH)
        pl.semaphore_signal(barrier, inc=1, device_id={"ctx": ctx_id((major + k) % SIDE, minor)}, device_id_type=MESH)
    for k in range(1, T):
        pl.semaphore_signal(barrier, inc=1, device_id={"tile": (tile + k) % T}, device_id_type=MESH)
    pl.semaphore_signal(barrier, inc=1, device_id={"ctx": sibling}, device_id_type=MESH)

    def put(step, i, half_rows, e):
        for t in range(T):
            part[step, t, i * Q : i * Q + H] = half_rows[t * H : (t + 1) * H]
            part[step, t, i * Q + H : (i + 1) * Q] = padded(e) if t == 0 else jnp.zeros((Q - H, 2 * M), F32)

    loads[0].wait()
    loads[1].wait()
    table = fst[...]
    p_st = dot(table, br[...]).astype(BF16)
    loads[2].wait()
    q_st = dot(table, bc[...]).astype(BF16)
    p_out[...] = p_st
    q_out[...] = q_st
    qq = jnp.concatenate([q_st, -q_st[M:], q_st[:M]], 0)
    pcat = jnp.concatenate([p_st[:M], p_st[M:]], 1)
    loads[3].wait()
    for m in range(2):
        a = dot(masks[m], qq, ((1,), (1,))).astype(BF16)
        s = dot(pcat, jnp.concatenate([a[:, : 2 * M], a[:, 2 * M :]], 0))
        put(0, m, *half_of(s))

    pl.semaphore_wait(barrier, T - 1 + 2 * (SIDE - 1) + 1)

    def tile_scatter(step):
        copies = []
        for k in range(1, T):
            to = (tile + k) % T
            copies.append(
                pltpu.make_async_remote_copy(
                    src_ref=part.at[step, to], dst_ref=part_in.at[step, k - 1],
                    send_sem=x_send.at[2 * step, k - 1], recv_sem=x_recv.at[2 * step, k - 1],
                    device_id={"tile": to}, device_id_type=MESH,
                )
            )
        for c in copies:
            c.start()
        return copies

    def tile_sum(step):
        return (part[step, tile] + part_in[step, 0]) + (part_in[step, 1] + part_in[step, 2])

    def to_ctx(ref, place, send_sem, recv_sem, to):
        return pltpu.make_async_remote_copy(
            src_ref=ref.at[place], dst_ref=ref.at[place], send_sem=send_sem, recv_sem=recv_sem,
            device_id={"ctx": to}, device_id_type=MESH,
        )

    minor_ids = {k: ctx_id(major, (minor + k) % SIDE) for k in NEAR_FIRST}
    major_ids = {k: ctx_id((major + k) % SIDE, minor) for k in NEAR_FIRST}
    first = half + major * SIDE

    def gather(buf, step, between, late, end):
        def along_minor(k, to):
            return to_ctx(buf, pl.ds(slot, 1), g_send.at[step], a_recv.at[step, k], to)

        def along_major(came, k):
            place = pl.ds(first + (minor + SIDE - came) % SIDE, 1)
            return to_ctx(buf, place, g_send.at[step], f_recv.at[step, k], major_ids[k])

        def to_sibling(row):
            return to_ctx(buf, pl.ds(half + row * SIDE, SIDE), s_send.at[step], s_recv.at[step], sibling)

        def bytes_of(blocks, send_sem, recv_sem):
            return to_ctx(buf, pl.ds(0, blocks), send_sem, recv_sem, sibling)

        for k in NEAR_FIRST:
            along_minor(k, minor_ids[k]).start()
        for k in NEAR_FIRST:
            along_major(0, k).start()
        between()

        def forward(i, _):
            came = near_first(i)
            along_minor(came, sibling).wait_recv()
            for k in NEAR_FIRST:
                along_major(came, k).start()
            return 0

        lax.fori_loop(1, SIDE, forward, 0)
        to_sibling(major).start()
        late()

        def arrive(i, _):
            k = near_first(i)
            bytes_of(SIDE, g_send.at[step], f_recv.at[step, k]).wait_recv()
            to_sibling((major + SIDE - k) % SIDE).start()
            return 0

        lax.fori_loop(1, SIDE, arrive, 0)
        end()
        bytes_of((SIDE - 1) * (SIDE + 1), g_send.at[step], f_recv.at[step, 0]).wait_send()
        bytes_of(SIDE * SIDE, s_send.at[step], s_recv.at[step]).wait()

    def line(buf, send, recv, phase):
        if phase == 2:
            places = [(pl.ds(half, SIDE * SIDE), sibling)]
        elif phase == 1:
            places = [(pl.ds(first, SIDE), major_ids[k]) for k in NEAR_FIRST]
        else:
            places = [(pl.ds(slot, 1), minor_ids[k]) for k in NEAR_FIRST]
        for place, to in places:
            to_ctx(buf, place, send.at[phase], recv.at[phase], to).start()
        blocks = (SIDE - 1, (SIDE - 1) * SIDE, SIDE * SIDE)[phase]
        return [to_ctx(buf, pl.ds(0, blocks), send.at[phase], recv.at[phase], sibling)]

    def spread_out(step, buf, es):
        total = tile_sum(step)
        buf[pl.ds(slot, 1)] = jnp.concatenate([total[:H], total[Q : Q + H]], 0).astype(BF16).reshape(1, 2 * H, 2 * M)
        es[pl.ds(slot, 1)] = jnp.concatenate([total[H : H + 1], total[Q + H : Q + H + 1]], 0).reshape(1, 2, 2 * M)
        e_sems = (e_send.at[step], e_recv.at[step])
        pending = []

        def between():
            pending.append(line(es, *e_sems, 0))
            if step == 0:
                wait_all(ids_copies.pop())
                ids_copies.append(line(ids_all, i_send, i_recv, 1))

        def late():
            wait_all(pending.pop())
            pending.append(line(es, *e_sems, 1))
            if step == 0:
                wait_all(ids_copies.pop())
                ids_copies.append(line(ids_all, i_send, i_recv, 2))

        def end():
            wait_all(pending.pop())
            pending.append(line(es, *e_sems, 2))

        gather(buf, step, between, late, end)
        wait_all(pending.pop())

    copies = tile_scatter(0)
    loads[9].wait()
    loads[10].wait()
    lane = lax.broadcasted_iota(jnp.int32, (1, 128), 1)
    own_ids = jnp.zeros((1, 128), jnp.int32)
    for c in range(2):
        for j in range(SRC):
            for place, value in ((0, ids_s[c, j]), (32, shifts_s[c, 0, j]), (64, shifts_s[c, 1, j])):
                own_ids = jnp.where(lane == place + c * SRC + j, value, own_ids)
    ids_all[pl.ds(slot, 1)] = own_ids.reshape(1, 1, 128)
    ids_copies = [line(ids_all, i_send, i_recv, 0)]

    rates = turn_rates(tile)
    for p in range(PAIRS):
        c, j = p // SRC, p % SRC
        phases[p] = cos_sin(rates, shifts_s[c, 0, j].astype(F32), shifts_s[c, 1, j].astype(F32))
    left64 = left_half((M, 2 * M))
    loads[4].wait()
    for k in range(K):
        pk = pupils[k]
        turned = swap(pk)
        prr[k] = jnp.where(left64, pk, turned)
        pii[k] = jnp.where(left64, -turned, pk)

    wait_all(copies)
    spread_out(0, g1, e1)
    wait_all(ids_copies.pop())

    leftq = left_half((Q, 2 * M))
    for c in range(2):
        sum_a = jnp.zeros((Q, 2 * M), F32)
        sum_b = jnp.zeros((Q, 2 * M), F32)
        for j in range(SRC):
            p = c * SRC + j
            master = ids_s[c, j]
            owner = master >> 1
            ocore = owner & 1
            oy = (owner >> 1) & (SIDE - 1)
            oz = owner >> 4
            place = ocore * (SIDE * SIDE) + oz * SIDE + oy + ocore * (SIDE - 1) * (oy - oz)
            g = pick(g1[place].astype(F32), e1[place], (master & 1) > 0)
            cs = phases[p]
            sum_a += g * cs
            sum_b += swap(g) * cs
        spec[tile, c * Q : (c + 1) * Q] = jnp.where(leftq, sum_a + swap(sum_a), swap(sum_b) - sum_b)
    copies = []
    for k in range(1, T):
        copies.append(
            pltpu.make_async_remote_copy(
                src_ref=spec.at[tile], dst_ref=spec.at[tile],
                send_sem=x_send.at[1, k - 1], recv_sem=x_recv.at[1, k - 1],
                device_id={"tile": (tile + k) % T}, device_id_type=MESH,
            )
        )
    for c in copies:
        c.start()
    listed[...] = pair_list(ids_all[...].reshape(CTX, 128), q)
    list_copy = pltpu.make_async_copy(listed, list_s, list_sem)
    list_copy.start()
    for copy in loads[5:9]:
        copy.wait()
    fown = fst[:, own]
    fcat = jnp.concatenate([fown[:M], fown[M:]], 1)
    gown = gown_v[...]
    wait_all(copies)

    halves = [jnp.concatenate([spec[t, c * Q : c * Q + H] for t in range(T)], 0) for c in range(2)]
    spectra = expand(halves, [spec[0, c * Q + H : c * Q + H + 1] for c in range(2)])
    for c in range(2):
        s = spectra[c]
        s_sw = swap(s)
        s2 = jnp.where(left64, -s_sw, s_sw)
        s2_sw = jnp.where(left64, s, -s)
        for k in range(K):
            a1 = prr[k] * s + pii[k] * s_sw
            a2 = prr[k] * s2 + pii[k] * s2_sw
            both = jnp.concatenate([a1, a2], 0).astype(BF16)
            u_all[c, k * R : (k + 1) * R] = dot(gown, both).astype(BF16)

    def field_of(i):
        c, b = i // T, i % T
        return dot(u_all[c], inv[:, b * 2 * R : (b + 1) * 2 * R])

    def use(i, field):
        c, b = i // T, i % T
        cols = slice(b * R, (b + 1) * R)
        intensity = jnp.zeros((R, R), F32)
        for k in range(K):
            fr = field[k * R : (k + 1) * R, :R]
            fi = field[k * R : (k + 1) * R, R:]
            intensity += fr * fr + fi * fi
        image = 1.0 / (1.0 + jnp.exp(-STEEPNESS * (intensity - THRESHOLD)))
        resist[c, :, cols] = image.astype(BF16)
        slope = (image - targets[c, :, cols].astype(F32)) * (2.0 * STEEPNESS) * image * (1.0 - image)
        slope2 = jnp.concatenate([slope, slope], 1)
        for k in range(K):
            pull[c, k * R : (k + 1) * R, b * 2 * R : (b + 1) * 2 * R] = (
                slope2 * field[k * R : (k + 1) * R]
            ).astype(BF16)

    def gradient(c):
        folded = dot(pull[c], adj[...]).astype(BF16)
        g_a = jnp.zeros((M, 2 * M), F32)
        g_b = jnp.zeros((M, 2 * M), F32)
        for k in range(K):
            fk = folded[k * R : (k + 1) * R]
            ga = dot(fcat, jnp.concatenate([fk[:, : 2 * M], fk[:, 2 * M :]], 0))
            g_a += prr[k] * ga
            g_b += pii[k] * ga
        return g_a + swap(g_b)

    grads = []
    coming = field_of(0)
    for i in range(2 * T):
        field = coming
        if i < 2 * T - 1:
            coming = field_of(i + 1)
        use(i, field)
        if i % T == T - 1:
            grads.append(gradient(i // T))
    for c, (half_rows, e) in enumerate(fold(grads)):
        put(1, c, half_rows, e)

    copies = tile_scatter(1)
    list_copy.wait()

    def pair_phases(i, _):
        for b in range(8):
            k = i * 8 + b
            pair_cs[k] = cos_sin(rates, list_s[1, k].astype(F32), list_s[2, k].astype(F32))
        return 0

    lax.fori_loop(0, CTX // 8, pair_phases, 0)
    wait_all(copies)
    spread_out(1, g2, e2)


def pair_terms(g2, e2, context, cs):
    host = context // 2
    g = pick(g2[host].astype(F32), e2[host], context % 2 > 0)
    return g * cs, swap(g) * cs


def several_kernel(list_v, ids_v, g2, e2, sums, list_s, ids_s, sems):
    me = lax.axis_index("ctx")
    rates = turn_rates(lax.axis_index("tile"))
    sums[...] = jnp.zeros_like(sums)

    @pl.when(jnp.max(list_v[5:6, :]) > 0)
    def _():
        copies = [
            pltpu.make_async_copy(list_v, list_s, sems.at[0]),
            pltpu.make_async_copy(ids_v, ids_s, sems.at[1]),
        ]
        for copy in copies:
            copy.start()
        wait_all(copies)

        def host(h, _):
            @pl.when(list_s[6, h] > 0)
            def _():
                def one(j, _):
                    master = ids_s[h, 0, j]

                    @pl.when(master >> 1 == me)
                    def _():
                        m = master & 1
                        cs = cos_sin(rates, ids_s[h, 0, 32 + j].astype(F32), ids_s[h, 0, 64 + j].astype(F32))
                        a, b = pair_terms(g2, e2, 2 * h + j // SRC, cs)
                        sums[2 * m] += a
                        sums[2 * m + 1] += b

                    return 0

                lax.fori_loop(0, PAIRS, one, 0)

            return 0

        lax.fori_loop(0, CTX, host, 0)


def rows_kernel(list_v, pair_cs, g2, e2, sums, rows, list_s, sem, x_send, x_recv):
    tile = lax.axis_index("tile")
    copy = pltpu.make_async_copy(list_v, list_s, sem)
    copy.start()
    barrier = pltpu.get_barrier_semaphore()
    for k in range(1, T):
        pl.semaphore_signal(barrier, inc=1, device_id={"tile": (tile + k) % T}, device_id_type=MESH)
    left = left_half((Q, 2 * M))
    copy.wait()
    block = 8

    def step(i, carry):
        total = list(carry)
        for b in range(block):
            k = i * block + b
            a, b = pair_terms(g2, e2, list_s[0, k], pair_cs[k])
            for m in range(2):
                weight = list_s[3 + m, k].astype(F32)
                total[2 * m] += a * weight
                total[2 * m + 1] += b * weight
        return tuple(total)

    total = lax.fori_loop(0, CTX // block, step, tuple(sums[i] for i in range(4)))
    for m in range(2):
        a, b = total[2 * m : 2 * m + 2]
        rows[tile, m * Q : (m + 1) * Q] = jnp.where(left, a - swap(a), b + swap(b)).astype(BF16)
    pl.semaphore_wait(barrier, T - 1)
    copies = []
    for k in range(1, T):
        copies.append(
            pltpu.make_async_remote_copy(
                src_ref=rows.at[tile], dst_ref=rows.at[tile],
                send_sem=x_send.at[k - 1], recv_sem=x_recv.at[k - 1],
                device_id={"tile": (tile + k) % T}, device_id_type=MESH,
            )
        )
    for c in copies:
        c.start()
    wait_all(copies)


def last_kernel(rows, p_st, q_st, resist_v, out, resist, held, sem):
    left = left_half((M, 2 * M))
    copies = [pltpu.make_async_copy(resist_v, resist, sem.at[2])]
    copies[0].start()
    for m in range(2):
        parts = [rows[t].astype(F32)[m * Q : (m + 1) * Q] for t in range(T)]
        g = jnp.concatenate([part[:H] for part in parts] + [to_rows(parts[0][H : H + 1])], 0)
        turned = swap(g)
        both = jnp.concatenate([g, jnp.where(left, turned, -turned)], 0).astype(BF16)
        lifted = dot(p_st[...], both, ((0,), (0,))).astype(BF16)
        held[m] = dot(lifted, q_st[...])
        copies.append(pltpu.make_async_copy(held.at[m], out.at[m], sem.at[m]))
        copies[-1].start()
    wait_all(copies)


def local(masks, blur_rows, blur_cols, pupils, targets, context_masters, offsets):
    vmem = pl.BlockSpec(memory_space=pltpu.VMEM)
    hbm = pl.BlockSpec(memory_space=pltpu.HBM)
    dma = pltpu.SemaphoreType.DMA
    stay = functools.partial(pltpu.with_memory_space_constraint, memory_space=pltpu.HBM)
    resist_v, g2, e2, ids_all, listed, pair_cs, p_st, q_st = pl.pallas_call(
        main_kernel,
        out_shape=(
            jax.ShapeDtypeStruct((2, R, N), BF16),
            jax.ShapeDtypeStruct((CTX, 2 * H, 2 * M), BF16),
            jax.ShapeDtypeStruct((CTX, 2, 2 * M), F32),
            jax.ShapeDtypeStruct((CTX, 1, 128), jnp.int32),
            jax.ShapeDtypeStruct((8, 128), jnp.int32),
            jax.ShapeDtypeStruct((CTX, Q, 2 * M), F32),
            jax.ShapeDtypeStruct((2 * M, R), BF16),
            jax.ShapeDtypeStruct((2 * M, N), BF16),
        ),
        in_specs=[hbm] * 11,
        out_specs=(vmem,) * 8,
        scratch_shapes=[
            pltpu.VMEM((2, R, N), BF16),
            pltpu.VMEM((N, R), BF16),
            pltpu.VMEM((N, N), BF16),
            pltpu.VMEM((K, M, 2 * M), F32),
            pltpu.VMEM((2, R, N), BF16),
            pltpu.VMEM((2 * M, N), BF16),
            pltpu.VMEM((R, 2 * M), BF16),
            pltpu.VMEM((2 * M, 2 * N), BF16),
            pltpu.VMEM((2 * N, 4 * M), BF16),
            pltpu.SMEM((2, SRC), jnp.int32),
            pltpu.SMEM((2, 2, SRC), jnp.int32),
            pltpu.SMEM((8, 128), jnp.int32),
            pltpu.VMEM((CTX, 2 * H, 2 * M), BF16),
            pltpu.VMEM((CTX, 2, 2 * M), F32),
            pltpu.VMEM((2, T, 2 * Q, 2 * M), F32),
            pltpu.VMEM((2, T - 1, 2 * Q, 2 * M), F32),
            pltpu.VMEM((T, 2 * Q, 2 * M), F32),
            pltpu.VMEM((K, M, 2 * M), F32),
            pltpu.VMEM((K, M, 2 * M), F32),
            pltpu.VMEM((2, K * R, 2 * M), BF16),
            pltpu.VMEM((2, K * R, 2 * N), BF16),
            pltpu.VMEM((PAIRS, Q, 2 * M), F32),
            dma((11,)),
            dma,
            dma((3, T - 1)),
            dma((3, T - 1)),
            dma((2,)),
            dma((2, SIDE)),
            dma((2, SIDE)),
            dma((2,)),
            dma((2,)),
            dma((3,)),
            dma((3,)),
            dma((2, 3)),
            dma((2, 3)),
        ],
        compiler_params=pltpu.CompilerParams(
            collective_id=0, has_side_effects=True, vmem_limit_bytes=40 << 20
        ),
        name="main",
    )(
        *map(stay, (masks, blur_rows, blur_cols, pupils, targets)),
        stay(context_masters),
        stay(jnp.transpose(offsets, (0, 2, 1))),
        *map(stay, map(jnp.asarray, tables())),
    )
    sums = pl.pallas_call(
        several_kernel,
        out_shape=jax.ShapeDtypeStruct((4, Q, 2 * M), F32),
        in_specs=[vmem] * 4,
        out_specs=vmem,
        scratch_shapes=[
            pltpu.SMEM((8, 128), jnp.int32),
            pltpu.SMEM((CTX, 1, 128), jnp.int32),
            dma((2,)),
        ],
        compiler_params=pltpu.CompilerParams(vmem_limit_bytes=32 << 20),
        name="several",
    )(listed, ids_all, g2, e2)
    rows = pl.pallas_call(
        rows_kernel,
        out_shape=jax.ShapeDtypeStruct((T, 2 * Q, 2 * M), BF16),
        in_specs=[vmem] * 5,
        out_specs=vmem,
        scratch_shapes=[pltpu.SMEM((8, 128), jnp.int32), dma, dma((T - 1,)), dma((T - 1,))],
        compiler_params=pltpu.CompilerParams(
            collective_id=1, has_side_effects=True, vmem_limit_bytes=32 << 20
        ),
        name="rows",
    )(listed, pair_cs, g2, e2, sums)
    mask_grad, resist = pl.pallas_call(
        last_kernel,
        out_shape=(
            jax.ShapeDtypeStruct((2, R, N), F32),
            jax.ShapeDtypeStruct((2, R, N), BF16),
        ),
        in_specs=[vmem] * 4,
        out_specs=(hbm, hbm),
        scratch_shapes=[pltpu.VMEM((2, R, N), F32), dma((3,))],
        compiler_params=pltpu.CompilerParams(vmem_limit_bytes=32 << 20),
        name="last",
    )(rows, p_st, q_st, resist_v)
    return (resist, mask_grad)


def solution(mesh):
    placed = (
        P("ctx", "tile", None),
        P(),
        P(),
        P(),
        P("ctx", "tile", None),
        P("ctx", None),
        P("ctx", None, None),
    )
    return jax.shard_map(
        local,
        mesh=mesh,
        in_specs=placed,
        out_specs=(P("ctx", "tile", None), P("ctx", "tile", None)),
        check_vma=False,
    )
```

```python
import functools
import math

import jax
import jax.numpy as jnp
import ml_dtypes
import numpy as np
from jax import lax
from jax.experimental import pallas as pl
from jax.experimental.pallas import tpu as pltpu
from jax.sharding import PartitionSpec as P

STEEPNESS = 4.0
THRESHOLD = 1.0
N = 512
M = 64
K = 6
T = 4
R = N // T
H = M // (2 * T)
Q = 16
SIDE = 8
CTX = 2 * SIDE * SIDE
SRC = 12
PAIRS = 2 * SRC
MESH = pl.DeviceIdType.MESH
F32 = jnp.float32
BF16 = jnp.bfloat16
NEAR_FIRST = (1, 7, 2, 6, 3, 5, 4)


def tables():
    freq = (np.arange(M) - M // 2) % N
    angle = (freq[:, None] * np.arange(N)[None, :] % N) * (2.0 * math.pi / N)
    cos = np.cos(angle) / math.sqrt(N)
    sin = np.sin(angle) / math.sqrt(N)
    fst = np.concatenate([cos, -sin], 0)
    gcat = np.concatenate([cos.T, sin.T], 1)
    inv = np.concatenate([np.concatenate([cos, sin], 1), np.concatenate([-sin, cos], 1)], 0)
    adj = np.concatenate([np.concatenate([cos.T, -sin.T], 1), np.concatenate([sin.T, cos.T], 1)], 0)
    adj = np.concatenate([adj, -adj[:, M:], adj[:, :M]], 1)
    order = np.arange(2 * N).reshape(2, T, N // T).transpose(1, 0, 2).reshape(-1)
    return [t.astype(ml_dtypes.bfloat16) for t in (fst, gcat, inv[:, order], adj[order])]


def sine_coefficients():
    w = 0.25 * np.cos(np.pi * (np.arange(400) + 0.5) / 400)
    powers = np.stack([w ** (2 * i + 1) for i in range(6)], 1)
    return [float(c) for c in np.linalg.lstsq(powers, np.sin(2 * np.pi * w), rcond=None)[0]]


SINE = sine_coefficients()


def swap(a):
    return pltpu.roll(a, M, 1)


def left_half(shape):
    return lax.broadcasted_iota(jnp.int32, shape, 1) < M


def grid(shape):
    return lax.broadcasted_iota(jnp.int32, shape, 0), lax.broadcasted_iota(jnp.int32, shape, 1)


def turn_rates(tile):
    row, lane = grid((Q, 2 * M))
    v = lane % M
    plain = row < H
    early = v <= M // 2
    f_u = jnp.where(plain, row + (tile * H - M // 2), jnp.where(early, 0, v - M // 2))
    f_v = jnp.where(plain | early, v - M // 2, -(M // 2))
    late = jnp.where(lane < M, 0.0, 0.25).astype(F32)
    return f_u.astype(F32) * (1.0 / N), f_v.astype(F32) * (1.0 / N), late


def from_rows(a):
    row, lane = grid(a.shape)
    real = jnp.where((lane == row + M // 2) & (row > 0), jnp.broadcast_to(a[:, 0:1], a.shape), 0.0)
    imag = jnp.where((lane == row + M + M // 2) & (row > 0), jnp.broadcast_to(a[:, M : M + 1], a.shape), 0.0)
    return jnp.sum(real + imag, axis=0, keepdims=True)


def to_rows(e):
    shape = (M // 2, 2 * M)
    row, lane = grid(shape)
    wide = jnp.broadcast_to(e, shape)
    real = jnp.sum(jnp.where((lane == row + M // 2) & (row > 0), wide, 0.0), axis=1, keepdims=True)
    imag = jnp.sum(jnp.where((lane == row + M + M // 2) & (row > 0), wide, 0.0), axis=1, keepdims=True)
    first = jnp.where((row == 0) & (lane % M <= M // 2), wide, 0.0)
    return first + jnp.where(lane == 0, real, 0.0) + jnp.where(lane == M, imag, 0.0)


def split(a):
    high = a.astype(BF16)
    return high, (a - high.astype(F32)).astype(BF16)


def mirrored(a):
    src, dst = grid((2 * M, 2 * M))
    real = jnp.where((src + dst == M) & (src < M) & (dst < M), 1.0, 0.0)
    both = real - jnp.where((src + dst == 3 * M) & (src >= M), 1.0, 0.0)
    out = dot(jnp.concatenate(split(a), 0), both.astype(BF16))
    return out[: a.shape[0]] + out[a.shape[0] :]


def flipped(blocks):
    row, col = grid((M // 2, M // 2))
    turn = jnp.where(row + col == M // 2, 1.0, 0.0).astype(BF16)
    out = dot(turn, jnp.concatenate([part for a in blocks for part in split(a)], 1))
    part = [out[:, i * 2 * M : (i + 1) * 2 * M] for i in range(2 * len(blocks))]
    return [part[2 * i] + part[2 * i + 1] for i in range(len(blocks))]


def expand(halves, es):
    row, lane = grid((M // 2, 2 * M))
    wide = [jnp.broadcast_to(e, (16, 2 * M)) for e in es]
    turned = mirrored(jnp.concatenate([*halves, *wide], 0))
    lower = flipped([turned[: M // 2], turned[M // 2 : M]])
    out = []
    for i in range(2):
        e_turned = jnp.broadcast_to(turned[M + 16 * i : M + 16 * i + 1], row.shape)
        first = jnp.where((row == 0) & (lane % M > M // 2), e_turned, 0.0)
        out.append(jnp.concatenate([halves[i], lower[i] + first + to_rows(es[i])], 0))
    return out


def fold(grads):
    low = [grad[M // 2 :] for grad in grads]
    turned = mirrored(jnp.concatenate(low, 0))
    upper = flipped([turned[: M // 2], turned[M // 2 :]])
    v = lax.broadcasted_iota(jnp.int32, (1, 2 * M), 1) % M
    out = []
    for i in range(2):
        t = turned[i * (M // 2) : i * (M // 2) + 1]
        e = jnp.where(v <= M // 2, low[i][0:1], 0.0) + jnp.where((v > 0) & (v < M // 2), t, 0.0)
        out.append((grads[i][: M // 2] + upper[i], e + from_rows(low[i])))
    return out


def half_of(spectrum):
    low = spectrum[M // 2 :]
    v = lax.broadcasted_iota(jnp.int32, (1, 2 * M), 1) % M
    return spectrum[: M // 2], jnp.where(v <= M // 2, low[0:1], 0.0) + from_rows(low)


def padded(e):
    return jnp.where(lax.broadcasted_iota(jnp.int32, (Q - H, 2 * M), 0) == 0, jnp.broadcast_to(e, (Q - H, 2 * M)), 0.0)


def pick(block, es, second):
    return jnp.concatenate(
        [jnp.where(second, block[H:], block[:H]), padded(jnp.where(second, es[1:2], es[0:1]))], 0
    )


def cos_sin(rates, r, s):
    y = rates[0] * r + rates[1] * s - rates[2]
    y = y - jnp.floor(y + 0.5)
    w = 0.25 - jnp.abs(y)
    z = w * w
    total = jnp.full_like(z, SINE[-1])
    for c in SINE[-2::-1]:
        total = total * z + c
    return total * w


def dot(a, b, dims=((1,), (0,))):
    return lax.dot_general(a, b, (dims, ((), ())), preferred_element_type=F32)


def wait_all(copies):
    for c in copies:
        c.wait()


def near_first(i):
    return (i % 2) * ((i + 1) // 2) + (1 - i % 2) * (SIDE - i // 2)


def pair_list(ids, me):
    row, lane = grid((CTX, 128))
    row8, lane8 = grid((8, 128))
    ones = jnp.full((8, 128), 1.0, BF16)
    before = jnp.where(row < lane, 1.0, 0.0).astype(BF16)
    r = pltpu.roll(ids, 128 - 32, 1)
    s = pltpu.roll(ids, 128 - 64, 1)
    match = jnp.where((ids >> 1 == me) & (lane < PAIRS), 1.0, 0.0)
    values = [jnp.where(lane >= SRC, 1.0, 0.0)] + [v.astype(F32) for v in (r >> 4, r & 15, s >> 4, s & 15, ids & 1)]
    count = dot(ones, match.astype(BF16), ((1,), (1,)))
    found = [dot(ones, (match * v).astype(BF16), ((1,), (1,))) for v in values]
    single = jnp.where(count == 1.0, 1.0, 0.0)
    rank = dot(single.astype(BF16), before)
    hot = jnp.where(
        (jnp.broadcast_to(rank[0:1], (CTX, 128)) == row.astype(F32))
        & (jnp.broadcast_to(single[0:1], (CTX, 128)) > 0.5),
        1.0, 0.0,
    ).astype(BF16)
    load = jnp.where(row8 == 6, single, 0.0)
    load = jnp.where(row8 == 0, single * (2.0 * lane8.astype(F32) + found[0]), load)
    for i in range(1, 6):
        load = jnp.where(row8 == i, single * found[i], load)
    listed = dot(load.astype(BF16), hot, ((1,), (1,)))
    at = [jnp.broadcast_to(listed[i : i + 1], (8, 128)) for i in range(7)]
    several = jnp.where(count > 1.5, 1.0, 0.0)
    out = [at[0], 16.0 * at[1] + at[2], 16.0 * at[3] + at[4], at[6] - at[5], at[5]]
    out += [jnp.broadcast_to(jnp.sum(several, axis=1, keepdims=True), (8, 128)), several]
    rows = jnp.zeros((8, 128), F32)
    for i, value in enumerate(out):
        rows = jnp.where(row8 == i, value, rows)
    return rows.astype(jnp.int32)


def single_phases(ids, me, rates):
    row, lane = grid((CTX, 128))
    match = jnp.where((ids >> 1 == me) & (lane < PAIRS), 1.0, 0.0)

    def column(values):
        return jnp.broadcast_to(jnp.sum(match * values.astype(F32), axis=1, keepdims=True), (CTX, 128))

    r = column(pltpu.roll(ids, 128 - 32, 1))
    s = column(pltpu.roll(ids, 128 - 64, 1))
    second = column(jnp.where(lane >= SRC, 1.0, 0.0))
    master = column(ids & 1)
    single = jnp.where(column(jnp.ones_like(match)) == 1.0, 1.0, 0.0)
    cs = cos_sin([jnp.broadcast_to(rate[H : H + 1], (CTX, 128)) for rate in rates], r, s)
    return jnp.where(single * (1.0 - master) > 0.5, cs, 0.0), jnp.where(single * master > 0.5, cs, 0.0), single * second


def main_kernel(
    masks_h, br_h, bc_h, pupils_h, targets_h, ids_h, shifts_h, fst_h, gcat_h, inv_h, adj_h,
    resist, g2, e2, ids_all, listed, pair_cs, single_cs, p_out, q_out,
    masks, br, bc, pupils, targets, fst, gown_v, inv, adj,
    ids_s, shifts_s, list_s, g1, e1, part, part_in, spec, prr, pii, u_all, pull, phases,
    load_sem, list_sem, x_send, x_recv, g_send, a_recv, f_recv, s_send, s_recv, i_send, i_recv, e_send, e_recv,
):
    tile = lax.axis_index("tile")
    q = lax.axis_index("ctx")
    core, y, z = q % 2, (q // 2) % SIDE, q // (2 * SIDE)
    major = z + core * (y - z)
    minor = y + core * (z - y)
    half = core * (SIDE * SIDE)
    slot = half + major * SIDE + minor
    own = pl.ds(pl.multiple_of(tile * R, R), R)

    loads = [
        pltpu.make_async_copy(src, dst, load_sem.at[i])
        for i, (src, dst) in enumerate(
            [
                (fst_h, fst),
                (br_h.at[:, own], br),
                (bc_h, bc),
                (masks_h, masks),
                (pupils_h, pupils),
                (gcat_h.at[own, :], gown_v),
                (inv_h, inv),
                (targets_h, targets),
                (adj_h, adj),
                (ids_h, ids_s),
                (shifts_h, shifts_s),
            ]
        )
    ]
    for copy in loads:
        copy.start()

    def ctx_id(mj, mn):
        zz = mj + core * (mn - mj)
        yy = mn + core * (mj - mn)
        return zz * (2 * SIDE) + yy * 2 + core

    sibling = q + 1 - 2 * core
    barrier = pltpu.get_barrier_semaphore()
    for k in range(1, SIDE):
        pl.semaphore_signal(barrier, inc=1, device_id={"ctx": ctx_id(major, (minor + k) % SIDE)}, device_id_type=MESH)
        pl.semaphore_signal(barrier, inc=1, device_id={"ctx": ctx_id((major + k) % SIDE, minor)}, device_id_type=MESH)
    for k in range(1, T):
        pl.semaphore_signal(barrier, inc=1, device_id={"tile": (tile + k) % T}, device_id_type=MESH)
    pl.semaphore_signal(barrier, inc=1, device_id={"ctx": sibling}, device_id_type=MESH)

    def put(step, i, half_rows, e):
        for t in range(T):
            part[step, t, i * Q : i * Q + H] = half_rows[t * H : (t + 1) * H]
            part[step, t, i * Q + H : (i + 1) * Q] = padded(e) if t == 0 else jnp.zeros((Q - H, 2 * M), F32)

    loads[0].wait()
    loads[1].wait()
    table = fst[...]
    p_st = dot(table, br[...]).astype(BF16)
    loads[2].wait()
    q_st = dot(table, bc[...]).astype(BF16)
    p_out[...] = p_st
    q_out[...] = q_st
    qq = jnp.concatenate([q_st, -q_st[M:], q_st[:M]], 0)
    pcat = jnp.concatenate([p_st[:M], p_st[M:]], 1)
    loads[3].wait()
    for m in range(2):
        a = dot(masks[m], qq, ((1,), (1,))).astype(BF16)
        s = dot(pcat, jnp.concatenate([a[:, : 2 * M], a[:, 2 * M :]], 0))
        put(0, m, *half_of(s))

    pl.semaphore_wait(barrier, T - 1 + 2 * (SIDE - 1) + 1)

    def tile_scatter(step):
        copies = []
        for k in range(1, T):
            to = (tile + k) % T
            copies.append(
                pltpu.make_async_remote_copy(
                    src_ref=part.at[step, to], dst_ref=part_in.at[step, k - 1],
                    send_sem=x_send.at[2 * step, k - 1], recv_sem=x_recv.at[2 * step, k - 1],
                    device_id={"tile": to}, device_id_type=MESH,
                )
            )
        for c in copies:
            c.start()
        return copies

    def tile_sum(step):
        return (part[step, tile] + part_in[step, 0]) + (part_in[step, 1] + part_in[step, 2])

    def to_ctx(ref, place, send_sem, recv_sem, to):
        return pltpu.make_async_remote_copy(
            src_ref=ref.at[place], dst_ref=ref.at[place], send_sem=send_sem, recv_sem=recv_sem,
            device_id={"ctx": to}, device_id_type=MESH,
        )

    minor_ids = {k: ctx_id(major, (minor + k) % SIDE) for k in NEAR_FIRST}
    major_ids = {k: ctx_id((major + k) % SIDE, minor) for k in NEAR_FIRST}
    first = half + major * SIDE

    def gather(buf, step, between, late, end):
        def along_minor(k, to):
            return to_ctx(buf, pl.ds(slot, 1), g_send.at[step], a_recv.at[step, k], to)

        def along_major(came, k):
            place = pl.ds(first + (minor + SIDE - came) % SIDE, 1)
            return to_ctx(buf, place, g_send.at[step], f_recv.at[step, k], major_ids[k])

        def to_sibling(row):
            return to_ctx(buf, pl.ds(half + row * SIDE, SIDE), s_send.at[step], s_recv.at[step], sibling)

        def bytes_of(blocks, send_sem, recv_sem):
            return to_ctx(buf, pl.ds(0, blocks), send_sem, recv_sem, sibling)

        for k in NEAR_FIRST:
            along_minor(k, minor_ids[k]).start()
        between()
        for k in NEAR_FIRST:
            along_major(0, k).start()

        def forward(i, _):
            came = near_first(i)
            along_minor(came, sibling).wait_recv()
            for k in NEAR_FIRST:
                along_major(came, k).start()
            return 0

        lax.fori_loop(1, SIDE, forward, 0)
        to_sibling(major).start()
        late()

        def arrive(i, _):
            k = near_first(i)
            bytes_of(SIDE, g_send.at[step], f_recv.at[step, k]).wait_recv()
            to_sibling((major + SIDE - k) % SIDE).start()
            return 0

        lax.fori_loop(1, SIDE, arrive, 0)
        end()
        bytes_of((SIDE - 1) * (SIDE + 1), g_send.at[step], f_recv.at[step, 0]).wait_send()
        bytes_of(SIDE * SIDE, s_send.at[step], s_recv.at[step]).wait()

    def line(buf, send, recv, phase):
        if phase == 2:
            places = [(pl.ds(half, SIDE * SIDE), sibling)]
        elif phase == 1:
            places = [(pl.ds(first, SIDE), major_ids[k]) for k in NEAR_FIRST]
        else:
            places = [(pl.ds(slot, 1), minor_ids[k]) for k in NEAR_FIRST]
        for place, to in places:
            to_ctx(buf, place, send.at[phase], recv.at[phase], to).start()
        blocks = (SIDE - 1, (SIDE - 1) * SIDE, SIDE * SIDE)[phase]
        return [to_ctx(buf, pl.ds(0, blocks), send.at[phase], recv.at[phase], sibling)]

    def spread_out(step, buf, es):
        total = tile_sum(step)
        buf[pl.ds(slot, 1)] = jnp.concatenate([total[:H], total[Q : Q + H]], 0).astype(BF16).reshape(1, 2 * H, 2 * M)
        es[pl.ds(slot, 1)] = jnp.concatenate([total[H : H + 1], total[Q + H : Q + H + 1]], 0).reshape(1, 2, 2 * M)
        e_sems = (e_send.at[step], e_recv.at[step])
        pending = []

        def between():
            pending.append(line(es, *e_sems, 0))
            if step == 0:
                wait_all(ids_copies.pop())
                ids_copies.append(line(ids_all, i_send, i_recv, 1))

        def late():
            wait_all(pending.pop())
            pending.append(line(es, *e_sems, 1))
            if step == 0:
                wait_all(ids_copies.pop())
                ids_copies.append(line(ids_all, i_send, i_recv, 2))

        def end():
            wait_all(pending.pop())
            pending.append(line(es, *e_sems, 2))

        gather(buf, step, between, late, end)
        wait_all(pending.pop())

    copies = tile_scatter(0)
    loads[9].wait()
    loads[10].wait()
    lane = lax.broadcasted_iota(jnp.int32, (1, 128), 1)
    own_ids = jnp.zeros((1, 128), jnp.int32)
    for c in range(2):
        for j in range(SRC):
            for place, value in ((0, ids_s[c, j]), (32, shifts_s[c, 0, j]), (64, shifts_s[c, 1, j])):
                own_ids = jnp.where(lane == place + c * SRC + j, value, own_ids)
    ids_all[pl.ds(slot, 1)] = own_ids.reshape(1, 1, 128)
    ids_copies = [line(ids_all, i_send, i_recv, 0)]

    rates = turn_rates(tile)
    for p in range(PAIRS):
        c, j = p // SRC, p % SRC
        phases[p] = cos_sin(rates, shifts_s[c, 0, j].astype(F32), shifts_s[c, 1, j].astype(F32))
    left64 = left_half((M, 2 * M))
    loads[4].wait()
    for k in range(K):
        pk = pupils[k]
        turned = swap(pk)
        prr[k] = jnp.where(left64, pk, turned)
        pii[k] = jnp.where(left64, -turned, pk)

    wait_all(copies)
    spread_out(0, g1, e1)
    wait_all(ids_copies.pop())

    leftq = left_half((Q, 2 * M))
    for c in range(2):
        sum_a = jnp.zeros((Q, 2 * M), F32)
        sum_b = jnp.zeros((Q, 2 * M), F32)
        for j in range(SRC):
            p = c * SRC + j
            master = ids_s[c, j]
            owner = master >> 1
            ocore = owner & 1
            oy = (owner >> 1) & (SIDE - 1)
            oz = owner >> 4
            place = ocore * (SIDE * SIDE) + oz * SIDE + oy + ocore * (SIDE - 1) * (oy - oz)
            g = pick(g1[place].astype(F32), e1[place], (master & 1) > 0)
            cs = phases[p]
            sum_a += g * cs
            sum_b += swap(g) * cs
        spec[tile, c * Q : (c + 1) * Q] = jnp.where(leftq, sum_a + swap(sum_a), swap(sum_b) - sum_b)
    copies = []
    for k in range(1, T):
        copies.append(
            pltpu.make_async_remote_copy(
                src_ref=spec.at[tile], dst_ref=spec.at[tile],
                send_sem=x_send.at[1, k - 1], recv_sem=x_recv.at[1, k - 1],
                device_id={"tile": (tile + k) % T}, device_id_type=MESH,
            )
        )
    for c in copies:
        c.start()
    listed[...] = pair_list(ids_all[...].reshape(CTX, 128), q)
    list_copy = pltpu.make_async_copy(listed, list_s, list_sem)
    list_copy.start()
    for copy in loads[5:9]:
        copy.wait()
    fown = fst[:, own]
    fcat = jnp.concatenate([fown[:M], fown[M:]], 1)
    gown = gown_v[...]
    wait_all(copies)

    halves = [jnp.concatenate([spec[t, c * Q : c * Q + H] for t in range(T)], 0) for c in range(2)]
    spectra = expand(halves, [spec[0, c * Q + H : c * Q + H + 1] for c in range(2)])
    for c in range(2):
        s = spectra[c]
        s_sw = swap(s)
        s2 = jnp.where(left64, -s_sw, s_sw)
        s2_sw = jnp.where(left64, s, -s)
        for k in range(K):
            a1 = prr[k] * s + pii[k] * s_sw
            a2 = prr[k] * s2 + pii[k] * s2_sw
            both = jnp.concatenate([a1, a2], 0).astype(BF16)
            u_all[c, k * R : (k + 1) * R] = dot(gown, both).astype(BF16)

    def field_of(i):
        c, b = i // T, i % T
        return dot(u_all[c], inv[:, b * 2 * R : (b + 1) * 2 * R])

    def use(i, field):
        c, b = i // T, i % T
        cols = slice(b * R, (b + 1) * R)
        intensity = jnp.zeros((R, R), F32)
        for k in range(K):
            fr = field[k * R : (k + 1) * R, :R]
            fi = field[k * R : (k + 1) * R, R:]
            intensity += fr * fr + fi * fi
        image = 1.0 / (1.0 + jnp.exp(-STEEPNESS * (intensity - THRESHOLD)))
        resist[c, :, cols] = image.astype(BF16)
        slope = (image - targets[c, :, cols].astype(F32)) * (2.0 * STEEPNESS) * image * (1.0 - image)
        slope2 = jnp.concatenate([slope, slope], 1)
        for k in range(K):
            pull[c, k * R : (k + 1) * R, b * 2 * R : (b + 1) * 2 * R] = (
                slope2 * field[k * R : (k + 1) * R]
            ).astype(BF16)

    def gradient(c):
        folded = dot(pull[c], adj[...]).astype(BF16)
        g_a = jnp.zeros((M, 2 * M), F32)
        g_b = jnp.zeros((M, 2 * M), F32)
        for k in range(K):
            fk = folded[k * R : (k + 1) * R]
            ga = dot(fcat, jnp.concatenate([fk[:, : 2 * M], fk[:, 2 * M :]], 0))
            g_a += prr[k] * ga
            g_b += pii[k] * ga
        return g_a + swap(g_b)

    grads = []
    coming = field_of(0)
    for i in range(2 * T):
        field = coming
        if i < 2 * T - 1:
            coming = field_of(i + 1)
        use(i, field)
        if i % T == T - 1:
            grads.append(gradient(i // T))
    for c, (half_rows, e) in enumerate(fold(grads)):
        put(1, c, half_rows, e)

    copies = tile_scatter(1)
    for i, value in enumerate(single_phases(ids_all[...].reshape(CTX, 128), q, rates)):
        single_cs[i] = value
    plain_rates = [rate[:H] for rate in rates]
    list_copy.wait()

    def pair_phases(i, _):
        for b in range(8):
            k = i * 8 + b
            pair_cs[k] = cos_sin(plain_rates, list_s[1, k].astype(F32), list_s[2, k].astype(F32))
        return 0

    lax.fori_loop(0, CTX // 8, pair_phases, 0)
    wait_all(copies)
    spread_out(1, g2, e2)


def pair_terms(g2, e2, context, cs):
    host = context // 2
    g = pick(g2[host].astype(F32), e2[host], context % 2 > 0)
    return g * cs, swap(g) * cs


def several_kernel(list_v, ids_v, g2, e2, sums, list_s, ids_s, sems):
    me = lax.axis_index("ctx")
    rates = turn_rates(lax.axis_index("tile"))
    sums[...] = jnp.zeros_like(sums)

    @pl.when(jnp.max(list_v[5:6, :]) > 0)
    def _():
        copies = [
            pltpu.make_async_copy(list_v, list_s, sems.at[0]),
            pltpu.make_async_copy(ids_v, ids_s, sems.at[1]),
        ]
        for copy in copies:
            copy.start()
        wait_all(copies)

        def host(h, _):
            @pl.when(list_s[6, h] > 0)
            def _():
                def one(j, _):
                    master = ids_s[h, 0, j]

                    @pl.when(master >> 1 == me)
                    def _():
                        m = master & 1
                        cs = cos_sin(rates, ids_s[h, 0, 32 + j].astype(F32), ids_s[h, 0, 64 + j].astype(F32))
                        a, b = pair_terms(g2, e2, 2 * h + j // SRC, cs)
                        sums[2 * m] += a
                        sums[2 * m + 1] += b

                    return 0

                lax.fori_loop(0, PAIRS, one, 0)

            return 0

        lax.fori_loop(0, CTX, host, 0)


def rows_kernel(list_v, pair_cs, single_cs, g2, e2, sums, rows, list_s, sem, x_send, x_recv):
    tile = lax.axis_index("tile")
    copy = pltpu.make_async_copy(list_v, list_s, sem)
    copy.start()
    barrier = pltpu.get_barrier_semaphore()
    for k in range(1, T):
        pl.semaphore_signal(barrier, inc=1, device_id={"tile": (tile + k) % T}, device_id_type=MESH)
    left = left_half((Q, 2 * M))
    copy.wait()
    block = 16

    def step(i, carry):
        total = list(carry)
        for b in range(block):
            k = i * block + b
            context = list_s[0, k]
            both = g2[context // 2].astype(F32)
            g = jnp.where(context % 2 > 0, both[H:], both[:H])
            cs = pair_cs[k]
            a = g * cs
            b = swap(g) * cs
            for m in range(2):
                weight = list_s[3 + m, k].astype(F32)
                total[2 * m] += a * weight
                total[2 * m + 1] += b * weight
        return tuple(total)

    e = jnp.where(single_cs[2] > 0.5, e2[:, 1, :], e2[:, 0, :])
    e_turned = swap(e)
    total = lax.fori_loop(0, CTX // block, step, (jnp.zeros((H, 2 * M), F32),) * 4)
    for m in range(2):
        cs = single_cs[m]
        a = jnp.sum(e * cs, axis=0, keepdims=True)
        b = jnp.sum(e_turned * cs, axis=0, keepdims=True)
        a = sums[2 * m] + jnp.concatenate([total[2 * m], padded(a)], 0)
        b = sums[2 * m + 1] + jnp.concatenate([total[2 * m + 1], padded(b)], 0)
        rows[tile, m * Q : (m + 1) * Q] = jnp.where(left, a - swap(a), b + swap(b)).astype(BF16)
    pl.semaphore_wait(barrier, T - 1)
    copies = []
    for k in range(1, T):
        copies.append(
            pltpu.make_async_remote_copy(
                src_ref=rows.at[tile], dst_ref=rows.at[tile],
                send_sem=x_send.at[k - 1], recv_sem=x_recv.at[k - 1],
                device_id={"tile": (tile + k) % T}, device_id_type=MESH,
            )
        )
    for c in copies:
        c.start()
    wait_all(copies)


def last_kernel(rows, p_st, q_st, resist_v, out, resist, held, sem):
    left = left_half((M, 2 * M))
    copies = [pltpu.make_async_copy(resist_v, resist, sem.at[4])]
    copies[0].start()
    for m in range(2):
        parts = [rows[t].astype(F32)[m * Q : (m + 1) * Q] for t in range(T)]
        g = jnp.concatenate([part[:H] for part in parts] + [to_rows(parts[0][H : H + 1])], 0)
        turned = swap(g)
        both = jnp.concatenate([g, jnp.where(left, turned, -turned)], 0).astype(BF16)
        lifted = dot(p_st[...], both, ((0,), (0,))).astype(BF16)
        for i in range(2):
            part = slice(i * (R // 2), (i + 1) * (R // 2))
            held[m, part] = dot(lifted[part], q_st[...])
            place = (m, pl.ds(i * (R // 2), R // 2))
            copies.append(pltpu.make_async_copy(held.at[place], out.at[place], sem.at[2 * m + i]))
            copies[-1].start()
    wait_all(copies)


def local(masks, blur_rows, blur_cols, pupils, targets, context_masters, offsets):
    vmem = pl.BlockSpec(memory_space=pltpu.VMEM)
    hbm = pl.BlockSpec(memory_space=pltpu.HBM)
    dma = pltpu.SemaphoreType.DMA
    stay = functools.partial(pltpu.with_memory_space_constraint, memory_space=pltpu.HBM)
    resist_v, g2, e2, ids_all, listed, pair_cs, single_cs, p_st, q_st = pl.pallas_call(
        main_kernel,
        out_shape=(
            jax.ShapeDtypeStruct((2, R, N), BF16),
            jax.ShapeDtypeStruct((CTX, 2 * H, 2 * M), BF16),
            jax.ShapeDtypeStruct((CTX, 2, 2 * M), F32),
            jax.ShapeDtypeStruct((CTX, 1, 128), jnp.int32),
            jax.ShapeDtypeStruct((8, 128), jnp.int32),
            jax.ShapeDtypeStruct((CTX, H, 2 * M), F32),
            jax.ShapeDtypeStruct((3, CTX, 2 * M), F32),
            jax.ShapeDtypeStruct((2 * M, R), BF16),
            jax.ShapeDtypeStruct((2 * M, N), BF16),
        ),
        in_specs=[hbm] * 11,
        out_specs=(vmem,) * 9,
        scratch_shapes=[
            pltpu.VMEM((2, R, N), BF16),
            pltpu.VMEM((N, R), BF16),
            pltpu.VMEM((N, N), BF16),
            pltpu.VMEM((K, M, 2 * M), F32),
            pltpu.VMEM((2, R, N), BF16),
            pltpu.VMEM((2 * M, N), BF16),
            pltpu.VMEM((R, 2 * M), BF16),
            pltpu.VMEM((2 * M, 2 * N), BF16),
            pltpu.VMEM((2 * N, 4 * M), BF16),
            pltpu.SMEM((2, SRC), jnp.int32),
            pltpu.SMEM((2, 2, SRC), jnp.int32),
            pltpu.SMEM((8, 128), jnp.int32),
            pltpu.VMEM((CTX, 2 * H, 2 * M), BF16),
            pltpu.VMEM((CTX, 2, 2 * M), F32),
            pltpu.VMEM((2, T, 2 * Q, 2 * M), F32),
            pltpu.VMEM((2, T - 1, 2 * Q, 2 * M), F32),
            pltpu.VMEM((T, 2 * Q, 2 * M), F32),
            pltpu.VMEM((K, M, 2 * M), F32),
            pltpu.VMEM((K, M, 2 * M), F32),
            pltpu.VMEM((2, K * R, 2 * M), BF16),
            pltpu.VMEM((2, K * R, 2 * N), BF16),
            pltpu.VMEM((PAIRS, Q, 2 * M), F32),
            dma((11,)),
            dma,
            dma((3, T - 1)),
            dma((3, T - 1)),
            dma((2,)),
            dma((2, SIDE)),
            dma((2, SIDE)),
            dma((2,)),
            dma((2,)),
            dma((3,)),
            dma((3,)),
            dma((2, 3)),
            dma((2, 3)),
        ],
        compiler_params=pltpu.CompilerParams(
            collective_id=0, has_side_effects=True, vmem_limit_bytes=40 << 20
        ),
        name="main",
    )(
        *map(stay, (masks, blur_rows, blur_cols, pupils, targets)),
        stay(context_masters),
        stay(jnp.transpose(offsets, (0, 2, 1))),
        *map(stay, map(jnp.asarray, tables())),
    )
    sums = pl.pallas_call(
        several_kernel,
        out_shape=jax.ShapeDtypeStruct((4, Q, 2 * M), F32),
        in_specs=[vmem] * 4,
        out_specs=vmem,
        scratch_shapes=[
            pltpu.SMEM((8, 128), jnp.int32),
            pltpu.SMEM((CTX, 1, 128), jnp.int32),
            dma((2,)),
        ],
        compiler_params=pltpu.CompilerParams(vmem_limit_bytes=32 << 20),
        name="several",
    )(listed, ids_all, g2, e2)
    rows = pl.pallas_call(
        rows_kernel,
        out_shape=jax.ShapeDtypeStruct((T, 2 * Q, 2 * M), BF16),
        in_specs=[vmem] * 6,
        out_specs=vmem,
        scratch_shapes=[pltpu.SMEM((8, 128), jnp.int32), dma, dma((T - 1,)), dma((T - 1,))],
        compiler_params=pltpu.CompilerParams(
            collective_id=1, has_side_effects=True, vmem_limit_bytes=32 << 20
        ),
        name="rows",
    )(listed, pair_cs, single_cs, g2, e2, sums)
    mask_grad, resist = pl.pallas_call(
        last_kernel,
        out_shape=(
            jax.ShapeDtypeStruct((2, R, N), F32),
            jax.ShapeDtypeStruct((2, R, N), BF16),
        ),
        in_specs=[vmem] * 4,
        out_specs=(hbm, hbm),
        scratch_shapes=[pltpu.VMEM((2, R, N), F32), dma((5,))],
        compiler_params=pltpu.CompilerParams(vmem_limit_bytes=32 << 20),
        name="last",
    )(rows, p_st, q_st, resist_v)
    return (resist, mask_grad)


def solution(mesh):
    placed = (
        P("ctx", "tile", None),
        P(),
        P(),
        P(),
        P("ctx", "tile", None),
        P("ctx", None),
        P("ctx", None, None),
    )
    return jax.shard_map(
        local,
        mesh=mesh,
        in_specs=placed,
        out_specs=(P("ctx", "tile", None), P("ctx", "tile", None)),
        check_vma=False,
    )
```

```python
import functools
import math

import jax
import jax.numpy as jnp
import ml_dtypes
import numpy as np
from jax import lax
from jax.experimental import pallas as pl
from jax.experimental.pallas import tpu as pltpu
from jax.sharding import PartitionSpec as P

STEEPNESS = 4.0
THRESHOLD = 1.0
N = 512
M = 64
K = 6
T = 4
FAR_FIRST = (2, 1, 3)
R = N // T
H = M // (2 * T)
Q = 16
SIDE = 8
CTX = 2 * SIDE * SIDE
SRC = 12
PAIRS = 2 * SRC
MESH = pl.DeviceIdType.MESH
F32 = jnp.float32
BF16 = jnp.bfloat16
NEAR_FIRST = (1, 7, 2, 6, 3, 5, 4)


def tables():
    freq = (np.arange(M) - M // 2) % N
    angle = (freq[:, None] * np.arange(N)[None, :] % N) * (2.0 * math.pi / N)
    cos = np.cos(angle) / math.sqrt(N)
    sin = np.sin(angle) / math.sqrt(N)
    fst = np.concatenate([cos, -sin], 0)
    gcat = np.concatenate([cos.T, sin.T], 1)
    inv = np.concatenate([np.concatenate([cos, sin], 1), np.concatenate([-sin, cos], 1)], 0)
    adj = np.concatenate([np.concatenate([cos.T, -sin.T], 1), np.concatenate([sin.T, cos.T], 1)], 0)
    adj = np.concatenate([adj, -adj[:, M:], adj[:, :M]], 1)
    order = np.arange(2 * N).reshape(2, T, N // T).transpose(1, 0, 2).reshape(-1)
    return [t.astype(ml_dtypes.bfloat16) for t in (fst, gcat, inv[:, order], adj[order])]


def sine_coefficients():
    w = 0.25 * np.cos(np.pi * (np.arange(400) + 0.5) / 400)
    powers = np.stack([w ** (2 * i + 1) for i in range(6)], 1)
    return [float(c) for c in np.linalg.lstsq(powers, np.sin(2 * np.pi * w), rcond=None)[0]]


SINE = sine_coefficients()


def swap(a):
    return pltpu.roll(a, M, 1)


def left_half(shape):
    return lax.broadcasted_iota(jnp.int32, shape, 1) < M


def grid(shape):
    return lax.broadcasted_iota(jnp.int32, shape, 0), lax.broadcasted_iota(jnp.int32, shape, 1)


def turn_rates(tile):
    row, lane = grid((Q, 2 * M))
    v = lane % M
    plain = row < H
    early = v <= M // 2
    f_u = jnp.where(plain, row + (tile * H - M // 2), jnp.where(early, 0, v - M // 2))
    f_v = jnp.where(plain | early, v - M // 2, -(M // 2))
    late = jnp.where(lane < M, 0.0, 0.25).astype(F32)
    return f_u.astype(F32) * (1.0 / N), f_v.astype(F32) * (1.0 / N), late


def from_rows(a):
    row, lane = grid(a.shape)
    real = jnp.where((lane == row + M // 2) & (row > 0), jnp.broadcast_to(a[:, 0:1], a.shape), 0.0)
    imag = jnp.where((lane == row + M + M // 2) & (row > 0), jnp.broadcast_to(a[:, M : M + 1], a.shape), 0.0)
    return jnp.sum(real + imag, axis=0, keepdims=True)


def to_rows(e):
    shape = (M // 2, 2 * M)
    row, lane = grid(shape)
    wide = jnp.broadcast_to(e, shape)
    real = jnp.sum(jnp.where((lane == row + M // 2) & (row > 0), wide, 0.0), axis=1, keepdims=True)
    imag = jnp.sum(jnp.where((lane == row + M + M // 2) & (row > 0), wide, 0.0), axis=1, keepdims=True)
    first = jnp.where((row == 0) & (lane % M <= M // 2), wide, 0.0)
    return first + jnp.where(lane == 0, real, 0.0) + jnp.where(lane == M, imag, 0.0)


def split(a):
    high = a.astype(BF16)
    return high, (a - high.astype(F32)).astype(BF16)


def mirrored(a):
    src, dst = grid((2 * M, 2 * M))
    real = jnp.where((src + dst == M) & (src < M) & (dst < M), 1.0, 0.0)
    both = real - jnp.where((src + dst == 3 * M) & (src >= M), 1.0, 0.0)
    out = dot(jnp.concatenate(split(a), 0), both.astype(BF16))
    return out[: a.shape[0]] + out[a.shape[0] :]


def flipped(blocks):
    row, col = grid((M // 2, M // 2))
    turn = jnp.where(row + col == M // 2, 1.0, 0.0).astype(BF16)
    out = dot(turn, jnp.concatenate([part for a in blocks for part in split(a)], 1))
    part = [out[:, i * 2 * M : (i + 1) * 2 * M] for i in range(2 * len(blocks))]
    return [part[2 * i] + part[2 * i + 1] for i in range(len(blocks))]


def expand(halves, es):
    row, lane = grid((M // 2, 2 * M))
    wide = [jnp.broadcast_to(e, (16, 2 * M)) for e in es]
    turned = mirrored(jnp.concatenate([*halves, *wide], 0))
    lower = flipped([turned[: M // 2], turned[M // 2 : M]])
    out = []
    for i in range(2):
        e_turned = jnp.broadcast_to(turned[M + 16 * i : M + 16 * i + 1], row.shape)
        first = jnp.where((row == 0) & (lane % M > M // 2), e_turned, 0.0)
        out.append(jnp.concatenate([halves[i], lower[i] + first + to_rows(es[i])], 0))
    return out


def fold(grads):
    low = [grad[M // 2 :] for grad in grads]
    turned = mirrored(jnp.concatenate(low, 0))
    upper = flipped([turned[: M // 2], turned[M // 2 :]])
    v = lax.broadcasted_iota(jnp.int32, (1, 2 * M), 1) % M
    out = []
    for i in range(2):
        t = turned[i * (M // 2) : i * (M // 2) + 1]
        e = jnp.where(v <= M // 2, low[i][0:1], 0.0) + jnp.where((v > 0) & (v < M // 2), t, 0.0)
        out.append((grads[i][: M // 2] + upper[i], e + from_rows(low[i])))
    return out


def half_of(spectrum):
    low = spectrum[M // 2 :]
    v = lax.broadcasted_iota(jnp.int32, (1, 2 * M), 1) % M
    return spectrum[: M // 2], jnp.where(v <= M // 2, low[0:1], 0.0) + from_rows(low)


def padded(e):
    return jnp.where(lax.broadcasted_iota(jnp.int32, (Q - H, 2 * M), 0) == 0, jnp.broadcast_to(e, (Q - H, 2 * M)), 0.0)


def pick(block, es, second):
    return jnp.concatenate(
        [jnp.where(second, block[H:], block[:H]), padded(jnp.where(second, es[1:2], es[0:1]))], 0
    )


def cos_sin(rates, r, s):
    y = rates[0] * r + rates[1] * s - rates[2]
    y = y - jnp.floor(y + 0.5)
    w = 0.25 - jnp.abs(y)
    z = w * w
    total = jnp.full_like(z, SINE[-1])
    for c in SINE[-2::-1]:
        total = total * z + c
    return total * w


def dot(a, b, dims=((1,), (0,))):
    return lax.dot_general(a, b, (dims, ((), ())), preferred_element_type=F32)


def wait_all(copies):
    for c in copies:
        c.wait()


def near_first(i):
    return (i % 2) * ((i + 1) // 2) + (1 - i % 2) * (SIDE - i // 2)


def pair_list(ids, me):
    row, lane = grid((CTX, 128))
    row8, lane8 = grid((8, 128))
    ones = jnp.full((8, 128), 1.0, BF16)
    before = jnp.where(row < lane, 1.0, 0.0).astype(BF16)
    r = pltpu.roll(ids, 128 - 32, 1)
    s = pltpu.roll(ids, 128 - 64, 1)
    match = jnp.where((ids >> 1 == me) & (lane < PAIRS), 1.0, 0.0)
    values = [jnp.where(lane >= SRC, 1.0, 0.0)] + [v.astype(F32) for v in (r >> 4, r & 15, s >> 4, s & 15, ids & 1)]
    count = dot(ones, match.astype(BF16), ((1,), (1,)))
    found = [dot(ones, (match * v).astype(BF16), ((1,), (1,))) for v in values]
    single = jnp.where(count == 1.0, 1.0, 0.0)
    rank = dot(single.astype(BF16), before)
    hot = jnp.where(
        (jnp.broadcast_to(rank[0:1], (CTX, 128)) == row.astype(F32))
        & (jnp.broadcast_to(single[0:1], (CTX, 128)) > 0.5),
        1.0, 0.0,
    ).astype(BF16)
    load = jnp.where(row8 == 6, single, 0.0)
    load = jnp.where(row8 == 0, single * (2.0 * lane8.astype(F32) + found[0]), load)
    for i in range(1, 6):
        load = jnp.where(row8 == i, single * found[i], load)
    listed = dot(load.astype(BF16), hot, ((1,), (1,)))
    at = [jnp.broadcast_to(listed[i : i + 1], (8, 128)) for i in range(7)]
    several = jnp.where(count > 1.5, 1.0, 0.0)
    out = [at[0], 16.0 * at[1] + at[2], 16.0 * at[3] + at[4], at[6] - at[5], at[5]]
    out += [jnp.broadcast_to(jnp.sum(several, axis=1, keepdims=True), (8, 128)), several]
    rows = jnp.zeros((8, 128), F32)
    for i, value in enumerate(out):
        rows = jnp.where(row8 == i, value, rows)
    return rows.astype(jnp.int32)


def single_phases(ids, me, rates):
    row, lane = grid((CTX, 128))
    match = jnp.where((ids >> 1 == me) & (lane < PAIRS), 1.0, 0.0)

    def column(values):
        return jnp.broadcast_to(jnp.sum(match * values.astype(F32), axis=1, keepdims=True), (CTX, 128))

    r = column(pltpu.roll(ids, 128 - 32, 1))
    s = column(pltpu.roll(ids, 128 - 64, 1))
    second = column(jnp.where(lane >= SRC, 1.0, 0.0))
    master = column(ids & 1)
    single = jnp.where(column(jnp.ones_like(match)) == 1.0, 1.0, 0.0)
    cs = cos_sin([jnp.broadcast_to(rate[H : H + 1], (CTX, 128)) for rate in rates], r, s)
    return jnp.where(single * (1.0 - master) > 0.5, cs, 0.0), jnp.where(single * master > 0.5, cs, 0.0), single * second


def main_kernel(
    masks_h, br_h, bc_h, pupils_h, targets_h, ids_h, shifts_h, fst_h, gcat_h, inv_h, adj_h,
    resist, g2, e2, ids_all, listed, pair_cs, single_cs, p_out, q_out,
    masks, br, bc, pupils, targets, fst, gown_v, inv, adj,
    ids_s, shifts_s, list_s, g1, e1, part, part_in, spec, prr, pii, u_all, pull, phases,
    load_sem, list_sem, x_send, x_recv, g_send, a_recv, f_recv, s_send, s_recv, i_send, i_recv, e_send, e_recv,
):
    tile = lax.axis_index("tile")
    q = lax.axis_index("ctx")
    core, y, z = q % 2, (q // 2) % SIDE, q // (2 * SIDE)
    major = z + core * (y - z)
    minor = y + core * (z - y)
    half = core * (SIDE * SIDE)
    slot = half + major * SIDE + minor
    own = pl.ds(pl.multiple_of(tile * R, R), R)

    loads = [
        pltpu.make_async_copy(src, dst, load_sem.at[i])
        for i, (src, dst) in enumerate(
            [
                (fst_h, fst),
                (br_h.at[:, own], br),
                (bc_h, bc),
                (masks_h, masks),
                (pupils_h, pupils),
                (gcat_h.at[own, :], gown_v),
                (inv_h, inv),
                (targets_h, targets),
                (adj_h, adj),
                (ids_h, ids_s),
                (shifts_h, shifts_s),
            ]
        )
    ]
    for copy in loads:
        copy.start()

    def ctx_id(mj, mn):
        zz = mj + core * (mn - mj)
        yy = mn + core * (mj - mn)
        return zz * (2 * SIDE) + yy * 2 + core

    sibling = q + 1 - 2 * core
    barrier = pltpu.get_barrier_semaphore()
    for k in range(1, SIDE):
        pl.semaphore_signal(barrier, inc=1, device_id={"ctx": ctx_id(major, (minor + k) % SIDE)}, device_id_type=MESH)
        pl.semaphore_signal(barrier, inc=1, device_id={"ctx": ctx_id((major + k) % SIDE, minor)}, device_id_type=MESH)
    for k in FAR_FIRST:
        pl.semaphore_signal(barrier, inc=1, device_id={"tile": (tile + k) % T}, device_id_type=MESH)
    pl.semaphore_signal(barrier, inc=1, device_id={"ctx": sibling}, device_id_type=MESH)

    def put(step, i, half_rows, e):
        for t in range(T):
            part[step, t, i * Q : i * Q + H] = half_rows[t * H : (t + 1) * H]
            part[step, t, i * Q + H : (i + 1) * Q] = padded(e) if t == 0 else jnp.zeros((Q - H, 2 * M), F32)

    loads[0].wait()
    loads[1].wait()
    table = fst[...]
    p_st = dot(table, br[...]).astype(BF16)
    loads[2].wait()
    q_st = dot(table, bc[...]).astype(BF16)
    p_out[...] = p_st
    q_out[...] = q_st
    qq = jnp.concatenate([q_st, -q_st[M:], q_st[:M]], 0)
    pcat = jnp.concatenate([p_st[:M], p_st[M:]], 1)
    loads[3].wait()
    for m in range(2):
        a = dot(masks[m], qq, ((1,), (1,))).astype(BF16)
        s = dot(pcat, jnp.concatenate([a[:, : 2 * M], a[:, 2 * M :]], 0))
        put(0, m, *half_of(s))

    pl.semaphore_wait(barrier, T - 1 + 2 * (SIDE - 1) + 1)

    def tile_scatter(step):
        copies = []
        for k in FAR_FIRST:
            to = (tile + k) % T
            copies.append(
                pltpu.make_async_remote_copy(
                    src_ref=part.at[step, to], dst_ref=part_in.at[step, k - 1],
                    send_sem=x_send.at[2 * step, k - 1], recv_sem=x_recv.at[2 * step, k - 1],
                    device_id={"tile": to}, device_id_type=MESH,
                )
            )
        for c in copies:
            c.start()
        return copies

    def tile_sum(step):
        return (part[step, tile] + part_in[step, 0]) + (part_in[step, 1] + part_in[step, 2])

    def to_ctx(ref, place, send_sem, recv_sem, to):
        return pltpu.make_async_remote_copy(
            src_ref=ref.at[place], dst_ref=ref.at[place], send_sem=send_sem, recv_sem=recv_sem,
            device_id={"ctx": to}, device_id_type=MESH,
        )

    minor_ids = {k: ctx_id(major, (minor + k) % SIDE) for k in NEAR_FIRST}
    major_ids = {k: ctx_id((major + k) % SIDE, minor) for k in NEAR_FIRST}
    first = half + major * SIDE

    def gather(buf, step, between, late, end):
        def along_minor(k, to):
            return to_ctx(buf, pl.ds(slot, 1), g_send.at[step], a_recv.at[step, k], to)

        def along_major(came, k):
            place = pl.ds(first + (minor + SIDE - came) % SIDE, 1)
            return to_ctx(buf, place, g_send.at[step], f_recv.at[step, k], major_ids[k])

        def to_sibling(row):
            return to_ctx(buf, pl.ds(half + row * SIDE, SIDE), s_send.at[step], s_recv.at[step], sibling)

        def bytes_of(blocks, send_sem, recv_sem):
            return to_ctx(buf, pl.ds(0, blocks), send_sem, recv_sem, sibling)

        for k in NEAR_FIRST:
            along_minor(k, minor_ids[k]).start()
        between()
        for k in NEAR_FIRST:
            along_major(0, k).start()

        def forward(i, _):
            came = near_first(i)
            along_minor(came, sibling).wait_recv()
            for k in NEAR_FIRST:
                along_major(came, k).start()
            return 0

        lax.fori_loop(1, SIDE, forward, 0)
        to_sibling(major).start()
        late()

        def arrive(i, _):
            k = near_first(i)
            bytes_of(SIDE, g_send.at[step], f_recv.at[step, k]).wait_recv()
            to_sibling((major + SIDE - k) % SIDE).start()
            return 0

        lax.fori_loop(1, SIDE, arrive, 0)
        end()
        bytes_of((SIDE - 1) * (SIDE + 1), g_send.at[step], f_recv.at[step, 0]).wait_send()
        bytes_of(SIDE * SIDE, s_send.at[step], s_recv.at[step]).wait()

    def line(buf, send, recv, phase):
        if phase == 2:
            places = [(pl.ds(half, SIDE * SIDE), sibling)]
        elif phase == 1:
            places = [(pl.ds(first, SIDE), major_ids[k]) for k in NEAR_FIRST]
        else:
            places = [(pl.ds(slot, 1), minor_ids[k]) for k in NEAR_FIRST]
        for place, to in places:
            to_ctx(buf, place, send.at[phase], recv.at[phase], to).start()
        blocks = (SIDE - 1, (SIDE - 1) * SIDE, SIDE * SIDE)[phase]
        return [to_ctx(buf, pl.ds(0, blocks), send.at[phase], recv.at[phase], sibling)]

    def spread_out(step, buf, es):
        total = tile_sum(step)
        buf[pl.ds(slot, 1)] = jnp.concatenate([total[:H], total[Q : Q + H]], 0).astype(BF16).reshape(1, 2 * H, 2 * M)
        es[pl.ds(slot, 1)] = jnp.concatenate([total[H : H + 1], total[Q + H : Q + H + 1]], 0).reshape(1, 2, 2 * M)
        e_sems = (e_send.at[step], e_recv.at[step])
        pending = []

        def between():
            pending.append(line(es, *e_sems, 0))
            if step == 0:
                wait_all(ids_copies.pop())
                ids_copies.append(line(ids_all, i_send, i_recv, 1))

        def late():
            wait_all(pending.pop())
            pending.append(line(es, *e_sems, 1))
            if step == 0:
                wait_all(ids_copies.pop())
                ids_copies.append(line(ids_all, i_send, i_recv, 2))

        def end():
            wait_all(pending.pop())
            pending.append(line(es, *e_sems, 2))

        gather(buf, step, between, late, end)
        wait_all(pending.pop())

    copies = tile_scatter(0)
    loads[9].wait()
    loads[10].wait()
    lane = lax.broadcasted_iota(jnp.int32, (1, 128), 1)
    own_ids = jnp.zeros((1, 128), jnp.int32)
    for c in range(2):
        for j in range(SRC):
            for place, value in ((0, ids_s[c, j]), (32, shifts_s[c, 0, j]), (64, shifts_s[c, 1, j])):
                own_ids = jnp.where(lane == place + c * SRC + j, value, own_ids)
    ids_all[pl.ds(slot, 1)] = own_ids.reshape(1, 1, 128)
    ids_copies = [line(ids_all, i_send, i_recv, 0)]

    rates = turn_rates(tile)
    for p in range(PAIRS):
        c, j = p // SRC, p % SRC
        phases[p] = cos_sin(rates, shifts_s[c, 0, j].astype(F32), shifts_s[c, 1, j].astype(F32))
    left64 = left_half((M, 2 * M))
    loads[4].wait()
    for k in range(K):
        pk = pupils[k]
        turned = swap(pk)
        prr[k] = jnp.where(left64, pk, turned)
        pii[k] = jnp.where(left64, -turned, pk)

    wait_all(copies)
    spread_out(0, g1, e1)
    wait_all(ids_copies.pop())

    leftq = left_half((Q, 2 * M))
    for c in range(2):
        sum_a = jnp.zeros((Q, 2 * M), F32)
        sum_b = jnp.zeros((Q, 2 * M), F32)
        for j in range(SRC):
            p = c * SRC + j
            master = ids_s[c, j]
            owner = master >> 1
            ocore = owner & 1
            oy = (owner >> 1) & (SIDE - 1)
            oz = owner >> 4
            place = ocore * (SIDE * SIDE) + oz * SIDE + oy + ocore * (SIDE - 1) * (oy - oz)
            g = pick(g1[place].astype(F32), e1[place], (master & 1) > 0)
            cs = phases[p]
            sum_a += g * cs
            sum_b += swap(g) * cs
        spec[tile, c * Q : (c + 1) * Q] = jnp.where(leftq, sum_a + swap(sum_a), swap(sum_b) - sum_b)
    copies = []
    for k in FAR_FIRST:
        copies.append(
            pltpu.make_async_remote_copy(
                src_ref=spec.at[tile], dst_ref=spec.at[tile],
                send_sem=x_send.at[1, k - 1], recv_sem=x_recv.at[1, k - 1],
                device_id={"tile": (tile + k) % T}, device_id_type=MESH,
            )
        )
    for c in copies:
        c.start()
    listed[...] = pair_list(ids_all[...].reshape(CTX, 128), q)
    list_copy = pltpu.make_async_copy(listed, list_s, list_sem)
    list_copy.start()
    for copy in loads[5:9]:
        copy.wait()
    fown = fst[:, own]
    fcat = jnp.concatenate([fown[:M], fown[M:]], 1)
    gown = gown_v[...]
    wait_all(copies)

    halves = [jnp.concatenate([spec[t, c * Q : c * Q + H] for t in range(T)], 0) for c in range(2)]
    spectra = expand(halves, [spec[0, c * Q + H : c * Q + H + 1] for c in range(2)])
    for c in range(2):
        s = spectra[c]
        s_sw = swap(s)
        s2 = jnp.where(left64, -s_sw, s_sw)
        s2_sw = jnp.where(left64, s, -s)
        for k in range(K):
            a1 = prr[k] * s + pii[k] * s_sw
            a2 = prr[k] * s2 + pii[k] * s2_sw
            both = jnp.concatenate([a1, a2], 0).astype(BF16)
            u_all[c, k * R : (k + 1) * R] = dot(gown, both).astype(BF16)

    def field_of(i):
        c, b = i // T, i % T
        return dot(u_all[c], inv[:, b * 2 * R : (b + 1) * 2 * R])

    def use(i, field):
        c, b = i // T, i % T
        cols = slice(b * R, (b + 1) * R)
        intensity = jnp.zeros((R, R), F32)
        for k in range(K):
            fr = field[k * R : (k + 1) * R, :R]
            fi = field[k * R : (k + 1) * R, R:]
            intensity += fr * fr + fi * fi
        image = 1.0 / (1.0 + jnp.exp(-STEEPNESS * (intensity - THRESHOLD)))
        resist[c, :, cols] = image.astype(BF16)
        slope = (image - targets[c, :, cols].astype(F32)) * (2.0 * STEEPNESS) * image * (1.0 - image)
        slope2 = jnp.concatenate([slope, slope], 1)
        for k in range(K):
            pull[c, k * R : (k + 1) * R, b * 2 * R : (b + 1) * 2 * R] = (
                slope2 * field[k * R : (k + 1) * R]
            ).astype(BF16)

    def gradient(c):
        folded = dot(pull[c], adj[...]).astype(BF16)
        g_a = jnp.zeros((M, 2 * M), F32)
        g_b = jnp.zeros((M, 2 * M), F32)
        for k in range(K):
            fk = folded[k * R : (k + 1) * R]
            ga = dot(fcat, jnp.concatenate([fk[:, : 2 * M], fk[:, 2 * M :]], 0))
            g_a += prr[k] * ga
            g_b += pii[k] * ga
        return g_a + swap(g_b)

    grads = []
    coming = field_of(0)
    for i in range(2 * T):
        field = coming
        if i < 2 * T - 1:
            coming = field_of(i + 1)
        use(i, field)
        if i % T == T - 1:
            grads.append(gradient(i // T))
    for c, (half_rows, e) in enumerate(fold(grads)):
        put(1, c, half_rows, e)

    copies = tile_scatter(1)
    for i, value in enumerate(single_phases(ids_all[...].reshape(CTX, 128), q, rates)):
        single_cs[i] = value
    plain_rates = [rate[:H] for rate in rates]
    list_copy.wait()

    def pair_phases(i, _):
        for b in range(8):
            k = i * 8 + b
            pair_cs[k] = cos_sin(plain_rates, list_s[1, k].astype(F32), list_s[2, k].astype(F32))
        return 0

    lax.fori_loop(0, CTX // 8, pair_phases, 0)
    wait_all(copies)
    spread_out(1, g2, e2)


def pair_terms(g2, e2, context, cs):
    host = context // 2
    g = pick(g2[host].astype(F32), e2[host], context % 2 > 0)
    return g * cs, swap(g) * cs


def several_kernel(list_v, ids_v, g2, e2, sums, list_s, ids_s, sems):
    me = lax.axis_index("ctx")
    rates = turn_rates(lax.axis_index("tile"))
    sums[...] = jnp.zeros_like(sums)

    @pl.when(jnp.max(list_v[5:6, :]) > 0)
    def _():
        copies = [
            pltpu.make_async_copy(list_v, list_s, sems.at[0]),
            pltpu.make_async_copy(ids_v, ids_s, sems.at[1]),
        ]
        for copy in copies:
            copy.start()
        wait_all(copies)

        def host(h, _):
            @pl.when(list_s[6, h] > 0)
            def _():
                def one(j, _):
                    master = ids_s[h, 0, j]

                    @pl.when(master >> 1 == me)
                    def _():
                        m = master & 1
                        cs = cos_sin(rates, ids_s[h, 0, 32 + j].astype(F32), ids_s[h, 0, 64 + j].astype(F32))
                        a, b = pair_terms(g2, e2, 2 * h + j // SRC, cs)
                        sums[2 * m] += a
                        sums[2 * m + 1] += b

                    return 0

                lax.fori_loop(0, PAIRS, one, 0)

            return 0

        lax.fori_loop(0, CTX, host, 0)


def rows_kernel(list_v, pair_cs, single_cs, g2, e2, sums, rows, list_s, sem, x_send, x_recv):
    tile = lax.axis_index("tile")
    copy = pltpu.make_async_copy(list_v, list_s, sem)
    copy.start()
    barrier = pltpu.get_barrier_semaphore()
    for k in FAR_FIRST:
        pl.semaphore_signal(barrier, inc=1, device_id={"tile": (tile + k) % T}, device_id_type=MESH)
    left = left_half((Q, 2 * M))
    copy.wait()
    block = 16

    def step(i, carry):
        total = list(carry)
        for b in range(block):
            k = i * block + b
            context = list_s[0, k]
            both = g2[context // 2].astype(F32)
            g = jnp.where(context % 2 > 0, both[H:], both[:H])
            cs = pair_cs[k]
            a = g * cs
            b = swap(g) * cs
            for m in range(2):
                weight = list_s[3 + m, k].astype(F32)
                total[2 * m] += a * weight
                total[2 * m + 1] += b * weight
        return tuple(total)

    e = jnp.where(single_cs[2] > 0.5, e2[:, 1, :], e2[:, 0, :])
    e_turned = swap(e)
    total = lax.fori_loop(0, CTX // block, step, (jnp.zeros((H, 2 * M), F32),) * 4)
    for m in range(2):
        cs = single_cs[m]
        a = jnp.sum(e * cs, axis=0, keepdims=True)
        b = jnp.sum(e_turned * cs, axis=0, keepdims=True)
        a = sums[2 * m] + jnp.concatenate([total[2 * m], padded(a)], 0)
        b = sums[2 * m + 1] + jnp.concatenate([total[2 * m + 1], padded(b)], 0)
        rows[tile, m * Q : (m + 1) * Q] = jnp.where(left, a - swap(a), b + swap(b)).astype(BF16)
    pl.semaphore_wait(barrier, T - 1)
    copies = []
    for k in FAR_FIRST:
        copies.append(
            pltpu.make_async_remote_copy(
                src_ref=rows.at[tile], dst_ref=rows.at[tile],
                send_sem=x_send.at[k - 1], recv_sem=x_recv.at[k - 1],
                device_id={"tile": (tile + k) % T}, device_id_type=MESH,
            )
        )
    for c in copies:
        c.start()
    wait_all(copies)


def last_kernel(rows, p_st, q_st, resist_v, out, resist, held, sem):
    left = left_half((M, 2 * M))
    copies = [pltpu.make_async_copy(resist_v, resist, sem.at[4])]
    copies[0].start()
    for m in range(2):
        parts = [rows[t].astype(F32)[m * Q : (m + 1) * Q] for t in range(T)]
        g = jnp.concatenate([part[:H] for part in parts] + [to_rows(parts[0][H : H + 1])], 0)
        turned = swap(g)
        both = jnp.concatenate([g, jnp.where(left, turned, -turned)], 0).astype(BF16)
        lifted = dot(p_st[...], both, ((0,), (0,))).astype(BF16)
        for i in range(2):
            part = slice(i * (R // 2), (i + 1) * (R // 2))
            held[m, part] = dot(lifted[part], q_st[...])
            place = (m, pl.ds(i * (R // 2), R // 2))
            copies.append(pltpu.make_async_copy(held.at[place], out.at[place], sem.at[2 * m + i]))
            copies[-1].start()
    wait_all(copies)


def local(masks, blur_rows, blur_cols, pupils, targets, context_masters, offsets):
    vmem = pl.BlockSpec(memory_space=pltpu.VMEM)
    hbm = pl.BlockSpec(memory_space=pltpu.HBM)
    dma = pltpu.SemaphoreType.DMA
    stay = functools.partial(pltpu.with_memory_space_constraint, memory_space=pltpu.HBM)
    resist_v, g2, e2, ids_all, listed, pair_cs, single_cs, p_st, q_st = pl.pallas_call(
        main_kernel,
        out_shape=(
            jax.ShapeDtypeStruct((2, R, N), BF16),
            jax.ShapeDtypeStruct((CTX, 2 * H, 2 * M), BF16),
            jax.ShapeDtypeStruct((CTX, 2, 2 * M), F32),
            jax.ShapeDtypeStruct((CTX, 1, 128), jnp.int32),
            jax.ShapeDtypeStruct((8, 128), jnp.int32),
            jax.ShapeDtypeStruct((CTX, H, 2 * M), F32),
            jax.ShapeDtypeStruct((3, CTX, 2 * M), F32),
            jax.ShapeDtypeStruct((2 * M, R), BF16),
            jax.ShapeDtypeStruct((2 * M, N), BF16),
        ),
        in_specs=[hbm] * 11,
        out_specs=(vmem,) * 9,
        scratch_shapes=[
            pltpu.VMEM((2, R, N), BF16),
            pltpu.VMEM((N, R), BF16),
            pltpu.VMEM((N, N), BF16),
            pltpu.VMEM((K, M, 2 * M), F32),
            pltpu.VMEM((2, R, N), BF16),
            pltpu.VMEM((2 * M, N), BF16),
            pltpu.VMEM((R, 2 * M), BF16),
            pltpu.VMEM((2 * M, 2 * N), BF16),
            pltpu.VMEM((2 * N, 4 * M), BF16),
            pltpu.SMEM((2, SRC), jnp.int32),
            pltpu.SMEM((2, 2, SRC), jnp.int32),
            pltpu.SMEM((8, 128), jnp.int32),
            pltpu.VMEM((CTX, 2 * H, 2 * M), BF16),
            pltpu.VMEM((CTX, 2, 2 * M), F32),
            pltpu.VMEM((2, T, 2 * Q, 2 * M), F32),
            pltpu.VMEM((2, T - 1, 2 * Q, 2 * M), F32),
            pltpu.VMEM((T, 2 * Q, 2 * M), F32),
            pltpu.VMEM((K, M, 2 * M), F32),
            pltpu.VMEM((K, M, 2 * M), F32),
            pltpu.VMEM((2, K * R, 2 * M), BF16),
            pltpu.VMEM((2, K * R, 2 * N), BF16),
            pltpu.VMEM((PAIRS, Q, 2 * M), F32),
            dma((11,)),
            dma,
            dma((3, T - 1)),
            dma((3, T - 1)),
            dma((2,)),
            dma((2, SIDE)),
            dma((2, SIDE)),
            dma((2,)),
            dma((2,)),
            dma((3,)),
            dma((3,)),
            dma((2, 3)),
            dma((2, 3)),
        ],
        compiler_params=pltpu.CompilerParams(
            collective_id=0, has_side_effects=True, vmem_limit_bytes=40 << 20
        ),
        name="main",
    )(
        *map(stay, (masks, blur_rows, blur_cols, pupils, targets)),
        stay(context_masters),
        stay(jnp.transpose(offsets, (0, 2, 1))),
        *map(stay, map(jnp.asarray, tables())),
    )
    sums = pl.pallas_call(
        several_kernel,
        out_shape=jax.ShapeDtypeStruct((4, Q, 2 * M), F32),
        in_specs=[vmem] * 4,
        out_specs=vmem,
        scratch_shapes=[
            pltpu.SMEM((8, 128), jnp.int32),
            pltpu.SMEM((CTX, 1, 128), jnp.int32),
            dma((2,)),
        ],
        compiler_params=pltpu.CompilerParams(vmem_limit_bytes=32 << 20),
        name="several",
    )(listed, ids_all, g2, e2)
    rows = pl.pallas_call(
        rows_kernel,
        out_shape=jax.ShapeDtypeStruct((T, 2 * Q, 2 * M), BF16),
        in_specs=[vmem] * 6,
        out_specs=vmem,
        scratch_shapes=[pltpu.SMEM((8, 128), jnp.int32), dma, dma((T - 1,)), dma((T - 1,))],
        compiler_params=pltpu.CompilerParams(
            collective_id=1, has_side_effects=True, vmem_limit_bytes=32 << 20
        ),
        name="rows",
    )(listed, pair_cs, single_cs, g2, e2, sums)
    mask_grad, resist = pl.pallas_call(
        last_kernel,
        out_shape=(
            jax.ShapeDtypeStruct((2, R, N), F32),
            jax.ShapeDtypeStruct((2, R, N), BF16),
        ),
        in_specs=[vmem] * 4,
        out_specs=(hbm, hbm),
        scratch_shapes=[pltpu.VMEM((2, R, N), F32), dma((5,))],
        compiler_params=pltpu.CompilerParams(vmem_limit_bytes=32 << 20),
        name="last",
    )(rows, p_st, q_st, resist_v)
    return (resist, mask_grad)


def solution(mesh):
    placed = (
        P("ctx", "tile", None),
        P(),
        P(),
        P(),
        P("ctx", "tile", None),
        P("ctx", None),
        P("ctx", None, None),
    )
    return jax.shard_map(
        local,
        mesh=mesh,
        in_specs=placed,
        out_specs=(P("ctx", "tile", None), P("ctx", "tile", None)),
        check_vma=False,
    )
```
